32 devices in a mesh: island: 4 (over y, x), expert: 4 (over z), tensor: 2 (over core).
Axes of the slice: x: 2, y: 2, z: 4, core: 2. Of those that a mesh axis runs over, the one named last changes fastest.
Arguments:
- tokens: bfloat16 [4, 1024, 2048], P('island', 'expert', 'tensor'), may hold values from -6 to 6
- token_grads: bfloat16 [4, 1024, 2048], P('island', 'expert', 'tensor'), may hold values from -6 to 6
- slot_token: int32 [4, 4, 4, 96], P('island', 'expert'), may hold values from 0 to 255, as said below
- slot_count: int32 [4, 4, 4], P('island', 'expert'), may hold values from 24 to 96, as said below
- slot_prob: float32 [4, 4, 4, 96], P('island', 'expert'), may hold values from 0.1 to 1
- gate_weight: bfloat16 [4, 4, 2048, 1536], P('island', 'expert', None, 'tensor'), may hold values from -0.125 to 0.125
- down_weight: bfloat16 [4, 4, 1536, 2048], P('island', 'expert', 'tensor'), may hold values from -0.15625 to 0.15625
- drift: bfloat16 [4, 4, 2048, 1536], P('island', 'expert', None, 'tensor'), may hold values from -6 to 6
- momentum: float32 [4, 2048, 1536], P('expert', None, 'tensor'), may hold values from -1.5 to 1.5
Outputs:
- new_momentum: float32 [4, 2048, 1536], P('expert', None, 'tensor')
- outer_step: bfloat16 [4, 2048, 1536], P('expert', None, 'tensor')
The draws below stay inside these ranges and needn't reach their ends.
Inputs may be any that keep to these rules, and one draw needn't show every extreme that they name: `slot_token`: for each island, source device and expert the 96 entries are distinct tokens of that source device. `slot_count`: in every island some expert is full from every source device.
All inputs are finite; a program needn't handle non-finite values.
Results may differ from the reference program's by a relative error of at most 0.0031.
The reference program's roundings to bfloat16 on the way (of `input_slots`, `grad_slots` and `hidden_grad`) count: a program that leaves them out, or rounds other values in their place, can miss the bound.
Values may be sent and summed in bfloat16 or wider, within the bound.
No kernel may reach another device: no remote copies, remote signals or barrier semaphores. Data moves between devices by JAX's collectives and lax.ppermute only.
A program may use at most 128 MiB of HBM per device.

```python
import math
import jax
import jax.numpy as jnp
from jax import lax

D = 2048
FF = 1536
TOK_DEV = 256
CAP = 96
ISLANDS = 4
SOURCES = 4
EXPERTS = 4
TOKENS = 1024
ROWS = 384


def draw_slot_token(key, part):
    row_count = ISLANDS * SOURCES * EXPERTS
    scores = jax.random.randint(key, (row_count, TOK_DEV), 0, 1 << 20) * TOK_DEV + jnp.arange(TOK_DEV, dtype=jnp.int32)[None, :]
    ranking = jnp.argsort(scores, axis=1, stable=True)[:, :CAP]
    return ranking.astype(jnp.int32).reshape(ISLANDS, SOURCES, EXPERTS, CAP)


def draw_slot_count(key, part):
    counts_drawn = jax.random.randint(jax.random.fold_in(key, 1), (ISLANDS, SOURCES, EXPERTS), CAP // 4, CAP + 1)
    full_expert = jax.random.randint(jax.random.fold_in(key, 2), (ISLANDS, 1, 1), 0, EXPERTS)
    chosen = jnp.arange(EXPERTS, dtype=jnp.int32)[None, None, :] == full_expert
    return jnp.where(chosen, CAP, counts_drawn).astype(jnp.int32)


def strengthened(result, rng, source, target, parts, factor):
    def block_of(dim):
        return (jnp.arange(result.shape[dim]) // (result.shape[dim] // parts)).reshape((-1,) + (1,) * (result.ndim - 1 - dim))

    near = jax.random.permutation(rng, parts)[block_of(target)]
    other_side = (block_of(target) + parts // 2) % parts
    return jnp.where((block_of(source) == near) | (block_of(source) == other_side), factor * result, result)


def block_scale(key, shape, cuts, least, high):
    factor_of = 1.0
    for axis_at, shards_of in cuts:
        heights = jax.random.uniform(jax.random.fold_in(jax.random.fold_in(key, 6), axis_at), (shards_of,), jnp.float32, least / len(cuts), high / len(cuts))
        factor_of = factor_of * jnp.repeat(jnp.exp(heights), shape[axis_at] // shards_of).reshape((-1,) + (1,) * (len(shape) - 1 - axis_at))
    return factor_of


def normal_values(stream_key, dims, width, limit, cuts=(), kind=jnp.bfloat16):
    loudness = block_scale(stream_key, dims, cuts, -0.22, 0.18) if cuts else 1.0
    drawn = jax.random.normal(stream_key, dims, jnp.float32) * width * loudness
    return jnp.minimum(jnp.maximum(drawn, -limit), limit).astype(kind)


def bell_draw_with(stream_key, dims, width, most, cuts, heavy, kind=jnp.bfloat16):
    entries = width * jax.random.normal(stream_key, dims, jnp.float32)
    if cuts:
        entries = entries * block_scale(stream_key, dims, cuts, -0.22, 0.18)
    return jnp.clip(strengthened(entries, jax.random.fold_in(stream_key, 3), *heavy), -most, most).astype(kind)


def setup_inputs(seed: int = 0) -> dict:
    key_list = jax.random.split(jax.random.key(seed), 10)
    return {
        "tokens": normal_values(key_list[0], (ISLANDS, TOKENS, D), 1.0, 6.0, ((0, 4), (1, 4), (2, 2))),
        "token_grads": normal_values(key_list[1], (ISLANDS, TOKENS, D), 1.0, 6.0, ((0, 4), (1, 4), (2, 2))),
        "slot_token": draw_slot_token(jax.random.fold_in(key_list[9], 71), 0),
        "slot_count": draw_slot_count(jax.random.fold_in(key_list[9], 71), 0),
        "slot_prob": jnp.clip(0.1 + 0.9 * jax.random.uniform(key_list[4], (ISLANDS, SOURCES, EXPERTS, CAP), jnp.float32) ** block_scale(key_list[4], (ISLANDS, SOURCES, EXPERTS, CAP), ((0, 4), (1, 4)), -0.2, 0.2), 0.1, 1.0),
        "gate_weight": normal_values(key_list[5], (ISLANDS, EXPERTS, D, FF), D ** -0.5, 0.125, ((0, 4), (1, 4), (3, 2))),
        "down_weight": normal_values(key_list[6], (ISLANDS, EXPERTS, FF, D), FF ** -0.5, 0.15625, ((0, 4), (1, 4), (2, 2))),
        "drift": bell_draw_with(key_list[7], (ISLANDS, EXPERTS, D, FF), 1.0, 6.0, ((0, 4), (1, 4), (3, 2)), (0, 2, 4, 2.0)),
        "momentum": normal_values(key_list[8], (EXPERTS, D, FF), 0.25, 1.5, ((0, 4), (2, 2)), jnp.float32),
    }


def island_pseudo(island_tokens, island_grads, island_slots, island_counts, island_probs, island_gate, island_down, island_drift):
    offsets = (jnp.arange(SOURCES, dtype=jnp.int32) * TOK_DEV)[:, None, None]
    slot_rows = (island_slots + offsets).astype(jnp.int32)
    live_slots = jnp.arange(CAP, dtype=jnp.int32)[None, None, :] < island_counts[:, :, None]
    input_slots = jnp.where(live_slots[..., None], island_tokens[slot_rows], jnp.zeros((), jnp.bfloat16))
    slot_weights = jnp.where(live_slots, island_probs, jnp.float32(0.0))[..., None]
    grad_slots = (slot_weights * island_grads[slot_rows].astype(jnp.float32)).astype(jnp.bfloat16)
    input_slots = input_slots.transpose(1, 0, 2, 3).reshape(EXPERTS, ROWS, D)
    grad_slots = grad_slots.transpose(1, 0, 2, 3).reshape(EXPERTS, ROWS, D)
    inputs_wide = input_slots.astype(jnp.float32)
    gate_value = jnp.einsum('erd,edf->erf', inputs_wide, island_gate.astype(jnp.float32))
    back_grad = jnp.einsum('erd,efd->erf', grad_slots.astype(jnp.float32), island_down.astype(jnp.float32))
    hidden_grad = (back_grad * jax.nn.silu(gate_value)).astype(jnp.bfloat16)
    gradient = jnp.einsum('erd,erf->edf', inputs_wide, hidden_grad.astype(jnp.float32))
    square_sum = jnp.sum(gradient * gradient)
    inner_scale = jnp.minimum(1.0, math.sqrt(EXPERTS * D * FF) / jnp.sqrt(square_sum + 1e-06))
    return island_drift.astype(jnp.float32) + inner_scale * gradient

def reference(tokens, token_grads, slot_token, slot_count, slot_prob, gate_weight, down_weight, drift, momentum):

    def accumulate(running, pieces):
        return (running + island_pseudo(*pieces), None)
    start = jnp.zeros((EXPERTS, D, FF), jnp.float32)
    total, _ = lax.scan(accumulate, start, (tokens, token_grads, slot_token, slot_count, slot_prob, gate_weight, down_weight, drift))
    average = total / ISLANDS
    square_sum = jnp.sum(average * average)
    outer_scale = jnp.minimum(1.0, 0.25 * math.sqrt(EXPERTS * D * FF) / jnp.sqrt(square_sum + 1e-06))
    clipped = outer_scale * average
    new_momentum = 0.9 * momentum + clipped
    outer_step = (0.7 * (clipped + 0.9 * new_momentum)).astype(jnp.bfloat16)
    return (new_momentum, outer_step)
```

```python
import functools
import math

import jax
import jax.numpy as jnp
from jax import lax
from jax.experimental import pallas as pl
from jax.experimental.pallas import tpu as pltpu
from jax.sharding import PartitionSpec as P

F32 = jnp.float32
BF16 = jnp.bfloat16
WIRE = jnp.float16


def partner(at, step, size):
    return at ^ step if size & (size - 1) == 0 else (at + step) % size


def origin(at, step, size):
    return at ^ step if size & (size - 1) == 0 else (at - step) % size


def swap(value, axis, step):
    size = lax.axis_size(axis)
    return lax.ppermute(value, axis, [(at, partner(at, step, size)) for at in range(size)])


def total(value, axes):
    for axis in axes:
        size = lax.axis_size(axis)
        if size & (size - 1):
            value = lax.psum(value, axis)
            continue
        step = 1
        while step < size:
            value = value + swap(value, axis, step)
            step *= 2
    return value


def update_kernel(place, factors, block, momentum, *rest):
    new_momentum, outer_step = rest[-2:]
    clipped = factors[0] * block[...]
    moved = 0.9 * momentum[0] + clipped
    new_momentum[0] = moved
    outer_step[0] = (0.7 * (clipped + 0.9 * moved)).astype(BF16)


def update_block(place, factor, block, momentum, outs):
    rows, columns = block.shape
    tile = rows // 4
    here = pl.BlockSpec((tile, columns), lambda r, place, factors: (r, 0))
    there = pl.BlockSpec(
        (1, tile, columns), lambda r, place, factors: (0, place[0] * 4 + r, place[1])
    )
    any_spec = pl.BlockSpec(memory_space=pl.ANY)
    return pl.pallas_call(
        update_kernel,
        grid_spec=pltpu.PrefetchScalarGridSpec(
            num_scalar_prefetch=2,
            grid=(4,),
            in_specs=[here, there] + [any_spec] * len(outs),
            out_specs=[there, there],
        ),
        out_shape=[
            jax.ShapeDtypeStruct(momentum.shape, F32),
            jax.ShapeDtypeStruct(momentum.shape, BF16),
        ],
        input_output_aliases={4 + n: n for n in range(len(outs))},
        compiler_params=pltpu.CompilerParams(vmem_limit_bytes=32 << 20),
        name="update_block",
    )(place, factor, block, momentum, *outs)


def body(
    tokens,
    token_grads,
    slot_token,
    slot_count,
    slot_prob,
    gate_weight,
    down_weight,
    drift,
    momentum,
):
    islands, experts, parts = (lax.axis_size(a) for a in ("island", "expert", "tensor"))
    island, expert, part = (lax.axis_index(a) for a in ("island", "expert", "tensor"))
    features, hidden = gate_weight.shape[2:]
    half = features // parts
    down, across = parts, islands // parts
    rows, columns = features // down, hidden // across
    entries = features * hidden * experts * parts

    def block_of(value, at):
        return lax.dynamic_slice(value, ((at // across) * rows, (at % across) * columns), (rows, columns))

    drift_block = block_of(drift[0, 0], island).astype(F32)
    drift_in = [
        swap(block_of(drift[0, 0], partner(island, d, islands)), "island", d)
        for d in range(1, islands)
    ]

    order = jnp.stack([partner(expert, d, experts) for d in range(experts)])
    table = slot_token[0, 0][order]
    filled = slot_count[0, 0][order]
    weights = slot_prob[0, 0][order]
    slots = table.shape[1]
    live = lax.broadcasted_iota(jnp.int32, table.shape, 1) < filled[:, None]
    picks = (
        (table[..., None] == lax.broadcasted_iota(jnp.int32, (1, 1, tokens.shape[1]), 2))
        & live[..., None]
    ).astype(BF16)
    input_slots = jnp.einsum("est,td->esd", picks, tokens[0], preferred_element_type=F32).astype(BF16)
    picked_grads = jnp.einsum("est,td->esd", picks, token_grads[0], preferred_element_type=F32)
    grad_slots = (weights[..., None] * picked_grads).astype(BF16)

    def routed(value):
        return [value[0]] + [swap(value[d], "expert", d) for d in range(1, experts)]

    inputs_in = routed(input_slots)
    grads_in = routed(grad_slots)
    inputs = jnp.concatenate(inputs_in)
    out_grads = jnp.concatenate(grads_in)

    inputs_all = [inputs] + [
        jnp.concatenate([swap(v, "tensor", t) for v in inputs_in]) for t in range(1, parts)
    ]
    grads_all = [out_grads] + [
        jnp.concatenate([swap(v, "tensor", t) for v in grads_in]) for t in range(1, parts)
    ]

    flat = [(i, t) for i in range(islands) for t in range(parts)]

    def send_features(d):
        pairs = []
        for at, t in flat:
            to = partner(at, d, islands)
            if t == to // across:
                pairs.append((at * parts + t, to * parts + t))
        return lax.ppermute(inputs, ("island", "tensor"), pairs)

    def spread(value):
        holder = island // across
        for t in range(1, parts):
            pairs = []
            for at in range(islands):
                keep = at // across
                pairs.append((at * parts + keep, at * parts + partner(keep, t, parts)))
            moved = lax.ppermute(value, ("island", "tensor"), pairs)
            value = jnp.where(part == partner(holder, t, parts), moved, value)
        return value

    def own_features():
        value = inputs
        holder = island // across
        for t in range(1, parts):
            value = jnp.where(part == partner(holder, t, parts), inputs_all[t], value)
        return value

    features_of = [own_features()] + [spread(send_features(d)) for d in range(1, islands)]

    def rows_of(weight, t, axis):
        return lax.dynamic_slice_in_dim(weight, origin(part, t, parts) * half, half, axis)

    gate_value = sum(
        jnp.einsum("rd,df->rf", v, rows_of(gate_weight[0, 0], t, 0), preferred_element_type=F32)
        for t, v in enumerate(inputs_all)
    )
    back_grad = sum(
        jnp.einsum("rd,fd->rf", v, rows_of(down_weight[0, 0], t, 1), preferred_element_type=F32)
        for t, v in enumerate(grads_all)
    )
    hidden_grad = (back_grad * jax.nn.silu(gate_value)).astype(BF16)

    def columns_of(value, at):
        return lax.dynamic_slice_in_dim(value, (at % across) * columns, columns, 1)

    hidden_of = [columns_of(hidden_grad, island)] + [
        swap(columns_of(hidden_grad, partner(island, d, islands)), "island", d)
        for d in range(1, islands)
    ]

    input_gram = sum(
        jnp.einsum("rd,sd->rs", v, v, preferred_element_type=F32) for v in inputs_all
    )
    hidden_gram = jnp.einsum("rf,sf->rs", hidden_grad, hidden_grad, preferred_element_type=F32)
    lanes = lax.broadcasted_iota(jnp.int32, (1, 128), 1)
    squares = jnp.where(lanes == island, jnp.sum(input_gram * hidden_gram), 0.0)
    squares = total(squares, ("tensor", "expert", "island"))
    scales = jnp.minimum(1.0, math.sqrt(entries) / jnp.sqrt(squares + 1e-06))

    average = drift_block
    for v in drift_in:
        average = average + v.astype(F32)
    for d in range(islands):
        gradient = jnp.einsum(
            "rd,rf->df", features_of[d], hidden_of[d], preferred_element_type=F32
        )
        average = average + scales[0, origin(island, d, islands)] * gradient
    average = average / islands

    peak = jnp.max(jnp.abs(average))
    peak = jnp.where(peak > 0, peak, 1.0)
    sent = (average / peak).astype(WIRE)
    blocks = [sent] + [swap(sent, "island", d) for d in range(1, islands)]

    notes = jnp.where(
        lanes == island, peak, jnp.where(lanes == islands, jnp.sum(average * average), 0.0)
    )
    notes = total(notes, ("island",))
    square = total(notes[:, islands : islands + 1], ("expert", "tensor"))
    clip = jnp.minimum(1.0, 0.25 * math.sqrt(entries) / jnp.sqrt(square[0, 0] + 1e-06))

    outs = []
    for d in range(islands):
        at = origin(island, d, islands)
        place = jnp.stack([at // across, at % across]).astype(jnp.int32)
        factor = (clip * notes[0, at])[None]
        outs = update_block(place, factor, blocks[d].astype(F32), momentum, outs)
    return tuple(outs)


def solution(mesh):
    return jax.shard_map(
        body,
        mesh=mesh,
        in_specs=(
            P("island", "expert", "tensor"),
            P("island", "expert", "tensor"),
            P("island", "expert", None, None),
            P("island", "expert", None),
            P("island", "expert", None, None),
            P("island", "expert", None, "tensor"),
            P("island", "expert", "tensor", None),
            P("island", "expert", None, "tensor"),
            P("expert", None, "tensor"),
        ),
        out_specs=(P("expert", None, "tensor"), P("expert", None, "tensor")),
        check_vma=False,
    )
```

```python
import math

import jax
import jax.numpy as jnp
from jax import lax
from jax.experimental import pallas as pl
from jax.experimental.pallas import tpu as pltpu
from jax.sharding import PartitionSpec as P

F32 = jnp.float32
BF16 = jnp.bfloat16
WIRE = jnp.float16
AXES = ("island", "expert", "tensor")

VMEM = pl.BlockSpec(memory_space=pltpu.VMEM)
SMEM = pl.BlockSpec(memory_space=pltpu.SMEM)
ANY = pl.BlockSpec(memory_space=pl.ANY)


def params(mib):
    return pltpu.CompilerParams(vmem_limit_bytes=mib << 20)


def partner(at, step, size):
    return at ^ step if size & (size - 1) == 0 else (at + step) % size


def origin(at, step, size):
    return at ^ step if size & (size - 1) == 0 else (at - step) % size


def swap(value, axis, step):
    size = lax.axis_size(axis)
    return lax.ppermute(value, axis, [(at, partner(at, step, size)) for at in range(size)])


def dot(a, b, contract):
    return lax.dot_general(a, b, (contract, ((), ())), preferred_element_type=F32)


def pick_kernel(experts, spot, table, count, weight, tokens, grads, *outs):
    slots = table.shape[-1]
    rows = lax.broadcasted_iota(jnp.int32, (slots, slots), 0)
    lanes = lax.broadcasted_iota(jnp.int32, (slots, slots), 1)

    def column(row):
        return jnp.sum(jnp.where(rows == lanes, row, 0), axis=1, keepdims=True)

    for d in range(experts):
        to = partner(spot[0], d, experts)
        live = lax.broadcasted_iota(jnp.int32, (slots, 1), 0) < count[0, 0, to]
        token = column(table[0, 0, pl.ds(to, 1), :].astype(F32)).astype(jnp.int32)
        chance = column(weight[0, 0, pl.ds(to, 1), :])
        ids = lax.broadcasted_iota(jnp.int32, (slots, tokens.shape[1]), 1)
        picks = jnp.where((ids == token) & live, 1.0, 0.0).astype(BF16)
        outs[d][...] = dot(picks, tokens[0], ((1,), (0,))).astype(BF16)
        picked = dot(picks, grads[0], ((1,), (0,)))
        outs[experts + d][...] = (chance * picked).astype(BF16)


def gather_kernel(pieces, blocks, *refs):
    inputs, drifts = refs[:pieces], refs[pieces : pieces + blocks]
    joined, turned, drift_sum = refs[pieces + blocks :]
    slots = inputs[0].shape[0]
    for n, piece in enumerate(inputs):
        joined[n * slots : (n + 1) * slots, :] = piece[...]
    turned[...] = joined[...].T
    added = drifts[0][...].astype(F32)
    for other in drifts[1:]:
        added = added + other[...].astype(F32)
    drift_sum[...] = added


def gate_kernel(parts, spot, weight, *refs):
    inputs, (silu, gram) = refs[:parts], refs[parts:]
    half = inputs[0].shape[1]
    value = 0.0
    squares = 0.0
    for t in range(parts):
        start = pl.multiple_of(origin(spot[1], t, parts) * half, half)
        features = inputs[t][...]
        value = value + dot(features, weight[0, 0, pl.ds(start, half), :], ((1,), (0,)))
        squares = squares + dot(features, features, ((1,), (1,)))
    silu[...] = value / (1.0 + jnp.exp(-value))
    gram[...] = squares


def hidden_kernel(parts, pieces, across, spot, weight, silu, gram, *refs):
    grads = refs[: parts * pieces]
    outs = refs[-across - 2 : -2]
    norms, joined = refs[-2:]
    slots, half = grads[0].shape
    columns = silu.shape[1] // across
    for t in range(parts):
        for n in range(pieces):
            joined[t, n * slots : (n + 1) * slots, :] = grads[t * pieces + n][...]
    squares = 0.0
    for r in range(across):
        first = pl.multiple_of(partner(spot[2], r, across) * columns, columns)
        value = 0.0
        for t in range(parts):
            start = pl.multiple_of(origin(spot[1], t, parts) * half, half)
            block = weight[0, 0, pl.ds(first, columns), pl.ds(start, half)]
            value = value + dot(joined[t], block, ((1,), (1,)))
        rounded = (value * silu[:, pl.ds(first, columns)]).astype(BF16)
        outs[r][...] = rounded
        squares = squares + dot(rounded, rounded, ((1,), (1,)))
    norms[...] = jnp.full(norms.shape, jnp.sum(squares * gram[...]), F32)


def average_kernel(islands, entries, spot, norms, drift_sum, *refs):
    inputs, hiddens = refs[:islands], refs[islands : 2 * islands]
    scaled, notes, total = refs[-3:]
    group = norms.shape[0] // islands
    average = drift_sum[...]
    for d in range(islands):
        at = origin(spot[3], d, islands)
        square = jnp.sum(norms[pl.ds(at * group, group)], axis=0)[:1, :1]
        scale = jnp.minimum(1.0, math.sqrt(entries) / jnp.sqrt(square + 1e-06))
        average = average + scale * dot(inputs[d][...], hiddens[d][...], ((1,), (0,)))
    average = average / islands
    total[...] = average
    peak = jnp.max(jnp.abs(average))
    peak = jnp.where(peak > 0, peak, 1.0)
    scaled[...] = total[...] / peak
    sublane = lax.broadcasted_iota(jnp.int32, notes.shape, 1)
    notes[...] = jnp.where(sublane == 0, jnp.sum(average * average), peak)


def update_kernel(entries, place, notes, block, momentum, *rest):
    new_momentum, outer_step = rest[-2:]
    square = jnp.sum(notes[...], axis=0)[:1, :1]
    clip = jnp.minimum(1.0, 0.25 * math.sqrt(entries) / jnp.sqrt(square + 1e-06))
    peak = notes[pl.ds(place[2], 1)][0, 1:2, :1]
    clipped = (clip * peak) * block[...]
    moved = 0.9 * momentum[0] + clipped
    new_momentum[0] = moved
    outer_step[0] = (0.7 * (clipped + 0.9 * moved)).astype(BF16)


def update_block(entries, place, notes, block, momentum, outs):
    rows, columns = block.shape
    steps = 2
    tile = rows // steps
    here = pl.BlockSpec((tile, columns), lambda r, place: (r, 0))
    there = pl.BlockSpec(
        (1, tile, columns), lambda r, place: (0, place[0] * steps + r, place[1])
    )
    whole = pl.BlockSpec(notes.shape, lambda r, place: (0, 0, 0))
    return pl.pallas_call(
        lambda *refs: update_kernel(entries, *refs),
        grid_spec=pltpu.PrefetchScalarGridSpec(
            num_scalar_prefetch=1,
            grid=(steps,),
            in_specs=[whole, here, there] + [ANY] * len(outs),
            out_specs=[there, there],
        ),
        out_shape=[
            jax.ShapeDtypeStruct(momentum.shape, F32),
            jax.ShapeDtypeStruct(momentum.shape, BF16),
        ],
        input_output_aliases={4 + n: n for n in range(len(outs))},
        compiler_params=params(32),
        name="update_block",
    )(place, notes, block, momentum, *outs)


def body(
    tokens,
    token_grads,
    slot_token,
    slot_count,
    slot_prob,
    gate_weight,
    down_weight,
    drift,
    momentum,
):
    islands, experts, parts = (lax.axis_size(a) for a in AXES)
    island, expert, part = (lax.axis_index(a) for a in AXES)
    devices = islands * experts * parts
    features, hidden = gate_weight.shape[2:]
    half = features // parts
    across = islands // parts
    columns = hidden // across
    entries = features * hidden * experts * parts
    slots = slot_token.shape[3]
    routed_rows = experts * slots
    spot = jnp.stack([expert, part, island % across, island]).astype(jnp.int32)

    piece = jax.ShapeDtypeStruct((slots, half), BF16)
    picked = pl.pallas_call(
        lambda *refs: pick_kernel(experts, *refs),
        in_specs=[SMEM, VMEM, SMEM, VMEM, VMEM, VMEM],
        out_specs=[VMEM] * (2 * experts),
        out_shape=[piece] * (2 * experts),
        compiler_params=params(32),
        name="pick_slots",
    )(spot, slot_token, slot_count, slot_prob, tokens, token_grads)

    def routed(values):
        return [values[0]] + [swap(values[d], "expert", d) for d in range(1, experts)]

    inputs_in = routed(picked[:experts])

    def block_of(at):
        return lax.dynamic_slice(
            drift[0, 0], ((at // across) * half, (at % across) * columns), (half, columns)
        )

    drift_in = [block_of(island)] + [
        swap(block_of(partner(island, d, islands)), "island", d) for d in range(1, islands)
    ]
    grads_in = routed(picked[experts:])
    inputs, turned, drift_sum = pl.pallas_call(
        lambda *refs: gather_kernel(experts, islands, *refs),
        in_specs=[VMEM] * (experts + islands),
        out_specs=[VMEM] * 3,
        out_shape=[
            jax.ShapeDtypeStruct((routed_rows, half), BF16),
            jax.ShapeDtypeStruct((half, routed_rows), BF16),
            jax.ShapeDtypeStruct((half, columns), F32),
        ],
        compiler_params=params(40),
        name="join_inputs",
    )(*inputs_in, *drift_in)

    inputs_all = [inputs] + [swap(inputs, "tensor", t) for t in range(1, parts)]

    def send_features(d):
        pairs = []
        for at in range(islands):
            to = partner(at, d, islands)
            holder = to // across
            pairs.append((at * parts + holder, to * parts + holder))
        return lax.ppermute(turned, ("island", "tensor"), pairs)

    def spread(value):
        holder = island // across
        result = value
        for t in range(1, parts):
            pairs = []
            for at in range(islands):
                keep = at // across
                pairs.append((at * parts + keep, at * parts + partner(keep, t, parts)))
            moved = lax.ppermute(value, ("island", "tensor"), pairs)
            result = jnp.where(part == partner(holder, t, parts), moved, result)
        return result

    features_of = [spread(turned)] + [spread(send_features(d)) for d in range(1, islands)]

    silu, gram = pl.pallas_call(
        lambda *refs: gate_kernel(parts, *refs),
        in_specs=[SMEM] + [VMEM] * (1 + parts),
        out_specs=[VMEM] * 2,
        out_shape=[
            jax.ShapeDtypeStruct((routed_rows, hidden), F32),
            jax.ShapeDtypeStruct((routed_rows, routed_rows), F32),
        ],
        compiler_params=params(40),
        name="gate_values",
    )(spot, gate_weight, *inputs_all)

    grads_all = [g for t in range(1, parts) for g in [swap(v, "tensor", t) for v in grads_in]]
    grads_all = list(grads_in) + grads_all
    hidden_piece = jax.ShapeDtypeStruct((routed_rows, columns), BF16)
    *hidden_out, norms = pl.pallas_call(
        lambda *refs: hidden_kernel(parts, experts, across, *refs),
        in_specs=[SMEM] + [VMEM] * (3 + len(grads_all)) + [ANY] * islands,
        out_specs=[VMEM] * (across + 1),
        out_shape=[hidden_piece] * across + [jax.ShapeDtypeStruct((devices, 8, 128), F32)],
        scratch_shapes=[pltpu.VMEM((parts, routed_rows, half), BF16)],
        compiler_params=params(40),
        name="hidden_grads",
    )(spot, down_weight, silu, gram, *grads_all, *features_of)

    def hidden_for(d):
        if islands & (islands - 1) == 0:
            return hidden_out[d % across]
        at = partner(island, d, islands) % across
        step = (at - island) % across
        return lax.select_n(step, *hidden_out) if across > 2 else jnp.where(step == 0, *hidden_out)

    hidden_of = [hidden_out[0]] + [
        swap(hidden_for(d), "island", d) for d in range(1, islands)
    ]
    norms = lax.all_to_all(norms, AXES, split_axis=0, concat_axis=0, tiled=True)

    scaled, notes = pl.pallas_call(
        lambda *refs: average_kernel(islands, entries, *refs),
        in_specs=[SMEM] + [VMEM] * (2 + 2 * islands),
        out_specs=[VMEM] * 2,
        out_shape=[
            jax.ShapeDtypeStruct((half, columns), F32),
            jax.ShapeDtypeStruct((devices, 8, 128), F32),
        ],
        scratch_shapes=[pltpu.VMEM((half, columns), F32)],
        compiler_params=params(40),
        name="average_block",
    )(spot, norms, drift_sum, *features_of, *hidden_of)
    notes = lax.all_to_all(notes, AXES, split_axis=0, concat_axis=0, tiled=True)

    sent = lax.optimization_barrier([h.astype(WIRE) for h in jnp.split(scaled, 2)])
    if islands == 4:
        first = [[sent[0], swap(sent[0], "island", 1), swap(sent[0], "island", 2), None]]
        second = [[sent[1], swap(sent[1], "island", 1), swap(sent[1], "island", 2), None]]
        first[0][3] = swap(first[0][1], "island", 2)
        second[0][3] = swap(second[0][2], "island", 1)
        halves = first + second
    else:
        halves = [[h] + [swap(h, "island", d) for d in range(1, islands)] for h in sent]

    outs = []
    for d in range(islands):
        at = origin(island, d, islands)
        source = (at * experts + expert) * parts + part
        for n in range(2):
            place = jnp.stack([(at // across) * 2 + n, at % across, source]).astype(jnp.int32)
            block = halves[n][d].astype(F32)
            outs = update_block(entries, place, notes, block, momentum, outs)
    return tuple(outs)


def solution(mesh):
    return jax.shard_map(
        body,
        mesh=mesh,
        in_specs=(
            P("island", "expert", "tensor"),
            P("island", "expert", "tensor"),
            P("island", "expert", None, None),
            P("island", "expert", None),
            P("island", "expert", None, None),
            P("island", "expert", None, "tensor"),
            P("island", "expert", "tensor", None),
            P("island", "expert", None, "tensor"),
            P("expert", None, "tensor"),
        ),
        out_specs=(P("expert", None, "tensor"), P("expert", None, "tensor")),
        check_vma=False,
    )
```

```python
import math

import jax
import jax.numpy as jnp
from jax import lax
from jax.experimental import pallas as pl
from jax.experimental.pallas import tpu as pltpu
from jax.sharding import PartitionSpec as P

F32 = jnp.float32
BF16 = jnp.bfloat16
WIRE = jnp.float16
AXES = ("island", "expert", "tensor")

VMEM = pl.BlockSpec(memory_space=pltpu.VMEM)
SMEM = pl.BlockSpec(memory_space=pltpu.SMEM)
ANY = pl.BlockSpec(memory_space=pl.ANY)


def params(mib):
    return pltpu.CompilerParams(vmem_limit_bytes=mib << 20)


def partner(at, step, size):
    return at ^ step if size & (size - 1) == 0 else (at + step) % size


def origin(at, step, size):
    return at ^ step if size & (size - 1) == 0 else (at - step) % size


def swap(value, axis, step):
    size = lax.axis_size(axis)
    return lax.ppermute(value, axis, [(at, partner(at, step, size)) for at in range(size)])


def dot(a, b, contract):
    return lax.dot_general(a, b, (contract, ((), ())), preferred_element_type=F32)


def pick_kernel(experts, islands, spot, table, count, weight, tokens, grads, drift, *refs):
    outs, blocks, sems = refs[:experts], refs[experts : experts + islands], refs[-1]
    across = spot[4]
    block_rows, block_columns = blocks[0].shape
    copies = []
    for d in range(islands):
        at = partner(spot[3], d, islands)
        top = pl.multiple_of(lax.div(at, across) * block_rows, block_rows)
        left = pl.multiple_of(lax.rem(at, across) * block_columns, block_columns)
        source = drift.at[0, 0, pl.ds(top, block_rows), pl.ds(left, block_columns)]
        copies.append(pltpu.make_async_copy(source, blocks[d], sems.at[d]))
        copies[-1].start()

    slots = table.shape[-1]
    rows = lax.broadcasted_iota(jnp.int32, (slots, slots), 0)
    lanes = lax.broadcasted_iota(jnp.int32, (slots, slots), 1)

    def column(row):
        return jnp.sum(jnp.where(rows == lanes, row, 0), axis=1, keepdims=True)

    for d in range(experts):
        to = partner(spot[0], d, experts)
        live = lax.broadcasted_iota(jnp.int32, (slots, 1), 0) < count[0, 0, to]
        token = column(table[0, 0, pl.ds(to, 1), :].astype(F32)).astype(jnp.int32)
        chance = column(weight[0, 0, pl.ds(to, 1), :])
        ids = lax.broadcasted_iota(jnp.int32, (slots, tokens.shape[1]), 1)
        picks = jnp.where((ids == token) & live, 1.0, 0.0).astype(BF16)
        outs[d][:slots, :] = dot(picks, tokens[0], ((1,), (0,))).astype(BF16)
        picked = dot(picks, grads[0], ((1,), (0,)))
        outs[d][slots:, :] = (chance * picked).astype(BF16)
    for copy in copies:
        copy.wait()


def join_kernel(pieces, blocks, *refs):
    arrived, drifts = refs[:pieces], refs[pieces : pieces + blocks]
    joined, turned, drift_sum = refs[pieces + blocks :]
    slots = arrived[0].shape[0] // 2
    for n, piece in enumerate(arrived):
        joined[n * slots : (n + 1) * slots, :] = piece[:slots, :]
        joined[(pieces + n) * slots : (pieces + n + 1) * slots, :] = piece[slots:, :]
    turned[...] = joined[: pieces * slots, :].T
    added = drifts[0][...].astype(F32)
    for other in drifts[1:]:
        added = added + other[...].astype(F32)
    drift_sum[...] = added


def hidden_kernel(parts, across, spot, gate, down, *refs):
    joined = refs[:parts]
    outs, norms = refs[parts:-1], refs[-1]
    rows, half = joined[0].shape[0] // 2, joined[0].shape[1]
    columns = outs[0].shape[1]
    starts = [pl.multiple_of(origin(spot[1], t, parts) * half, half) for t in range(parts)]
    hidden_gram = 0.0
    for r in range(across):
        first = pl.multiple_of(partner(spot[2], r, across) * columns, columns)
        value = 0.0
        back = 0.0
        for t in range(parts):
            block = gate[0, 0, pl.ds(starts[t], half), pl.ds(first, columns)]
            value = value + dot(joined[t][:rows, :], block, ((1,), (0,)))
            block = down[0, 0, pl.ds(first, columns), pl.ds(starts[t], half)]
            back = back + dot(joined[t][rows:, :], block, ((1,), (1,)))
        rounded = (back * (value / (1.0 + jnp.exp(-value)))).astype(BF16)
        outs[r][...] = rounded
        hidden_gram = hidden_gram + dot(rounded, rounded, ((1,), (1,)))
    input_gram = 0.0
    for t in range(parts):
        inputs = joined[t][:rows, :]
        input_gram = input_gram + dot(inputs, inputs, ((1,), (1,)))
    norms[...] = jnp.full(norms.shape, jnp.sum(hidden_gram * input_gram), F32)


def average_kernel(islands, entries, spot, norms, drift_sum, *refs):
    hiddens = refs[4 : 4 + islands]
    scaled, notes, inputs, total, sems = refs[-5:]

    def fetch(own, rest):
        pltpu.make_async_copy(own, inputs.at[0], sems.at[0]).start()
        for d in range(1, islands):
            pltpu.make_async_copy(rest.at[d - 1], inputs.at[d], sems.at[d]).start()

    pl.when(spot[5] == 1)(lambda: fetch(refs[0], refs[2]))
    pl.when(spot[5] != 1)(lambda: fetch(refs[1], refs[3]))

    group = norms.shape[0] // islands
    average = drift_sum[...]
    for d in range(islands):
        at = origin(spot[3], d, islands)
        square = jnp.sum(norms[pl.ds(at * group, group)], axis=0)[:1, :1]
        scale = jnp.minimum(1.0, math.sqrt(entries) / jnp.sqrt(square + 1e-06))
        pltpu.make_async_copy(refs[0], inputs.at[d], sems.at[d]).wait()
        average = average + scale * dot(inputs[d], hiddens[d][...], ((1,), (0,)))
    average = average / islands
    total[...] = average
    unit = jnp.maximum(jnp.max(jnp.abs(average)), 1e-30) / 32768
    scaled[...] = total[...] * (1 / unit)
    sublane = lax.broadcasted_iota(jnp.int32, notes.shape, 1)
    notes[...] = jnp.where(sublane == 0, jnp.sum(average * average), unit)


def copy_all(sems, pairs):
    copies = [pltpu.make_async_copy(*pair, sems.at[n]) for n, pair in enumerate(pairs)]
    for copy in copies:
        copy.start()
    for copy in copies:
        copy.wait()


def hand_kernel(count, norms, *refs):
    passed, joined, sems = refs[count:]
    pairs = [(refs[n], joined.at[n]) for n in range(count)] + [(norms, passed)]
    copy_all(sems, pairs)


def pass_kernel(count, notes, *refs):
    copy_all(refs[-1], [(refs[n], refs[count + n]) for n in range(count)])


def update_kernel(entries, place, notes, block, momentum, *rest):
    new_momentum, outer_step = rest[-2:]
    square = jnp.sum(notes[...], axis=0)[:1, :1]
    clip = jnp.minimum(1.0, 0.25 * math.sqrt(entries) / jnp.sqrt(square + 1e-06))
    unit = notes[pl.ds(place[2], 1)][0, 1:2, :1]
    clipped = (clip * unit) * block[...]
    moved = 0.9 * momentum[0] + clipped
    new_momentum[0] = moved
    outer_step[0] = (0.7 * (clipped + 0.9 * moved)).astype(BF16)


def update_block(entries, place, notes, block, momentum, outs):
    rows, columns = block.shape
    steps = 2
    tile = rows // steps
    here = pl.BlockSpec((tile, columns), lambda r, place: (r, 0))
    there = pl.BlockSpec(
        (1, tile, columns), lambda r, place: (0, place[0] * steps + r, place[1])
    )
    whole = pl.BlockSpec(notes.shape, lambda r, place: (0, 0, 0))
    return pl.pallas_call(
        lambda *refs: update_kernel(entries, *refs),
        grid_spec=pltpu.PrefetchScalarGridSpec(
            num_scalar_prefetch=1,
            grid=(steps,),
            in_specs=[whole, here, there] + [ANY] * len(outs),
            out_specs=[there, there],
        ),
        out_shape=[
            jax.ShapeDtypeStruct(momentum.shape, F32),
            jax.ShapeDtypeStruct(momentum.shape, BF16),
        ],
        input_output_aliases={4 + n: n for n in range(len(outs))},
        compiler_params=params(32),
        name="update_block",
    )(place, notes, block, momentum, *outs)


def body(
    tokens,
    token_grads,
    slot_token,
    slot_count,
    slot_prob,
    gate_weight,
    down_weight,
    drift,
    momentum,
):
    islands, experts, parts = (lax.axis_size(a) for a in AXES)
    island, expert, part = (lax.axis_index(a) for a in AXES)
    devices = islands * experts * parts
    features, hidden = gate_weight.shape[2:]
    half = features // parts
    across = islands // parts
    columns = hidden // across
    entries = features * hidden * experts * parts
    slots = slot_token.shape[3]
    routed_rows = experts * slots
    holder = island // across
    spot = jnp.stack(
        [expert, part, island % across, island, jnp.int32(across), (part == holder).astype(jnp.int32)]
    ).astype(jnp.int32)
    drift_block = jax.ShapeDtypeStruct((half, columns), BF16)

    picked = pl.pallas_call(
        lambda *refs: pick_kernel(experts, islands, *refs),
        in_specs=[SMEM, VMEM, SMEM, VMEM, VMEM, VMEM, ANY],
        out_specs=[VMEM] * experts + [ANY] * islands,
        out_shape=[jax.ShapeDtypeStruct((2 * slots, half), BF16)] * experts
        + [drift_block] * islands,
        scratch_shapes=[pltpu.SemaphoreType.DMA((islands,))],
        compiler_params=params(32),
        name="pick_slots",
    )(spot, slot_token, slot_count, slot_prob, tokens, token_grads, drift)
    arrived = [picked[0]] + [swap(picked[d], "expert", d) for d in range(experts - 1, 0, -1)]
    blocks = picked[experts:]
    drift_in = [blocks[0]] + [swap(blocks[d], "island", d) for d in range(1, islands)]
    joined, turned, drift_sum = pl.pallas_call(
        lambda *refs: join_kernel(experts, islands, *refs),
        in_specs=[VMEM] * (experts + islands),
        out_specs=[VMEM] * 3,
        out_shape=[
            jax.ShapeDtypeStruct((2 * routed_rows, half), BF16),
            jax.ShapeDtypeStruct((half, routed_rows), BF16),
            jax.ShapeDtypeStruct((half, columns), F32),
        ],
        compiler_params=params(40),
        name="join_slots",
    )(*arrived, *drift_in)

    joined_all = [joined] + [swap(joined, "tensor", t) for t in range(1, parts)]

    def send_features(d):
        pairs = []
        for at in range(islands):
            to = partner(at, d, islands)
            pairs.append((at * parts + to // across, to * parts + to // across))
        return lax.ppermute(turned, ("island", "tensor"), pairs)

    def spread(value):
        result = value
        for t in range(1, parts):
            pairs = []
            for at in range(islands):
                keep = at // across
                pairs.append((at * parts + keep, at * parts + partner(keep, t, parts)))
            moved = lax.ppermute(value, ("island", "tensor"), pairs)
            result = moved if t == 1 else result + moved
        return result

    features_in = [send_features(d) for d in range(1, islands)]
    turned_moved = spread(turned)

    hidden_piece = jax.ShapeDtypeStruct((routed_rows, columns), BF16)
    *hidden_out, norms = pl.pallas_call(
        lambda *refs: hidden_kernel(parts, across, *refs),
        in_specs=[SMEM] + [VMEM] * (2 + parts),
        out_specs=[VMEM] * (across + 1),
        out_shape=[hidden_piece] * across + [jax.ShapeDtypeStruct((devices, 8, 128), F32)],
        compiler_params=params(48),
        name="hidden_grads",
    )(spot, gate_weight, down_weight, *joined_all)

    def hidden_for(d):
        at = partner(island, d, islands) % across
        if islands & (islands - 1) == 0:
            return hidden_out[d % across]
        return lax.select_n((at - island) % across, *hidden_out)

    hidden_of = [hidden_out[0]] + [
        swap(hidden_for(d), "island", d) for d in range(1, islands)
    ]
    norms, features_in = pl.pallas_call(
        lambda *refs: hand_kernel(islands - 1, *refs),
        in_specs=[ANY] * islands,
        out_specs=[ANY] * 2,
        out_shape=[
            jax.ShapeDtypeStruct(norms.shape, F32),
            jax.ShapeDtypeStruct((islands - 1, half, routed_rows), BF16),
        ],
        scratch_shapes=[pltpu.SemaphoreType.DMA((islands,))],
        compiler_params=params(16),
        name="hand_features",
    )(norms, *features_in)
    features_moved = spread(features_in)
    norms = lax.all_to_all(norms, AXES, split_axis=0, concat_axis=0, tiled=True)

    scaled, notes = pl.pallas_call(
        lambda *refs: average_kernel(islands, entries, *refs),
        in_specs=[SMEM, VMEM, VMEM] + [ANY] * 4 + [VMEM] * islands,
        out_specs=[VMEM] * 2,
        out_shape=[
            jax.ShapeDtypeStruct((half, columns), F32),
            jax.ShapeDtypeStruct((devices, 8, 128), F32),
        ],
        scratch_shapes=[
            pltpu.VMEM((islands, half, routed_rows), BF16),
            pltpu.VMEM((half, columns), F32),
            pltpu.SemaphoreType.DMA((islands,)),
        ],
        compiler_params=params(48),
        name="average_block",
    )(spot, norms, drift_sum, turned, turned_moved, features_in, features_moved, *hidden_of)
    notes = lax.all_to_all(notes, AXES, split_axis=0, concat_axis=0, tiled=True)

    rounded = lax.reduce_precision(scaled, 5, 10)
    own = [rounded[: half // 2], rounded[half // 2 :]]
    sent = [h.astype(WIRE) for h in own]
    if islands == 4:
        later = pl.pallas_call(
            lambda *refs: pass_kernel(2, *refs),
            in_specs=[ANY] * 3,
            out_specs=[ANY] * 2,
            out_shape=[jax.ShapeDtypeStruct(h.shape, F32) for h in own],
            scratch_shapes=[pltpu.SemaphoreType.DMA((2,))],
            compiler_params=params(16),
            name="pass_halves",
        )(notes, *own)
        later = [h.astype(WIRE) for h in later]
        beside = swap(sent[0], "island", 1)
        below = swap(sent[1], "island", 2)
        halves = [
            [own[0], beside, swap(later[0], "island", 2), swap(beside, "island", 2)],
            [own[1], swap(later[1], "island", 1), below, swap(below, "island", 1)],
        ]
    else:
        halves = [[o] + [swap(h, "island", d) for d in range(1, islands)] for o, h in zip(own, sent)]

    outs = []
    for d in range(islands):
        at = origin(island, d, islands)
        source = (at * experts + expert) * parts + part
        for n in range(2):
            place = jnp.stack([(at // across) * 2 + n, at % across, source]).astype(jnp.int32)
            block = halves[n][d].astype(F32)
            outs = update_block(entries, place, notes, block, momentum, outs)
    return tuple(outs)


def solution(mesh):
    return jax.shard_map(
        body,
        mesh=mesh,
        in_specs=(
            P("island", "expert", "tensor"),
            P("island", "expert", "tensor"),
            P("island", "expert", None, None),
            P("island", "expert", None),
            P("island", "expert", None, None),
            P("island", "expert", None, "tensor"),
            P("island", "expert", "tensor", None),
            P("island", "expert", None, "tensor"),
            P("expert", None, "tensor"),
        ),
        out_specs=(P("expert", None, "tensor"), P("expert", None, "tensor")),
        check_vma=False,
    )
```

```python
import math

import jax
import jax.numpy as jnp
from jax import lax
from jax.experimental import pallas as pl
from jax.experimental.pallas import tpu as pltpu
from jax.sharding import PartitionSpec as P

F32 = jnp.float32
BF16 = jnp.bfloat16
WIRE = jnp.float16
AXES = ("island", "expert", "tensor")

VMEM = pl.BlockSpec(memory_space=pltpu.VMEM)
SMEM = pl.BlockSpec(memory_space=pltpu.SMEM)
ANY = pl.BlockSpec(memory_space=pl.ANY)


def params(mib):
    return pltpu.CompilerParams(vmem_limit_bytes=mib << 20)


def partner(at, step, size):
    return at ^ step if size & (size - 1) == 0 else (at + step) % size


def origin(at, step, size):
    return at ^ step if size & (size - 1) == 0 else (at - step) % size


def swap(value, axis, step):
    size = lax.axis_size(axis)
    return lax.ppermute(value, axis, [(at, partner(at, step, size)) for at in range(size)])


def dot(a, b, contract):
    return lax.dot_general(a, b, (contract, ((), ())), preferred_element_type=F32)


def copy_all(sems, pairs):
    copies = [pltpu.make_async_copy(*pair, sems.at[n]) for n, pair in enumerate(pairs)]
    for copy in copies:
        copy.start()
    return copies


def pick_kernel(experts, islands, pieces, spot, *refs):
    sources, drift = refs[:5], refs[5]
    outs, blocks = refs[6 : 6 + experts], refs[6 + experts : -6]
    table, count, weight, tokens, grads, sems = refs[-6:]
    loads = copy_all(sems, list(zip(sources, refs[-6:-1])))
    rows, columns = blocks[0].shape
    pairs = []
    for d, first, count_rows, target, at_row in pieces:
        at = partner(spot[3], d, islands)
        top = pl.multiple_of(lax.div(at, spot[4]) * rows, rows) + first
        left = pl.multiple_of(lax.rem(at, spot[4]) * columns, columns)
        pairs.append(
            (
                drift.at[0, 0, pl.ds(top, count_rows), pl.ds(left, columns)],
                blocks[target].at[pl.ds(at_row, count_rows)],
            )
        )
    copies = copy_all(sems.at[pl.ds(5, len(pairs))], pairs)
    for copy in loads:
        copy.wait()

    slots = table.shape[-1]
    rows = lax.broadcasted_iota(jnp.int32, (slots, slots), 0)
    lanes = lax.broadcasted_iota(jnp.int32, (slots, slots), 1)

    def column(row):
        return jnp.sum(jnp.where(rows == lanes, row, 0), axis=1, keepdims=True)

    for d in range(experts):
        to = partner(spot[0], d, experts)
        live = lax.broadcasted_iota(jnp.int32, (slots, 1), 0) < count[0, 0, to]
        token = column(table[0, 0, pl.ds(to, 1), :].astype(F32)).astype(jnp.int32)
        chance = column(weight[0, 0, pl.ds(to, 1), :])
        ids = lax.broadcasted_iota(jnp.int32, (slots, tokens.shape[1]), 1)
        picks = jnp.where((ids == token) & live, 1.0, 0.0).astype(BF16)
        outs[d][:slots, :] = dot(picks, tokens[0], ((1,), (0,))).astype(BF16)
        picked = dot(picks, grads[0], ((1,), (0,)))
        outs[d][slots:, :] = (chance * picked).astype(BF16)
    for copy in copies:
        copy.wait()


def join_kernel(count, blocks, *refs):
    arrived, drifts = refs[:count], refs[count : count + blocks]
    joined, turned, drift_sum = refs[count + blocks : count + blocks + 3]
    slots = arrived[0].shape[0] // 2
    rows = drift_sum.shape[0]
    for n, ref in enumerate(refs[count + blocks + 3 :]):
        ref[...] = drifts[1 + n][rows:, :]
    for n, piece in enumerate(arrived):
        joined[n * slots : (n + 1) * slots, :] = piece[:slots, :]
        joined[(count + n) * slots : (count + n + 1) * slots, :] = piece[slots:, :]
    turned[...] = joined[: count * slots, :].T
    added = drifts[0][...].astype(F32)
    for other in drifts[1:]:
        added = added + other[:rows, :].astype(F32)
    drift_sum[...] = added


def hidden_kernel(parts, across, spot, gate, down, *refs):
    joined, outs = refs[:parts], refs[parts : parts + across]
    norms, gate_part, down_part, inputs, sems = refs[parts + across :]
    rows, half = joined[0].shape[0] // 2, joined[0].shape[1]
    columns = outs[0].shape[1]
    loads = [[pltpu.make_async_copy(joined[t], inputs.at[t], sems.at[t])] for t in range(parts)]
    for r in range(across):
        first = pl.multiple_of(partner(spot[2], r, across) * columns, columns)
        at = parts + 2 * r
        loads.append(
            [
                pltpu.make_async_copy(
                    gate.at[0, 0, :, pl.ds(first, columns)], gate_part.at[r], sems.at[at]
                ),
                pltpu.make_async_copy(
                    down.at[0, 0, pl.ds(first, columns), :], down_part.at[r], sems.at[at + 1]
                ),
            ]
        )
    for group in loads:
        for copy in group:
            copy.start()
    starts = [pl.multiple_of(origin(spot[1], t, parts) * half, half) for t in range(parts)]
    input_gram = 0.0
    for t in range(parts):
        loads[t][0].wait()
        features = inputs[t, :rows, :]
        input_gram = input_gram + dot(features, features, ((1,), (1,)))
    hidden_gram = 0.0
    for r in range(across):
        value = 0.0
        back = 0.0
        loads[parts + r][0].wait()
        for t in range(parts):
            block = gate_part[r, pl.ds(starts[t], half), :]
            value = value + dot(inputs[t, :rows, :], block, ((1,), (0,)))
        loads[parts + r][1].wait()
        for t in range(parts):
            block = down_part[r, :, pl.ds(starts[t], half)]
            back = back + dot(inputs[t, rows:, :], block, ((1,), (1,)))
        rounded = (back * (value / (1.0 + jnp.exp(-value)))).astype(BF16)
        outs[r][...] = rounded
        hidden_gram = hidden_gram + dot(rounded, rounded, ((1,), (1,)))
    norms[...] = jnp.full(norms.shape, jnp.sum(hidden_gram * input_gram), F32)


def average_kernel(islands, entries, tiles, relays, spot, norms, *refs):
    drift_sum, own, moved = refs[:3]
    handed = refs[3 + islands : 3 + islands + relays]
    scaled, notes, inputs, hiddens, total, extra, sems = refs[-7:]
    rows = total.shape[0] // tiles
    across = [pltpu.make_async_copy(refs[3 + d], hiddens.at[d], sems.at[0, d]) for d in range(islands)]
    if handed:
        size = handed[0].shape[0]
        for n, ref in enumerate(handed):
            place = extra.at[pl.ds(n * size, size)]
            across.append(pltpu.make_async_copy(ref, place, sems.at[0, islands + n]))
    for copy in across:
        copy.start()

    def part(m):
        return pl.ds(m * rows, rows)

    def fetch(features):
        for m in range(tiles):
            pltpu.make_async_copy(drift_sum.at[part(m)], total.at[part(m)], sems.at[1 + m, islands]).start()
            for d in range(islands):
                source = features.at[d, part(m)]
                pltpu.make_async_copy(source, inputs.at[d, part(m)], sems.at[1 + m, d]).start()

    pl.when(spot[5] == 1)(lambda: fetch(own))
    pl.when(spot[5] != 1)(lambda: fetch(moved))

    group = norms.shape[0] // islands
    scales = []
    for d in range(islands):
        at = origin(spot[3], d, islands)
        square = jnp.sum(norms[pl.ds(at * group, group)], axis=0)[:1, :1]
        scales.append(jnp.minimum(1.0, math.sqrt(entries) / jnp.sqrt(square + 1e-06)) / islands)
    for copy in across:
        copy.wait()
    square = 0.0
    peak = 0.0
    for m in range(tiles):
        pltpu.make_async_copy(drift_sum.at[part(m)], total.at[part(m)], sems.at[1 + m, islands]).wait()
        average = total[part(m), :]
        if handed:
            average = average + extra[part(m), :].astype(F32)
        average = average * (1.0 / islands)
        for d in range(islands):
            pltpu.make_async_copy(
                own.at[d, part(m)], inputs.at[d, part(m)], sems.at[1 + m, d]
            ).wait()
            average = average + scales[d] * dot(inputs[d, part(m)], hiddens[d], ((1,), (0,)))
        total[part(m), :] = average
        square = square + jnp.sum(average * average, axis=0, keepdims=True)
        peak = jnp.maximum(peak, jnp.max(jnp.abs(average), axis=0, keepdims=True))
    unit = jnp.maximum(jnp.max(peak), 1e-30) / 32768
    scaled[...] = total[...] * (1 / unit)
    sublane = lax.broadcasted_iota(jnp.int32, notes.shape, 1)
    notes[...] = jnp.where(sublane == 0, jnp.sum(square), unit)


def hand_kernel(count, norms, *refs):
    passed, joined, sems = refs[-3:]
    pairs = [(refs[n], joined.at[n]) for n in range(count)] + [(norms, passed)]
    for copy in copy_all(sems, pairs):
        copy.wait()


def pass_kernel(count, notes, *refs):
    for copy in copy_all(refs[-1], [(refs[n], refs[count + n]) for n in range(count)]):
        copy.wait()


def update_kernel(entries, count, place, notes, momentum, *refs):
    pieces = refs[:count]
    new_momentum, outer_step, values, old, step, loads, stores = refs[-7:]
    rows, columns = pieces[0].shape
    spots = []
    for n in range(count):
        top = pl.multiple_of(place[3 * n] * rows, rows)
        left = pl.multiple_of(place[3 * n + 1] * columns, columns)
        spots.append((0, pl.ds(top, rows), pl.ds(left, columns)))
    pairs = []
    for n in range(count):
        pairs += [(pieces[n], values.at[n]), (momentum.at[spots[n]], old.at[n])]
    fetched = copy_all(loads, pairs)
    square = jnp.sum(notes[...], axis=0)[:1, :1]
    clip = jnp.minimum(1.0, 0.25 * math.sqrt(entries) / jnp.sqrt(square + 1e-06))
    stored = []
    for n in range(count):
        unit = notes[pl.ds(place[3 * n + 2], 1)][0, 1:2, :1]
        fetched[2 * n].wait()
        fetched[2 * n + 1].wait()
        clipped = (clip * unit) * values[n]
        moved = 0.9 * old[n] + clipped
        old[n] = moved
        step[n] = (0.7 * (clipped + 0.9 * moved)).astype(BF16)
        pairs = [(old.at[n], new_momentum.at[spots[n]]), (step.at[n], outer_step.at[spots[n]])]
        stored += copy_all(stores.at[n], pairs)
    for copy in stored:
        copy.wait()


def update_pieces(entries, places, notes, momentum, pieces, outs):
    count = len(pieces)
    shape = (count, *pieces[0].shape)
    return pl.pallas_call(
        lambda *refs: update_kernel(entries, count, *refs),
        in_specs=[SMEM, VMEM] + [ANY] * (1 + count + len(outs)),
        out_specs=[ANY, ANY],
        out_shape=[
            jax.ShapeDtypeStruct(momentum.shape, F32),
            jax.ShapeDtypeStruct(momentum.shape, BF16),
        ],
        scratch_shapes=[
            pltpu.VMEM(shape, F32),
            pltpu.VMEM(shape, F32),
            pltpu.VMEM(shape, BF16),
            pltpu.SemaphoreType.DMA((2 * count,)),
            pltpu.SemaphoreType.DMA((count, 2)),
        ],
        input_output_aliases={3 + count + n: n for n in range(len(outs))},
        compiler_params=params(48),
        name="update_pieces",
    )(jnp.concatenate(places), notes, momentum, *pieces, *outs)


def body(
    tokens,
    token_grads,
    slot_token,
    slot_count,
    slot_prob,
    gate_weight,
    down_weight,
    drift,
    momentum,
):
    islands, experts, parts = (lax.axis_size(a) for a in AXES)
    island, expert, part = (lax.axis_index(a) for a in AXES)
    devices = islands * experts * parts
    features, hidden = gate_weight.shape[2:]
    half = features // parts
    across = islands // parts
    columns = hidden // across
    entries = features * hidden * experts * parts
    slots = slot_token.shape[3]
    routed_rows = experts * slots
    holder = island // across
    spot = jnp.stack(
        [expert, part, island % across, island, jnp.int32(across), (part == holder).astype(jnp.int32)]
    ).astype(jnp.int32)

    handed = half // 2 if islands == 4 else 0
    steps = [0, 1, 2] if handed else list(range(islands))
    pieces = [(d, 0, half, n, 0) for n, d in enumerate(steps)]
    if handed:
        pieces += [(3, 0, handed, 1, half), (3, handed, handed, 2, half)]
    block_rows = [half + (handed if d else 0) for d in steps]
    picked = pl.pallas_call(
        lambda *refs: pick_kernel(experts, islands, pieces, *refs),
        in_specs=[SMEM] + [ANY] * 6,
        out_specs=[VMEM] * experts + [ANY] * len(steps),
        out_shape=[jax.ShapeDtypeStruct((2 * slots, half), BF16)] * experts
        + [jax.ShapeDtypeStruct((rows, columns), BF16) for rows in block_rows],
        scratch_shapes=[
            pltpu.VMEM(slot_token.shape, jnp.int32),
            pltpu.SMEM(slot_count.shape, jnp.int32),
            pltpu.VMEM(slot_prob.shape, F32),
            pltpu.VMEM(tokens.shape, BF16),
            pltpu.VMEM(token_grads.shape, BF16),
            pltpu.SemaphoreType.DMA((5 + len(pieces),)),
        ],
        compiler_params=params(56),
        name="pick_slots",
    )(spot, slot_token, slot_count, slot_prob, tokens, token_grads, drift)
    arrived = [picked[0]] + [swap(picked[d], "expert", d) for d in range(1, experts)]
    blocks = picked[experts:]
    drift_in = [blocks[0]] + [swap(blocks[d], "island", d) for d in steps[1:]]
    joined, turned, drift_sum, *relays = pl.pallas_call(
        lambda *refs: join_kernel(experts, len(steps), *refs),
        in_specs=[VMEM] * (experts + len(steps)),
        out_specs=[VMEM] * (5 if handed else 3),
        out_shape=[
            jax.ShapeDtypeStruct((2 * routed_rows, half), BF16),
            jax.ShapeDtypeStruct((half, routed_rows), BF16),
            jax.ShapeDtypeStruct((half, columns), F32),
        ]
        + [jax.ShapeDtypeStruct((handed, columns), BF16)] * (2 if handed else 0),
        compiler_params=params(12 + routed_rows // 48),
        name="join_slots",
    )(*arrived, *drift_in)
    relays = [swap(v, "island", 2 - n) for n, v in enumerate(relays)]

    joined_all = [joined] + [swap(joined, "tensor", t) for t in range(1, parts)]

    def send_features(d):
        pairs = []
        for at in range(islands):
            to = partner(at, d, islands)
            pairs.append((at * parts + to // across, to * parts + to // across))
        return lax.ppermute(turned, ("island", "tensor"), pairs)

    def spread(value):
        result = value
        for t in range(1, parts):
            pairs = []
            for at in range(islands):
                keep = at // across
                pairs.append((at * parts + keep, at * parts + partner(keep, t, parts)))
            moved = lax.ppermute(value, ("island", "tensor"), pairs)
            result = moved if t == 1 else result + moved
        return result

    features_in = [send_features(d) for d in range(1, islands)]

    hidden_piece = jax.ShapeDtypeStruct((routed_rows, columns), BF16)
    *hidden_out, norms = pl.pallas_call(
        lambda *refs: hidden_kernel(parts, across, *refs),
        in_specs=[SMEM] + [ANY] * (2 + parts),
        out_specs=[VMEM] * (across + 1),
        out_shape=[hidden_piece] * across + [jax.ShapeDtypeStruct((devices, 8, 128), F32)],
        scratch_shapes=[
            pltpu.VMEM((across, features, columns), BF16),
            pltpu.VMEM((across, columns, features), BF16),
            pltpu.VMEM((parts, 2 * routed_rows, half), BF16),
            pltpu.SemaphoreType.DMA((parts + 2 * across,)),
        ],
        compiler_params=params(16 + routed_rows // 48),
        name="hidden_grads",
    )(spot, gate_weight, down_weight, *joined_all)

    def hidden_for(d):
        at = partner(island, d, islands) % across
        if islands & (islands - 1) == 0:
            return hidden_out[d % across]
        return lax.select_n((at - island) % across, *hidden_out)

    hidden_of = [hidden_out[0]] + [
        swap(hidden_for(d), "island", d) for d in range(1, islands)
    ]
    norms, features_in = pl.pallas_call(
        lambda *refs: hand_kernel(islands, *refs),
        in_specs=[ANY] * (islands + 1 + len(relays)),
        out_specs=[ANY] * 2,
        out_shape=[
            jax.ShapeDtypeStruct(norms.shape, F32),
            jax.ShapeDtypeStruct((islands, half, routed_rows), BF16),
        ],
        scratch_shapes=[pltpu.SemaphoreType.DMA((islands + 1,))],
        compiler_params=params(2),
        name="hand_features",
    )(norms, turned, *features_in, *relays)
    features_moved = spread(features_in)
    norms = lax.all_to_all(norms, AXES, split_axis=0, concat_axis=0, tiled=True)

    scaled, notes = pl.pallas_call(
        lambda *refs: average_kernel(islands, entries, 4, len(relays), *refs),
        in_specs=[SMEM, VMEM] + [ANY] * (3 + islands + len(relays)),
        out_specs=[VMEM] * 2,
        out_shape=[
            jax.ShapeDtypeStruct((half, columns), F32),
            jax.ShapeDtypeStruct((devices, 8, 128), F32),
        ],
        scratch_shapes=[
            pltpu.VMEM((islands, half, routed_rows), BF16),
            pltpu.VMEM((islands, routed_rows, columns), BF16),
            pltpu.VMEM((half, columns), F32),
            pltpu.VMEM((half, columns), BF16),
            pltpu.SemaphoreType.DMA((5, islands + 2)),
        ],
        compiler_params=params(8 + routed_rows // 48),
        name="average_block",
    )(spot, norms, drift_sum, features_in, features_moved, *hidden_of, *relays)
    notes = lax.all_to_all(notes, AXES, split_axis=0, concat_axis=0, tiled=True)

    first, second = scaled[: half // 2], scaled[half // 2 :]
    sent = [first.astype(WIRE), second.astype(WIRE)]
    own = lax.reduce_precision(scaled, 5, 10)

    def places(at, pieces, n):
        source = (at * experts + expert) * parts + part
        top = (at // across) * pieces + n
        return jnp.stack([top, at % across, source]).astype(jnp.int32)

    def update(outs, pieces):
        spots = [places(origin(island, d, islands), *n) for d, n, _ in pieces]
        values = [v.astype(F32) for _, _, v in pieces]
        return update_pieces(entries, spots, notes, momentum, values, outs)

    outs = update([], [(0, (1, 0), own)])
    if islands == 4:
        later = pl.pallas_call(
            lambda *refs: pass_kernel(2, *refs),
            in_specs=[ANY] * 3,
            out_specs=[ANY] * 2,
            out_shape=[jax.ShapeDtypeStruct(first.shape, F32)] * 2,
            scratch_shapes=[pltpu.SemaphoreType.DMA((2,))],
            compiler_params=params(2),
            name="pass_halves",
        )(notes, first, second)
        later = [h.astype(WIRE) for h in later]
        beside = swap(sent[0], "island", 1)
        below = swap(sent[1], "island", 2)
        far = [swap(beside, "island", 2), swap(below, "island", 1)]
        crossed = [swap(later[0], "island", 2), swap(later[1], "island", 1)]
        outs = update(outs, [(1, (2, 0), beside), (2, (2, 1), below)])
        outs = update(outs, [(2, (2, 0), crossed[0]), (1, (2, 1), crossed[1])])
        outs = update(outs, [(3, (2, 0), far[0]), (3, (2, 1), far[1])])
    else:
        for d in range(1, islands):
            moved = [swap(h, "island", d) for h in sent]
            outs = update(outs, [(d, (2, n), h) for n, h in enumerate(moved)])
    return tuple(outs)


def solution(mesh):
    return jax.shard_map(
        body,
        mesh=mesh,
        in_specs=(
            P("island", "expert", "tensor"),
            P("island", "expert", "tensor"),
            P("island", "expert", None, None),
            P("island", "expert", None),
            P("island", "expert", None, None),
            P("island", "expert", None, "tensor"),
            P("island", "expert", "tensor", None),
            P("island", "expert", None, "tensor"),
            P("expert", None, "tensor"),
        ),
        out_specs=(P("expert", None, "tensor"), P("expert", None, "tensor")),
        check_vma=False,
    )
```

```python
import math

import jax
import jax.numpy as jnp
from jax import lax
from jax.experimental import pallas as pl
from jax.experimental.pallas import tpu as pltpu
from jax.sharding import PartitionSpec as P

F32 = jnp.float32
BF16 = jnp.bfloat16
WIRE = jnp.float16
AXES = ("island", "expert", "tensor")

VMEM = pl.BlockSpec(memory_space=pltpu.VMEM)
SMEM = pl.BlockSpec(memory_space=pltpu.SMEM)
ANY = pl.BlockSpec(memory_space=pl.ANY)


def params(mib):
    return pltpu.CompilerParams(vmem_limit_bytes=mib << 20)


def partner(at, step, size):
    return at ^ step if size & (size - 1) == 0 else (at + step) % size


def origin(at, step, size):
    return at ^ step if size & (size - 1) == 0 else (at - step) % size


def swap(value, axis, step):
    size = lax.axis_size(axis)
    return lax.ppermute(value, axis, [(at, partner(at, step, size)) for at in range(size)])


def dot(a, b, contract):
    return lax.dot_general(a, b, (contract, ((), ())), preferred_element_type=F32)


def copy_all(sems, pairs):
    copies = [pltpu.make_async_copy(*pair, sems.at[n]) for n, pair in enumerate(pairs)]
    for copy in copies:
        copy.start()
    return copies


def pick_kernel(experts, islands, pieces, spot, *refs):
    sources, drift = refs[:5], refs[5]
    outs, blocks = refs[6 : 6 + experts], refs[6 + experts : -6]
    table, count, weight, tokens, grads, sems = refs[-6:]
    loads = copy_all(sems, list(zip(sources, refs[-6:-1])))
    rows, columns = blocks[0].shape
    pairs = []
    for d, first, count_rows, target, at_row in pieces:
        at = partner(spot[3], d, islands)
        top = pl.multiple_of(lax.div(at, spot[4]) * rows, rows) + first
        left = pl.multiple_of(lax.rem(at, spot[4]) * columns, columns)
        pairs.append(
            (
                drift.at[0, 0, pl.ds(top, count_rows), pl.ds(left, columns)],
                blocks[target].at[pl.ds(at_row, count_rows)],
            )
        )
    copies = copy_all(sems.at[pl.ds(5, len(pairs))], pairs)
    for copy in loads:
        copy.wait()

    slots = table.shape[-1]
    rows = lax.broadcasted_iota(jnp.int32, (slots, slots), 0)
    lanes = lax.broadcasted_iota(jnp.int32, (slots, slots), 1)

    def column(row):
        return jnp.sum(jnp.where(rows == lanes, row, 0), axis=1, keepdims=True)

    for d in range(experts):
        to = partner(spot[0], d, experts)
        live = lax.broadcasted_iota(jnp.int32, (slots, 1), 0) < count[0, 0, to]
        token = column(table[0, 0, pl.ds(to, 1), :].astype(F32)).astype(jnp.int32)
        chance = column(weight[0, 0, pl.ds(to, 1), :])
        ids = lax.broadcasted_iota(jnp.int32, (slots, tokens.shape[1]), 1)
        picks = jnp.where((ids == token) & live, 1.0, 0.0).astype(BF16)
        outs[d][:slots, :] = dot(picks, tokens[0], ((1,), (0,))).astype(BF16)
        picked = dot(picks, grads[0], ((1,), (0,)))
        outs[d][slots:, :] = (chance * picked).astype(BF16)
    for copy in copies:
        copy.wait()


def join_kernel(count, blocks, *refs):
    arrived, drifts = refs[:count], refs[count : count + blocks]
    joined, turned, drift_sum = refs[count + blocks : count + blocks + 3]
    slots = arrived[0].shape[0] // 2
    rows = drift_sum.shape[0]
    for n, ref in enumerate(refs[count + blocks + 3 :]):
        ref[...] = drifts[1 + n][rows:, :]
    for n, piece in enumerate(arrived):
        joined[n * slots : (n + 1) * slots, :] = piece[:slots, :]
        joined[(count + n) * slots : (count + n + 1) * slots, :] = piece[slots:, :]
    turned[...] = joined[: count * slots, :].T
    added = drifts[0][...].astype(F32)
    for other in drifts[1:]:
        added = added + other[:rows, :].astype(F32)
    drift_sum[...] = added


def hidden_kernel(parts, across, spot, gate, down, *refs):
    joined, outs, norms = refs[:parts], refs[parts : parts + across], refs[-1]
    rows, half = joined[0].shape[0] // 2, joined[0].shape[1]
    columns = outs[0].shape[1]
    starts = [pl.multiple_of(origin(spot[1], t, parts) * half, half) for t in range(parts)]
    hidden_gram = 0.0
    for r in range(across):
        first = pl.multiple_of(partner(spot[2], r, across) * columns, columns)
        value = 0.0
        back = 0.0
        for t in range(parts):
            block = gate[0, 0, pl.ds(starts[t], half), pl.ds(first, columns)]
            value = value + dot(joined[t][:rows, :], block, ((1,), (0,)))
            block = down[0, 0, pl.ds(first, columns), pl.ds(starts[t], half)]
            back = back + dot(joined[t][rows:, :], block, ((1,), (1,)))
        rounded = (back * (value / (1.0 + jnp.exp(-value)))).astype(BF16)
        outs[r][...] = rounded
        hidden_gram = hidden_gram + dot(rounded, rounded, ((1,), (1,)))
    input_gram = 0.0
    for t in range(parts):
        features = joined[t][:rows, :]
        input_gram = input_gram + dot(features, features, ((1,), (1,)))
    norms[...] = jnp.full(norms.shape, jnp.sum(hidden_gram * input_gram), F32)


def average_kernel(islands, entries, tiles, spot, norms, drift_sum, own, moved, *refs):
    hiddens, handed = refs[:islands], refs[islands:-4]
    scaled, notes, total, square = refs[-4:]
    rows = total.shape[0] // tiles
    group = norms.shape[0] // islands
    scales = []
    for d in range(islands):
        at = origin(spot[3], d, islands)
        norm = jnp.sum(norms[pl.ds(at * group, group)], axis=0)[:1, :1]
        scales.append(jnp.minimum(1.0, math.sqrt(entries) / jnp.sqrt(norm + 1e-06)) / islands)

    def compute(features):
        squares = 0.0
        for m in range(tiles):
            part = slice(m * rows, (m + 1) * rows)
            average = drift_sum[part, :]
            if handed:
                size = handed[0].shape[0]
                n, first = divmod(m * rows, size)
                average = average + handed[n][first : first + rows, :].astype(F32)
            average = average * (1.0 / islands)
            for d in range(islands):
                average = average + scales[d] * dot(features[d, part, :], hiddens[d][...], ((1,), (0,)))
            total[part, :] = average
            squares = squares + jnp.sum(average * average, axis=0, keepdims=True)
        square[...] = squares

    pl.when(spot[5] == 1)(lambda: compute(own))
    pl.when(spot[5] != 1)(lambda: compute(moved))
    peak = jnp.max(jnp.abs(total[...]))
    unit = jnp.maximum(peak, 1e-30) / 32768
    scaled[...] = total[...] * (1 / unit)
    sublane = lax.broadcasted_iota(jnp.int32, notes.shape, 1)
    notes[...] = jnp.where(sublane == 0, jnp.sum(square[...]), unit)


def hand_kernel(count, norms, *refs):
    passed, joined = refs[-2:]
    for n in range(count):
        joined[n] = refs[n][...]
    passed[...] = norms[...]


def own_kernel(slots, block, slots_out, block_out):
    slots_out[...] = slots[...]
    block_out[...] = block[...]


def update_kernel(entries, pieces, place, notes, momentum, *refs):
    values = refs[: len(pieces)]
    new_momentum, outer_step, moved, step, sems = refs[-5:]
    square = jnp.sum(notes[...], axis=0)[:1, :1]
    clip = jnp.minimum(1.0, 0.25 * math.sqrt(entries) / jnp.sqrt(square + 1e-06))
    columns = values[0].shape[1]
    stored = []
    for n, (d, first) in enumerate(pieces):
        rows = values[n].shape[0]
        top = pl.multiple_of(place[3 * d], 32) + first
        left = pl.multiple_of(place[3 * d + 1], columns)
        unit = notes[pl.ds(place[3 * d + 2], 1)][0, 1:2, :1]
        for m in range(2):
            size = rows // 2
            here = pl.ds(m * size, size)
            there = (0, pl.ds(pl.multiple_of(top + m * size, 32), size), pl.ds(left, columns))
            clipped = (clip * unit) * values[n][here, :]
            fresh = 0.9 * momentum[there] + clipped
            moved[d, pl.ds(first + m * size, size), :] = fresh
            step[d, pl.ds(first + m * size, size), :] = (0.7 * (clipped + 0.9 * fresh)).astype(BF16)
            source = (d, pl.ds(first + m * size, size))
            for k, (here_ref, there_ref) in enumerate(((moved, new_momentum), (step, outer_step))):
                copy = pltpu.make_async_copy(here_ref.at[source], there_ref.at[there], sems.at[n, m, k])
                copy.start()
                stored.append(copy)
    for copy in stored:
        copy.wait()


def body(
    tokens,
    token_grads,
    slot_token,
    slot_count,
    slot_prob,
    gate_weight,
    down_weight,
    drift,
    momentum,
):
    islands, experts, parts = (lax.axis_size(a) for a in AXES)
    island, expert, part = (lax.axis_index(a) for a in AXES)
    devices = islands * experts * parts
    features, hidden = gate_weight.shape[2:]
    half = features // parts
    across = islands // parts
    columns = hidden // across
    entries = features * hidden * experts * parts
    slots = slot_token.shape[3]
    routed_rows = experts * slots
    holder = island // across
    spot = jnp.stack(
        [expert, part, island % across, island, jnp.int32(across), (part == holder).astype(jnp.int32)]
    ).astype(jnp.int32)

    handed = half // 2 if islands == 4 else 0
    steps = [0, 1, 2] if handed else list(range(islands))
    pieces = [(d, 0, half, n, 0) for n, d in enumerate(steps)]
    if handed:
        pieces += [(3, 0, handed, 1, half), (3, handed, handed, 2, half)]
    block_rows = [half + (handed if d else 0) for d in steps]
    picked = pl.pallas_call(
        lambda *refs: pick_kernel(experts, islands, pieces, *refs),
        in_specs=[SMEM] + [ANY] * 6,
        out_specs=[VMEM] * (experts + len(steps)),
        out_shape=[jax.ShapeDtypeStruct((2 * slots, half), BF16)] * experts
        + [jax.ShapeDtypeStruct((rows, columns), BF16) for rows in block_rows],
        scratch_shapes=[
            pltpu.VMEM(slot_token.shape, jnp.int32),
            pltpu.SMEM(slot_count.shape, jnp.int32),
            pltpu.VMEM(slot_prob.shape, F32),
            pltpu.VMEM(tokens.shape, BF16),
            pltpu.VMEM(token_grads.shape, BF16),
            pltpu.SemaphoreType.DMA((5 + len(pieces),)),
        ],
        compiler_params=params(56),
        name="pick_slots",
    )(spot, slot_token, slot_count, slot_prob, tokens, token_grads, drift)
    arrived = [picked[0]] + [swap(picked[d], "expert", d) for d in range(1, experts)]
    blocks = list(picked[experts:])
    arrived[0], blocks[0] = pl.pallas_call(
        own_kernel,
        in_specs=[VMEM] * 2,
        out_specs=[VMEM] * 2,
        out_shape=[
            jax.ShapeDtypeStruct((2 * slots, half), BF16),
            jax.ShapeDtypeStruct((half, columns), BF16),
        ],
        compiler_params=params(6),
        name="own_parts",
    )(arrived[0], blocks[0])
    drift_in = [blocks[0]] + [swap(blocks[d], "island", d) for d in steps[1:]]
    joined, turned, drift_sum, *relays = pl.pallas_call(
        lambda *refs: join_kernel(experts, len(steps), *refs),
        in_specs=[VMEM] * (experts + len(steps)),
        out_specs=[VMEM] * (5 if handed else 3),
        out_shape=[
            jax.ShapeDtypeStruct((2 * routed_rows, half), BF16),
            jax.ShapeDtypeStruct((half, routed_rows), BF16),
            jax.ShapeDtypeStruct((half, columns), F32),
        ]
        + [jax.ShapeDtypeStruct((handed, columns), BF16)] * (2 if handed else 0),
        compiler_params=params(12 + routed_rows // 48),
        name="join_slots",
    )(*arrived, *drift_in)
    relays = [swap(v, "island", 2 - n) for n, v in enumerate(relays)]

    joined_all = [joined] + [swap(joined, "tensor", t) for t in range(1, parts)]

    def send_features(d):
        pairs = []
        for at in range(islands):
            to = partner(at, d, islands)
            pairs.append((at * parts + to // across, to * parts + to // across))
        return lax.ppermute(turned, ("island", "tensor"), pairs)

    def spread(value):
        result = value
        for t in range(1, parts):
            pairs = []
            for at in range(islands):
                keep = at // across
                pairs.append((at * parts + keep, at * parts + partner(keep, t, parts)))
            moved = lax.ppermute(value, ("island", "tensor"), pairs)
            result = moved if t == 1 else result + moved
        return result

    features_in = [send_features(d) for d in range(1, islands)]

    hidden_piece = jax.ShapeDtypeStruct((routed_rows, columns), BF16)
    *hidden_out, norms = pl.pallas_call(
        lambda *refs: hidden_kernel(parts, across, *refs),
        in_specs=[SMEM] + [VMEM] * (2 + parts),
        out_specs=[VMEM] * (across + 1),
        out_shape=[hidden_piece] * across + [jax.ShapeDtypeStruct((devices, 8, 128), F32)],
        compiler_params=params(16 + routed_rows // 48),
        name="hidden_grads",
    )(spot, gate_weight, down_weight, *joined_all)

    def hidden_for(d):
        at = partner(island, d, islands) % across
        if islands & (islands - 1) == 0:
            return hidden_out[d % across]
        return lax.select_n((at - island) % across, *hidden_out)

    hidden_of = [hidden_out[0]] + [
        swap(hidden_for(d), "island", d) for d in range(1, islands)
    ]
    norms, features_in = pl.pallas_call(
        lambda *refs: hand_kernel(islands, *refs),
        in_specs=[VMEM] * (islands + 1) + [ANY] * len(relays),
        out_specs=[VMEM] * 2,
        out_shape=[
            jax.ShapeDtypeStruct(norms.shape, F32),
            jax.ShapeDtypeStruct((islands, half, routed_rows), BF16),
        ],
        compiler_params=params(4 + routed_rows // 48),
        name="hand_features",
    )(norms, turned, *features_in, *relays)
    features_moved = spread(features_in)
    norms = lax.all_to_all(norms, AXES, split_axis=0, concat_axis=0, tiled=True)

    scaled, notes = pl.pallas_call(
        lambda *refs: average_kernel(islands, entries, 4, *refs),
        in_specs=[SMEM] + [VMEM] * (4 + islands + len(relays)),
        out_specs=[VMEM] * 2,
        out_shape=[
            jax.ShapeDtypeStruct((half, columns), F32),
            jax.ShapeDtypeStruct((devices, 8, 128), F32),
        ],
        scratch_shapes=[pltpu.VMEM((half, columns), F32), pltpu.VMEM((1, columns), F32)],
        compiler_params=params(8 + routed_rows // 48),
        name="average_block",
    )(spot, norms, drift_sum, features_in, features_moved, *hidden_of, *relays)
    notes = lax.all_to_all(notes, AXES, split_axis=0, concat_axis=0, tiled=True)

    parted = half // 2 if islands == 4 else half
    sent = [scaled[first : first + parted].astype(WIRE) for first in range(0, half, parted)]
    values = {(0, 0): lax.reduce_precision(scaled, 5, 10)}
    if islands == 4:
        beside, below = swap(sent[0], "island", 1), swap(sent[1], "island", 2)
        values[1, 0], values[2, parted] = beside, below
        values[2, 0], values[1, parted] = swap(sent[0], "island", 2), swap(sent[1], "island", 1)
        values[3, 0], values[3, parted] = swap(beside, "island", 2), swap(below, "island", 1)
    else:
        for d in range(1, islands):
            values[d, 0] = swap(sent[0], "island", d)
    place = []
    for d in range(islands):
        at = origin(island, d, islands)
        source = (at * experts + expert) * parts + part
        place += [(at // across) * half, (at % across) * columns, source]
    block = (islands, half, columns)
    return tuple(
        pl.pallas_call(
            lambda *refs: update_kernel(entries, list(values), *refs),
            in_specs=[SMEM] + [VMEM] * (2 + len(values)),
            out_specs=[ANY, ANY],
            out_shape=[
                jax.ShapeDtypeStruct(momentum.shape, F32),
                jax.ShapeDtypeStruct(momentum.shape, BF16),
            ],
            scratch_shapes=[
                pltpu.VMEM(block, F32),
                pltpu.VMEM(block, BF16),
                pltpu.SemaphoreType.DMA((len(values), 2, 2)),
            ],
            compiler_params=params(14),
            name="update_outputs",
        )(
            jnp.stack(place).astype(jnp.int32),
            notes,
            momentum,
            *[v.astype(F32) for v in values.values()],
        )
    )


def solution(mesh):
    return jax.shard_map(
        body,
        mesh=mesh,
        in_specs=(
            P("island", "expert", "tensor"),
            P("island", "expert", "tensor"),
            P("island", "expert", None, None),
            P("island", "expert", None),
            P("island", "expert", None, None),
            P("island", "expert", None, "tensor"),
            P("island", "expert", "tensor", None),
            P("island", "expert", None, "tensor"),
            P("expert", None, "tensor"),
        ),
        out_specs=(P("expert", None, "tensor"), P("expert", None, "tensor")),
        check_vma=False,
    )
```

```python
import math

import jax
import jax.numpy as jnp
from jax import lax
from jax.experimental import pallas as pl
from jax.experimental.pallas import tpu as pltpu
from jax.sharding import PartitionSpec as P

F32 = jnp.float32
BF16 = jnp.bfloat16
WIRE = jnp.float16
AXES = ("island", "expert", "tensor")

VMEM = pl.BlockSpec(memory_space=pltpu.VMEM)
SMEM = pl.BlockSpec(memory_space=pltpu.SMEM)
ANY = pl.BlockSpec(memory_space=pl.ANY)


def params(mib):
    return pltpu.CompilerParams(vmem_limit_bytes=mib << 20)


def partner(at, step, size):
    return at ^ step if size & (size - 1) == 0 else (at + step) % size


def origin(at, step, size):
    return at ^ step if size & (size - 1) == 0 else (at - step) % size


def swap(value, axis, step):
    size = lax.axis_size(axis)
    return lax.ppermute(value, axis, [(at, partner(at, step, size)) for at in range(size)])


def dot(a, b, contract):
    return lax.dot_general(a, b, (contract, ((), ())), preferred_element_type=F32)


def copy_all(sems, pairs):
    copies = [pltpu.make_async_copy(*pair, sems.at[n]) for n, pair in enumerate(pairs)]
    for copy in copies:
        copy.start()
    return copies


def pick_kernel(experts, islands, pieces, spot, *refs):
    sources, drift = refs[:5], refs[5]
    outs, blocks = refs[6 : 6 + experts], refs[6 + experts : -10]
    table, count, weight, tokens, grads, picked, cut, sems, in_sems, out_sems = refs[-10:]
    loads = copy_all(sems, list(zip(sources, refs[-10:-5])))
    rows, columns = blocks[0].shape
    pairs, stores = [], []
    for d, first, count_rows, target, at_row in pieces:
        at = partner(spot[3], d, islands)
        top = pl.multiple_of(lax.div(at, spot[4]) * rows, rows) + first
        left = pl.multiple_of(lax.rem(at, spot[4]) * columns, columns)
        place = pl.ds(sum(p[2] for p in pieces[: len(pairs)]), count_rows)
        pairs.append((drift.at[0, 0, pl.ds(top, count_rows), pl.ds(left, columns)], cut.at[place]))
        stores.append((cut.at[place], blocks[target].at[pl.ds(at_row, count_rows)]))
    copies = copy_all(in_sems, pairs)
    for copy in loads:
        copy.wait()

    slots = table.shape[-1]
    rows = lax.broadcasted_iota(jnp.int32, (slots, slots), 0)
    lanes = lax.broadcasted_iota(jnp.int32, (slots, slots), 1)

    def column(row):
        return jnp.sum(jnp.where(rows == lanes, row, 0), axis=1, keepdims=True)

    done = []
    for d in [*range(1, experts), 0]:
        to = partner(spot[0], d, experts)
        live = lax.broadcasted_iota(jnp.int32, (slots, 1), 0) < count[0, 0, to]
        token = column(table[0, 0, pl.ds(to, 1), :].astype(F32)).astype(jnp.int32)
        chance = column(weight[0, 0, pl.ds(to, 1), :])
        ids = lax.broadcasted_iota(jnp.int32, (slots, tokens.shape[1]), 1)
        picks = jnp.where((ids == token) & live, 1.0, 0.0).astype(BF16)
        picked[d, :slots, :] = dot(picks, tokens[0], ((1,), (0,))).astype(BF16)
        chosen = dot(picks, grads[0], ((1,), (0,)))
        picked[d, slots:, :] = (chance * chosen).astype(BF16)
        done.append(pltpu.make_async_copy(picked.at[d], outs[d], out_sems.at[len(pairs) + d]))
        done[-1].start()
    for n, copy in enumerate(copies):
        copy.wait()
        done.append(pltpu.make_async_copy(*stores[n], out_sems.at[n]))
        done[-1].start()
    for copy in done:
        copy.wait()


def join_kernel(count, blocks, *refs):
    arrived, drifts = refs[:count], refs[count : count + blocks]
    joined, turned, drift_sum = refs[count + blocks : count + blocks + 3]
    slots = arrived[0].shape[0] // 2
    rows = drift_sum.shape[0]
    for n, ref in enumerate(refs[count + blocks + 3 :]):
        ref[...] = drifts[1 + n][rows:, :]
    for n, piece in enumerate(arrived):
        joined[n * slots : (n + 1) * slots, :] = piece[:slots, :]
        joined[(count + n) * slots : (count + n + 1) * slots, :] = piece[slots:, :]
    turned[...] = joined[: count * slots, :].T
    added = drifts[0][...].astype(F32)
    for other in drifts[1:]:
        added = added + other[:rows, :].astype(F32)
    drift_sum[...] = added


def hidden_kernel(parts, across, spot, gate, down, *refs):
    joined, outs, norms = refs[:parts], refs[parts : parts + across], refs[-1]
    rows, half = joined[0].shape[0] // 2, joined[0].shape[1]
    columns = outs[0].shape[1]
    starts = [pl.multiple_of(origin(spot[1], t, parts) * half, half) for t in range(parts)]
    hidden_gram = 0.0
    for r in range(across):
        first = pl.multiple_of(partner(spot[2], r, across) * columns, columns)
        value = 0.0
        back = 0.0
        for t in range(parts):
            block = gate[0, 0, pl.ds(starts[t], half), pl.ds(first, columns)]
            value = value + dot(joined[t][:rows, :], block, ((1,), (0,)))
            block = down[0, 0, pl.ds(first, columns), pl.ds(starts[t], half)]
            back = back + dot(joined[t][rows:, :], block, ((1,), (1,)))
        rounded = (back * (value / (1.0 + jnp.exp(-value)))).astype(BF16)
        outs[r][...] = rounded
        hidden_gram = hidden_gram + dot(rounded, rounded, ((1,), (1,)))
    input_gram = 0.0
    for t in range(parts):
        features = joined[t][:rows, :]
        input_gram = input_gram + dot(features, features, ((1,), (1,)))
    norms[...] = jnp.full(norms.shape, jnp.sum(hidden_gram * input_gram), F32)


def average_kernel(islands, entries, tiles, spot, norms, drift_sum, own, moved, *refs):
    hiddens, handed = refs[:islands], refs[islands:-5]
    *halves, notes, total, square = refs[-5:]
    rows = total.shape[0] // tiles
    group = norms.shape[0] // islands
    scales = []
    for d in range(islands):
        at = origin(spot[3], d, islands)
        norm = jnp.sum(norms[pl.ds(at * group, group)], axis=0)[:1, :1]
        scales.append(jnp.minimum(1.0, math.sqrt(entries) / jnp.sqrt(norm + 1e-06)) / islands)

    def compute(features):
        squares = 0.0
        for m in range(tiles):
            part = slice(m * rows, (m + 1) * rows)
            average = drift_sum[part, :]
            if handed:
                size = handed[0].shape[0]
                n, first = divmod(m * rows, size)
                average = average + handed[n][first : first + rows, :].astype(F32)
            average = average * (1.0 / islands)
            for d in range(islands):
                average = average + scales[d] * dot(features[d, part, :], hiddens[d][...], ((1,), (0,)))
            total[part, :] = average
            squares = squares + jnp.sum(average * average, axis=0, keepdims=True)
        square[...] = squares

    pl.when(spot[5] == 1)(lambda: compute(own))
    pl.when(spot[5] != 1)(lambda: compute(moved))
    peak = jnp.max(jnp.abs(total[...]))
    unit = jnp.maximum(peak, 1e-30) / 32768
    for n, half in enumerate(halves):
        size = half.shape[0]
        value = total[n * size : (n + 1) * size, :] * (1 / unit)
        spread_out = value * 8193.0
        value = spread_out - (spread_out - value)
        half[...] = jnp.where(jnp.abs(value) < 2.0**-13, 0.0, value)
    sublane = lax.broadcasted_iota(jnp.int32, notes.shape, 1)
    notes[...] = jnp.where(sublane == 0, jnp.sum(square[...]), unit)


def hand_kernel(count, *refs):
    for n in range(count):
        refs[-1][n] = refs[n][...]


def own_kernel(slots, block, slots_out, block_out):
    slots_out[...] = slots[...]
    block_out[...] = block[...]


def update_kernel(entries, pieces, place, notes, momentum, *refs):
    values = refs[: len(pieces)]
    new_momentum, outer_step, moved, step, in_sems, out_sems = refs[-6:]
    rows, columns = values[0].shape
    spots, loads = [], []
    for n, (d, first) in enumerate(pieces):
        top = pl.multiple_of(pl.multiple_of(place[3 * d], 32) + first, 32)
        left = pl.multiple_of(place[3 * d + 1], columns)
        spots.append((0, pl.ds(top, rows), pl.ds(left, columns)))
        loads.append(pltpu.make_async_copy(momentum.at[spots[n]], moved.at[n], in_sems.at[n]))
        loads[-1].start()
    square = jnp.sum(notes[...], axis=0)[:1, :1]
    clip = jnp.minimum(1.0, 0.25 * math.sqrt(entries) / jnp.sqrt(square + 1e-06))
    stored = []
    for n, (d, _) in enumerate(pieces):
        unit = notes[pl.ds(place[3 * d + 2], 1)][0, 1:2, :1]
        loads[n].wait()
        clipped = (clip * unit) * values[n][...]
        fresh = 0.9 * moved[n] + clipped
        moved[n] = fresh
        step[n] = (0.7 * (clipped + 0.9 * fresh)).astype(BF16)
        for k, (here, there) in enumerate(((moved, new_momentum), (step, outer_step))):
            stored.append(pltpu.make_async_copy(here.at[n], there.at[spots[n]], out_sems.at[n, k]))
            stored[-1].start()
    for copy in stored:
        copy.wait()


def update_pieces(entries, place, notes, momentum, values, outs, cost):
    pieces, arrays = list(values), [v.astype(F32) for v in values.values()]
    shape = (len(pieces), *arrays[0].shape)
    return pl.pallas_call(
        lambda *refs: update_kernel(entries, pieces, *refs),
        in_specs=[SMEM, VMEM, ANY] + [VMEM] * len(pieces) + [ANY] * len(outs),
        out_specs=[ANY, ANY],
        out_shape=[
            jax.ShapeDtypeStruct(momentum.shape, F32),
            jax.ShapeDtypeStruct(momentum.shape, BF16),
        ],
        scratch_shapes=[
            pltpu.VMEM(shape, F32),
            pltpu.VMEM(shape, BF16),
            pltpu.SemaphoreType.DMA((len(pieces),)),
            pltpu.SemaphoreType.DMA((len(pieces), 2)),
        ],
        input_output_aliases={3 + len(pieces) + n: n for n in range(len(outs))},
        cost_estimate=pl.CostEstimate(flops=0, bytes_accessed=cost, transcendentals=0),
        compiler_params=params(50),
        name="update_pieces",
    )(place, notes, momentum, *arrays, *outs)


def body(
    tokens,
    token_grads,
    slot_token,
    slot_count,
    slot_prob,
    gate_weight,
    down_weight,
    drift,
    momentum,
):
    islands, experts, parts = (lax.axis_size(a) for a in AXES)
    island, expert, part = (lax.axis_index(a) for a in AXES)
    devices = islands * experts * parts
    features, hidden = gate_weight.shape[2:]
    half = features // parts
    across = islands // parts
    columns = hidden // across
    entries = features * hidden * experts * parts
    slots = slot_token.shape[3]
    routed_rows = experts * slots
    holder = island // across
    spot = jnp.stack(
        [expert, part, island % across, island, jnp.int32(across), (part == holder).astype(jnp.int32)]
    ).astype(jnp.int32)

    handed = half // 2 if islands == 4 else 0
    steps = [0, 1, 2] if handed else list(range(islands))
    pieces = [(d, 0, half, n, 0) for n, d in enumerate(steps)]
    if handed:
        pieces += [(3, 0, handed, 1, half), (3, handed, handed, 2, half)]
    block_rows = [half + (handed if d else 0) for d in steps]
    picked = pl.pallas_call(
        lambda *refs: pick_kernel(experts, islands, pieces, *refs),
        in_specs=[SMEM] + [ANY] * 6,
        out_specs=[ANY] * (experts + len(steps)),
        out_shape=[jax.ShapeDtypeStruct((2 * slots, half), BF16)] * experts
        + [jax.ShapeDtypeStruct((rows, columns), BF16) for rows in block_rows],
        scratch_shapes=[
            pltpu.VMEM(slot_token.shape, jnp.int32),
            pltpu.SMEM(slot_count.shape, jnp.int32),
            pltpu.VMEM(slot_prob.shape, F32),
            pltpu.VMEM(tokens.shape, BF16),
            pltpu.VMEM(token_grads.shape, BF16),
            pltpu.VMEM((experts, 2 * slots, half), BF16),
            pltpu.VMEM((sum(p[2] for p in pieces), columns), BF16),
            pltpu.SemaphoreType.DMA((5,)),
            pltpu.SemaphoreType.DMA((len(pieces),)),
            pltpu.SemaphoreType.DMA((len(pieces) + experts,)),
        ],
        compiler_params=params(56),
        name="pick_slots",
    )(spot, slot_token, slot_count, slot_prob, tokens, token_grads, drift)
    arrived = [picked[0]] + [swap(picked[d], "expert", d) for d in range(1, experts)]
    blocks = list(picked[experts:])
    arrived[0], blocks[0] = pl.pallas_call(
        own_kernel,
        in_specs=[VMEM] * 2,
        out_specs=[VMEM] * 2,
        out_shape=[
            jax.ShapeDtypeStruct((2 * slots, half), BF16),
            jax.ShapeDtypeStruct((half, columns), BF16),
        ],
        compiler_params=params(6),
        name="own_parts",
    )(arrived[0], blocks[0])
    drift_in = [blocks[0]] + [swap(blocks[d], "island", d) for d in steps[1:]]
    joined, turned, drift_sum, *relays = pl.pallas_call(
        lambda *refs: join_kernel(experts, len(steps), *refs),
        in_specs=[VMEM] * (experts + len(steps)),
        out_specs=[VMEM] * (5 if handed else 3),
        out_shape=[
            jax.ShapeDtypeStruct((2 * routed_rows, half), BF16),
            jax.ShapeDtypeStruct((half, routed_rows), BF16),
            jax.ShapeDtypeStruct((half, columns), F32),
        ]
        + [jax.ShapeDtypeStruct((handed, columns), BF16)] * (2 if handed else 0),
        compiler_params=params(12 + routed_rows // 48),
        name="join_slots",
    )(*arrived, *drift_in)
    relays = [swap(v, "island", 2 - n) for n, v in enumerate(relays)]

    joined_all = [joined] + [swap(joined, "tensor", t) for t in range(1, parts)]

    def send_features(d):
        pairs = []
        for at in range(islands):
            to = partner(at, d, islands)
            pairs.append((at * parts + to // across, to * parts + to // across))
        return lax.ppermute(turned, ("island", "tensor"), pairs)

    def spread(value):
        result = value
        for t in range(1, parts):
            pairs = []
            for at in range(islands):
                keep = at // across
                pairs.append((at * parts + keep, at * parts + partner(keep, t, parts)))
            moved = lax.ppermute(value, ("island", "tensor"), pairs)
            result = moved if t == 1 else result + moved
        return result

    features_in = [send_features(d) for d in range(1, islands)]

    hidden_piece = jax.ShapeDtypeStruct((routed_rows, columns), BF16)
    *hidden_out, norms = pl.pallas_call(
        lambda *refs: hidden_kernel(parts, across, *refs),
        in_specs=[SMEM] + [VMEM] * (2 + parts),
        out_specs=[VMEM] * (across + 1),
        out_shape=[hidden_piece] * across + [jax.ShapeDtypeStruct((devices, 8, 128), F32)],
        compiler_params=params(16 + routed_rows // 48),
        name="hidden_grads",
    )(spot, gate_weight, down_weight, *joined_all)

    def hidden_for(d):
        at = partner(island, d, islands) % across
        if islands & (islands - 1) == 0:
            return hidden_out[d % across]
        return lax.select_n((at - island) % across, *hidden_out)

    hidden_of = [hidden_out[0]] + [
        swap(hidden_for(d), "island", d) for d in range(1, islands)
    ]
    norms = lax.all_to_all(norms, AXES, split_axis=0, concat_axis=0, tiled=True)
    features_in = pl.pallas_call(
        lambda *refs: hand_kernel(islands, *refs),
        in_specs=[VMEM] * islands + [ANY] * (1 + len(relays)),
        out_specs=VMEM,
        out_shape=jax.ShapeDtypeStruct((islands, half, routed_rows), BF16),
        compiler_params=params(4 + routed_rows // 48),
        name="hand_features",
    )(turned, *features_in, norms, *relays)
    features_moved = spread(features_in)

    *halves, notes = pl.pallas_call(
        lambda *refs: average_kernel(islands, entries, 4, *refs),
        in_specs=[SMEM] + [VMEM] * (4 + islands + len(relays)),
        out_specs=[VMEM] * 3,
        out_shape=[jax.ShapeDtypeStruct((half // 2, columns), F32)] * 2
        + [jax.ShapeDtypeStruct((devices, 8, 128), F32)],
        scratch_shapes=[pltpu.VMEM((half, columns), F32), pltpu.VMEM((1, columns), F32)],
        compiler_params=params(8 + routed_rows // 48),
        name="average_block",
    )(spot, norms, drift_sum, features_in, features_moved, *hidden_of, *relays)
    notes = lax.all_to_all(notes, AXES, split_axis=0, concat_axis=0, tiled=True)

    parted = half // 2
    sent = [v.astype(WIRE) for v in halves]
    values = {(0, 0): halves[0], (0, parted): halves[1]}
    last = {}
    if islands == 4:
        nothing = jnp.minimum(notes[0, 1:2, :1], 0.0).astype(WIRE)

        def after_notes(value):
            return lax.dynamic_update_slice(value, value[:1, :128] + nothing, (0, 0))

        values[2, 0], values[1, parted] = swap(sent[0], "island", 2), swap(sent[1], "island", 1)
        beside, below = swap(sent[0], "island", 1), swap(sent[1], "island", 2)
        beside, below = after_notes(beside), after_notes(below)
        values[1, 0], values[2, parted] = beside, below
        last[3, 0], last[3, parted] = swap(beside, "island", 2), swap(below, "island", 1)
    else:
        for d in range(1, islands):
            for n in range(2):
                last[d, n * parted] = swap(sent[n], "island", d)
    place = []
    for d in range(islands):
        at = origin(island, d, islands)
        source = (at * experts + expert) * parts + part
        place += [(at // across) * half, (at % across) * columns, source]
    place = jnp.stack(place).astype(jnp.int32)
    outs = update_pieces(entries, place, notes, momentum, values, [], 12 * momentum.size)
    outs = update_pieces(entries, place, notes, momentum, last, outs, 3 * momentum.size)
    return tuple(outs)


def solution(mesh):
    return jax.shard_map(
        body,
        mesh=mesh,
        in_specs=(
            P("island", "expert", "tensor"),
            P("island", "expert", "tensor"),
            P("island", "expert", None, None),
            P("island", "expert", None),
            P("island", "expert", None, None),
            P("island", "expert", None, "tensor"),
            P("island", "expert", "tensor", None),
            P("island", "expert", None, "tensor"),
            P("expert", None, "tensor"),
        ),
        out_specs=(P("expert", None, "tensor"), P("expert", None, "tensor")),
        check_vma=False,
    )
```

```python
import math

import jax
import jax.numpy as jnp
from jax import lax
from jax.experimental import pallas as pl
from jax.experimental.pallas import tpu as pltpu
from jax.sharding import PartitionSpec as P

F32 = jnp.float32
BF16 = jnp.bfloat16
WIRE = jnp.float16
AXES = ("island", "expert", "tensor")
NOTE_ROWS = 16

VMEM = pl.BlockSpec(memory_space=pltpu.VMEM)
SMEM = pl.BlockSpec(memory_space=pltpu.SMEM)
ANY = pl.BlockSpec(memory_space=pl.ANY)


def params(mib):
    return pltpu.CompilerParams(vmem_limit_bytes=mib << 20)


def partner(at, step, size):
    return at ^ step if size & (size - 1) == 0 else (at + step) % size


def origin(at, step, size):
    return at ^ step if size & (size - 1) == 0 else (at - step) % size


def swap(value, axis, step):
    size = lax.axis_size(axis)
    return lax.ppermute(value, axis, [(at, partner(at, step, size)) for at in range(size)])


def dot(a, b, contract):
    return lax.dot_general(a, b, (contract, ((), ())), preferred_element_type=F32)


def copy_all(sems, pairs):
    copies = [pltpu.make_async_copy(*pair, sems.at[n]) for n, pair in enumerate(pairs)]
    for copy in copies:
        copy.start()
    return copies


def pick_kernel(experts, islands, pieces, spot, *refs):
    sources, drift = refs[:5], refs[5]
    outs, blocks = refs[6 : 6 + experts], refs[6 + experts : -10]
    table, count, weight, tokens, grads, picked, cut, sems, in_sems, out_sems = refs[-10:]
    loads = copy_all(sems, list(zip(sources, refs[-10:-5])))
    rows, columns = blocks[0].shape
    pairs, stores = [], []
    for d, first, count_rows, target, at_row in pieces:
        at = partner(spot[3], d, islands)
        top = pl.multiple_of(lax.div(at, spot[4]) * rows, rows) + first
        left = pl.multiple_of(lax.rem(at, spot[4]) * columns, columns)
        place = pl.ds(sum(p[2] for p in pieces[: len(pairs)]), count_rows)
        pairs.append((drift.at[0, 0, pl.ds(top, count_rows), pl.ds(left, columns)], cut.at[place]))
        stores.append((cut.at[place], blocks[target].at[pl.ds(at_row, count_rows)]))
    copies = copy_all(in_sems, pairs)
    for copy in loads:
        copy.wait()

    slots = table.shape[-1]
    rows = lax.broadcasted_iota(jnp.int32, (slots, slots), 0)
    lanes = lax.broadcasted_iota(jnp.int32, (slots, slots), 1)

    def column(row):
        return jnp.sum(jnp.where(rows == lanes, row, 0), axis=1, keepdims=True)

    done = []
    for d in [*range(1, experts), 0]:
        to = partner(spot[0], d, experts)
        live = lax.broadcasted_iota(jnp.int32, (slots, 1), 0) < count[0, 0, to]
        token = column(table[0, 0, pl.ds(to, 1), :].astype(F32)).astype(jnp.int32)
        chance = column(weight[0, 0, pl.ds(to, 1), :])
        ids = lax.broadcasted_iota(jnp.int32, (slots, tokens.shape[1]), 1)
        picks = jnp.where((ids == token) & live, 1.0, 0.0).astype(BF16)
        picked[d, :slots, :] = dot(picks, tokens[0], ((1,), (0,))).astype(BF16)
        chosen = dot(picks, grads[0], ((1,), (0,)))
        picked[d, slots:, :] = (chance * chosen).astype(BF16)
        done.append(pltpu.make_async_copy(picked.at[d], outs[d], out_sems.at[len(pairs) + d]))
        done[-1].start()
    for n, copy in enumerate(copies):
        copy.wait()
        done.append(pltpu.make_async_copy(*stores[n], out_sems.at[n]))
        done[-1].start()
    for copy in done:
        copy.wait()


def join_kernel(count, blocks, *refs):
    arrived, drifts = refs[:count], refs[count : count + blocks]
    joined, turned, drift_sum = refs[count + blocks : count + blocks + 3]
    slots = arrived[0].shape[0] // 2
    rows = drift_sum.shape[0]
    for n, ref in enumerate(refs[count + blocks + 3 :]):
        ref[...] = drifts[1 + n][rows:, :]
    for n, piece in enumerate(arrived):
        joined[n * slots : (n + 1) * slots, :] = piece[:slots, :]
        joined[(count + n) * slots : (count + n + 1) * slots, :] = piece[slots:, :]
    turned[...] = joined[: count * slots, :].T
    added = drifts[0][...].astype(F32)
    for other in drifts[1:]:
        added = added + other[:rows, :].astype(F32)
    drift_sum[...] = added


def hidden_kernel(parts, across, spot, gate, down, *refs):
    joined, out, norms = refs[:parts], refs[parts], refs[-1]
    rows, half = joined[0].shape[0] // 2, joined[0].shape[1]
    columns = out.shape[2]
    starts = [pl.multiple_of(origin(spot[1], t, parts) * half, half) for t in range(parts)]
    hidden_gram = 0.0
    for r in range(across):
        first = r * columns
        value = 0.0
        back = 0.0
        for t in range(parts):
            block = gate[0, 0, pl.ds(starts[t], half), first : first + columns]
            value = value + dot(joined[t][:rows, :], block, ((1,), (0,)))
            block = down[0, 0, first : first + columns, pl.ds(starts[t], half)]
            back = back + dot(joined[t][rows:, :], block, ((1,), (1,)))
        rounded = (back * (value / (1.0 + jnp.exp(-value)))).astype(BF16)
        out[r] = rounded
        hidden_gram = hidden_gram + dot(rounded, rounded, ((1,), (1,)))
    input_gram = 0.0
    for t in range(parts):
        features = joined[t][:rows, :]
        input_gram = input_gram + dot(features, features, ((1,), (1,)))
    norms[...] = jnp.full(norms.shape, jnp.sum(hidden_gram * input_gram), F32)


def average_kernel(islands, entries, tiles, spot, drift_sum, own, moved, *refs):
    messages = refs[:islands]
    *halves, notes, total, square = refs[islands:]
    rows = total.shape[0] // tiles
    slots = own.shape[2]
    scales = []
    for message in messages:
        norm = sum(message[n : n + 1, :1].astype(F32) for n in range(3))
        scales.append(jnp.minimum(1.0, math.sqrt(entries) / jnp.sqrt(norm + 1e-06)) / islands)
    handed = [m for m in messages[:0:-1] if m.shape[0] > NOTE_ROWS + slots]

    def compute(features):
        squares = 0.0
        for m in range(tiles):
            part = slice(m * rows, (m + 1) * rows)
            average = drift_sum[part, :]
            if handed:
                size = handed[0].shape[0] - NOTE_ROWS - slots
                n, first = divmod(m * rows, size)
                first += NOTE_ROWS + slots
                average = average + handed[n][first : first + rows, :].astype(F32)
            average = average * (1.0 / islands)
            for d in range(islands):
                factor = messages[d][NOTE_ROWS : NOTE_ROWS + slots, :]
                average = average + scales[d] * dot(features[d, part, :], factor, ((1,), (0,)))
            total[part, :] = average
            squares = squares + jnp.sum(average * average, axis=0, keepdims=True)
        square[...] = squares

    pl.when(spot[5] == 1)(lambda: compute(own))
    pl.when(spot[5] != 1)(lambda: compute(moved))
    peak = jnp.max(jnp.abs(total[...]))
    unit = jnp.maximum(peak, 1e-30) / 32768
    for n, half in enumerate(halves):
        size = half.shape[0]
        value = total[n * size : (n + 1) * size, :] * (1 / unit)
        spread_out = value * 8193.0
        value = spread_out - (spread_out - value)
        half[...] = jnp.where(jnp.abs(value) < 2.0**-13, 0.0, value)
    sublane = lax.broadcasted_iota(jnp.int32, notes.shape, 1)
    notes[...] = jnp.where(sublane == 0, jnp.sum(square[...]), unit)


def hand_kernel(islands, tails, spot, norms, hidden, *refs):
    features, relays = refs[:islands], refs[islands : islands + len(tails)]
    joined, *messages = refs[islands + len(tails) :]
    across, slots, columns = hidden.shape
    for n in range(islands):
        joined[n] = features[n][...]
    left = jnp.sum(norms[...], axis=0)[:1, :1]
    rows = lax.broadcasted_iota(jnp.int32, (NOTE_ROWS, columns), 0)
    note = jnp.zeros((NOTE_ROWS, columns), F32)
    for n in range(3):
        summand = left.astype(BF16).astype(F32)
        note = jnp.where(rows == n, summand, note)
        left = left - summand
    for d, message in enumerate(messages):
        message[:NOTE_ROWS, :] = note.astype(BF16)
        block = lax.rem(partner(spot[3], d, islands), across)
        message[NOTE_ROWS : NOTE_ROWS + slots, :] = hidden[pl.ds(block, 1)][0]
        if d in tails:
            message[NOTE_ROWS + slots :, :] = relays[tails.index(d)][...]


def own_kernel(slots, block, slots_out, block_out):
    slots_out[...] = slots[...]
    block_out[...] = block[...]


def update_kernel(entries, pieces, place, notes, momentum, *refs):
    values = refs[: len(pieces)]
    new_momentum, outer_step, moved, step, in_sems, sems = refs[-6:]
    rows, columns = values[0].shape
    spots, loads = [], []
    for n, (d, first) in enumerate(pieces):
        top = pl.multiple_of(pl.multiple_of(place[3 * d], 32) + first, 32)
        left = pl.multiple_of(place[3 * d + 1], columns)
        spots.append((0, pl.ds(top, rows), pl.ds(left, columns)))
        loads.append(pltpu.make_async_copy(momentum.at[spots[n]], moved.at[n], in_sems.at[n]))
        loads[-1].start()
    square = jnp.sum(notes[...], axis=0)[:1, :1]
    clip = jnp.minimum(1.0, 0.25 * math.sqrt(entries) / jnp.sqrt(square + 1e-06))
    stored = []
    for n, (d, first) in enumerate(pieces):
        unit = notes[pl.ds(place[3 * d + 2], 1)][0, 1:2, :1]
        clipped = (clip * unit) * values[n][...]
        loads[n].wait()
        fresh = 0.9 * moved[n] + clipped
        moved[n] = fresh
        step[n] = (0.7 * (clipped + 0.9 * fresh)).astype(BF16)
        for k, (here, out) in enumerate(((moved, new_momentum), (step, outer_step))):
            stored.append(pltpu.make_async_copy(here.at[n], out.at[spots[n]], sems.at[n, k]))
            stored[-1].start()
    for copy in stored:
        copy.wait()


def body(
    tokens,
    token_grads,
    slot_token,
    slot_count,
    slot_prob,
    gate_weight,
    down_weight,
    drift,
    momentum,
):
    islands, experts, parts = (lax.axis_size(a) for a in AXES)
    island, expert, part = (lax.axis_index(a) for a in AXES)
    devices = islands * experts * parts
    features, hidden = gate_weight.shape[2:]
    half = features // parts
    across = islands // parts
    columns = hidden // across
    entries = features * hidden * experts * parts
    slots = slot_token.shape[3]
    routed_rows = experts * slots
    holder = island // across
    spot = jnp.stack(
        [expert, part, island % across, island, jnp.int32(across), (part == holder).astype(jnp.int32)]
    ).astype(jnp.int32)

    handed = half // 2 if islands == 4 else 0
    steps = [0, 1, 2] if handed else list(range(islands))
    pieces = [(d, 0, half, n, 0) for n, d in enumerate(steps)]
    if handed:
        pieces += [(3, 0, handed, 1, half), (3, handed, handed, 2, half)]
    block_rows = [half + (handed if d else 0) for d in steps]
    picked = pl.pallas_call(
        lambda *refs: pick_kernel(experts, islands, pieces, *refs),
        in_specs=[SMEM] + [ANY] * 6,
        out_specs=[ANY] * (experts + len(steps)),
        out_shape=[jax.ShapeDtypeStruct((2 * slots, half), BF16)] * experts
        + [jax.ShapeDtypeStruct((rows, columns), BF16) for rows in block_rows],
        scratch_shapes=[
            pltpu.VMEM(slot_token.shape, jnp.int32),
            pltpu.SMEM(slot_count.shape, jnp.int32),
            pltpu.VMEM(slot_prob.shape, F32),
            pltpu.VMEM(tokens.shape, BF16),
            pltpu.VMEM(token_grads.shape, BF16),
            pltpu.VMEM((experts, 2 * slots, half), BF16),
            pltpu.VMEM((sum(p[2] for p in pieces), columns), BF16),
            pltpu.SemaphoreType.DMA((5,)),
            pltpu.SemaphoreType.DMA((len(pieces),)),
            pltpu.SemaphoreType.DMA((len(pieces) + experts,)),
        ],
        compiler_params=params(56),
        name="pick_slots",
    )(spot, slot_token, slot_count, slot_prob, tokens, token_grads, drift)
    arrived = [picked[0]] + [swap(picked[d], "expert", d) for d in range(1, experts)]
    blocks = list(picked[experts:])
    arrived[0], blocks[0] = pl.pallas_call(
        own_kernel,
        in_specs=[VMEM] * 2,
        out_specs=[VMEM] * 2,
        out_shape=[
            jax.ShapeDtypeStruct((2 * slots, half), BF16),
            jax.ShapeDtypeStruct((half, columns), BF16),
        ],
        compiler_params=params(6),
        name="own_parts",
    )(arrived[0], blocks[0])
    drift_in = [blocks[0]] + [swap(blocks[d], "island", d) for d in steps[1:]]
    joined, turned, drift_sum, *relays = pl.pallas_call(
        lambda *refs: join_kernel(experts, len(steps), *refs),
        in_specs=[VMEM] * (experts + len(steps)),
        out_specs=[VMEM] * (5 if handed else 3),
        out_shape=[
            jax.ShapeDtypeStruct((2 * routed_rows, half), BF16),
            jax.ShapeDtypeStruct((half, routed_rows), BF16),
            jax.ShapeDtypeStruct((half, columns), F32),
        ]
        + [jax.ShapeDtypeStruct((handed, columns), BF16)] * (2 if handed else 0),
        compiler_params=params(12 + routed_rows // 48),
        name="join_slots",
    )(*arrived, *drift_in)

    joined_all = [joined] + [swap(joined, "tensor", t) for t in range(1, parts)]

    def send_features(d):
        pairs = []
        for at in range(islands):
            to = partner(at, d, islands)
            pairs.append((at * parts + to // across, to * parts + to // across))
        return lax.ppermute(turned, ("island", "tensor"), pairs)

    def spread(value):
        result = value
        for t in range(1, parts):
            pairs = []
            for at in range(islands):
                keep = at // across
                pairs.append((at * parts + keep, at * parts + partner(keep, t, parts)))
            moved = lax.ppermute(value, ("island", "tensor"), pairs)
            result = moved if t == 1 else result + moved
        return result

    features_in = [send_features(d) for d in range(1, islands)]

    hidden_out, norms = pl.pallas_call(
        lambda *refs: hidden_kernel(parts, across, *refs),
        in_specs=[SMEM] + [VMEM] * (2 + parts),
        out_specs=[VMEM] * 2,
        out_shape=[
            jax.ShapeDtypeStruct((across, routed_rows, columns), BF16),
            jax.ShapeDtypeStruct((experts * parts, 8, 128), F32),
        ],
        compiler_params=params(16 + routed_rows // 48),
        name="hidden_grads",
    )(spot, gate_weight, down_weight, *joined_all)
    norms = lax.all_to_all(norms, AXES[1:], split_axis=0, concat_axis=0, tiled=True)

    tails = [2, 1] if handed else []
    message_rows = [
        NOTE_ROWS + routed_rows + (half - handed if d in tails else 0) for d in range(islands)
    ]
    features_in, *messages = pl.pallas_call(
        lambda *refs: hand_kernel(islands, tails, *refs),
        in_specs=[SMEM] + [VMEM] * (2 + islands + len(relays)),
        out_specs=[VMEM] * (1 + islands),
        out_shape=[jax.ShapeDtypeStruct((islands, half, routed_rows), BF16)]
        + [jax.ShapeDtypeStruct((rows, columns), BF16) for rows in message_rows],
        compiler_params=params(6 + routed_rows // 48),
        name="hand_on",
    )(spot, norms, hidden_out, turned, *features_in, *relays)
    features_moved = spread(features_in)
    messages_in = [messages[0]] + [swap(messages[d], "island", d) for d in range(1, islands)]

    *halves, notes = pl.pallas_call(
        lambda *refs: average_kernel(islands, entries, 4, *refs),
        in_specs=[SMEM] + [VMEM] * (3 + islands),
        out_specs=[VMEM] * 3,
        out_shape=[jax.ShapeDtypeStruct((half // 2, columns), F32)] * 2
        + [jax.ShapeDtypeStruct((devices, 8, 128), F32)],
        scratch_shapes=[pltpu.VMEM((half, columns), F32), pltpu.VMEM((1, columns), F32)],
        compiler_params=params(8 + routed_rows // 48),
        name="average_block",
    )(spot, drift_sum, features_in, features_moved, *messages_in)
    notes = lax.all_to_all(notes, AXES, split_axis=0, concat_axis=0, tiled=True)

    parted = half // 2
    sent = [v.astype(WIRE) for v in halves]
    values = {(0, 0): halves[0], (0, parted): halves[1]}
    last = {}
    if islands == 4:
        values[2, 0], values[1, parted] = swap(sent[0], "island", 2), swap(sent[1], "island", 1)
        beside, below = swap(sent[0], "island", 1), swap(sent[1], "island", 2)
        values[1, 0], values[2, parted] = beside, below
        last[3, 0], last[3, parted] = swap(beside, "island", 2), swap(below, "island", 1)
    else:
        for d in range(1, islands):
            for n in range(2):
                last[d, n * parted] = swap(sent[n], "island", d)
    place = []
    for d in range(islands):
        at = origin(island, d, islands)
        source = (at * experts + expert) * parts + part
        place += [(at // across) * half, (at % across) * columns, source]
    place = jnp.stack(place).astype(jnp.int32)
    values |= last
    return tuple(
        pl.pallas_call(
            lambda *refs: update_kernel(entries, list(values), *refs),
            in_specs=[SMEM, VMEM, ANY] + [VMEM] * len(values),
            out_specs=[ANY, ANY],
            out_shape=[
                jax.ShapeDtypeStruct(momentum.shape, F32),
                jax.ShapeDtypeStruct(momentum.shape, BF16),
            ],
            scratch_shapes=[
                pltpu.VMEM((len(values), parted, columns), F32),
                pltpu.VMEM((len(values), parted, columns), BF16),
                pltpu.SemaphoreType.DMA((len(values),)),
                pltpu.SemaphoreType.DMA((len(values), 2)),
            ],
            compiler_params=params(50),
            name="update_outputs",
        )(place, notes, momentum, *[v.astype(F32) for v in values.values()])
    )


def solution(mesh):
    return jax.shard_map(
        body,
        mesh=mesh,
        in_specs=(
            P("island", "expert", "tensor"),
            P("island", "expert", "tensor"),
            P("island", "expert", None, None),
            P("island", "expert", None),
            P("island", "expert", None, None),
            P("island", "expert", None, "tensor"),
            P("island", "expert", "tensor", None),
            P("island", "expert", None, "tensor"),
            P("expert", None, "tensor"),
        ),
        out_specs=(P("expert", None, "tensor"), P("expert", None, "tensor")),
        check_vma=False,
    )
```

```python
import functools
import math

import jax
import jax.numpy as jnp
from jax import lax
from jax.experimental import pallas as pl
from jax.experimental.pallas import tpu as pltpu
from jax.sharding import PartitionSpec as P

F32 = jnp.float32
BF16 = jnp.bfloat16
WIRE = jnp.float16
AXES = ("island", "expert", "tensor")

VMEM = pl.BlockSpec(memory_space=pltpu.VMEM)
SMEM = pl.BlockSpec(memory_space=pltpu.SMEM)
ANY = pl.BlockSpec(memory_space=pl.ANY)


def params(mib):
    return pltpu.CompilerParams(vmem_limit_bytes=mib << 20)


def partner(at, step, size):
    return at ^ step if size & (size - 1) == 0 else (at + step) % size


def origin(at, step, size):
    return at ^ step if size & (size - 1) == 0 else (at - step) % size


def swap(value, axis, step):
    size = lax.axis_size(axis)
    return lax.ppermute(value, axis, [(at, partner(at, step, size)) for at in range(size)])


def dot(a, b, contract):
    return lax.dot_general(a, b, (contract, ((), ())), preferred_element_type=F32)


def copy_all(sems, pairs):
    copies = [pltpu.make_async_copy(*pair, sems.at[n]) for n, pair in enumerate(pairs)]
    for copy in copies:
        copy.start()
    return copies


def pick_kernel(experts, spot, *refs):
    sources, outs = refs[:5], refs[5 : 5 + experts]
    table, count, weight, tokens, grads, sems = refs[5 + experts :]
    loads = copy_all(sems, list(zip(sources, refs[5 + experts : -1])))
    for copy in loads:
        copy.wait()
    slots = table.shape[-1]
    rows = lax.broadcasted_iota(jnp.int32, (slots, slots), 0)
    lanes = lax.broadcasted_iota(jnp.int32, (slots, slots), 1)

    def column(row):
        return jnp.sum(jnp.where(rows == lanes, row, 0), axis=1, keepdims=True)

    for d in range(experts):
        to = partner(spot[0], d, experts)
        live = lax.broadcasted_iota(jnp.int32, (slots, 1), 0) < count[0, 0, to]
        token = column(table[0, 0, pl.ds(to, 1), :].astype(F32)).astype(jnp.int32)
        chance = column(weight[0, 0, pl.ds(to, 1), :])
        ids = lax.broadcasted_iota(jnp.int32, (slots, tokens.shape[1]), 1)
        picks = jnp.where((ids == token) & live, 1.0, 0.0).astype(BF16)
        outs[d][:slots, :] = dot(picks, tokens[0], ((1,), (0,))).astype(BF16)
        chosen = dot(picks, grads[0], ((1,), (0,)))
        outs[d][slots:, :] = (chance * chosen).astype(BF16)


def cut_kernel(islands, pieces, spot, drift, *refs):
    *blocks, sems = refs
    rows, columns = blocks[0].shape
    pairs = []
    for d, first, count_rows, target, at_row in pieces:
        at = partner(spot[3], d, islands)
        top = pl.multiple_of(lax.div(at, spot[4]) * rows, rows) + first
        left = pl.multiple_of(lax.rem(at, spot[4]) * columns, columns)
        source = drift.at[0, 0, pl.ds(top, count_rows), pl.ds(left, columns)]
        pairs.append((source, blocks[target].at[pl.ds(at_row, count_rows)]))
    for copy in copy_all(sems, pairs):
        copy.wait()


def gather_kernel(count, *refs):
    arrived, joined = refs[:count], refs[count]
    slots = arrived[0].shape[0] // 2
    for n, piece in enumerate(arrived):
        joined[n * slots : (n + 1) * slots, :] = piece[:slots, :]
        joined[(count + n) * slots : (count + n + 1) * slots, :] = piece[slots:, :]


def join_kernel(blocks, joined, *refs):
    drifts, (turned, drift_sum) = refs[:blocks], refs[blocks : blocks + 2]
    rows = drift_sum.shape[0]
    for n, ref in enumerate(refs[blocks + 2 :]):
        ref[...] = drifts[1 + n][rows:, :]
    turned[...] = joined[: joined.shape[0] // 2, :].T
    added = drifts[0][...].astype(F32)
    for other in drifts[1:]:
        added = added + other[:rows, :].astype(F32)
    drift_sum[...] = added


def hidden_kernel(parts, across, spot, gate, down, *refs):
    joined, out, norms = refs[:parts], refs[parts], refs[-1]
    rows, half = joined[0].shape[0] // 2, joined[0].shape[1]
    columns = out.shape[2]
    starts = [pl.multiple_of(origin(spot[1], t, parts) * half, half) for t in range(parts)]
    hidden_gram = 0.0
    for r in range(across):
        first = r * columns
        value = 0.0
        back = 0.0
        for t in range(parts):
            block = gate[0, 0, pl.ds(starts[t], half), first : first + columns]
            value = value + dot(joined[t][:rows, :], block, ((1,), (0,)))
            block = down[0, 0, first : first + columns, pl.ds(starts[t], half)]
            back = back + dot(joined[t][rows:, :], block, ((1,), (1,)))
        rounded = (back * (value / (1.0 + jnp.exp(-value)))).astype(BF16)
        out[r] = rounded
        hidden_gram = hidden_gram + dot(rounded, rounded, ((1,), (1,)))
    input_gram = 0.0
    for t in range(parts):
        features = joined[t][:rows, :]
        input_gram = input_gram + dot(features, features, ((1,), (1,)))
    norms[...] = jnp.full(norms.shape, jnp.sum(hidden_gram * input_gram), F32)


def average_kernel(islands, entries, tiles, spot, norms, drift_sum, own, moved, *refs):
    messages = refs[:islands]
    *halves, notes, total, square = refs[islands:]
    rows = total.shape[0] // tiles
    slots = own.shape[2]
    group = norms.shape[0] // islands
    scales = []
    for d in range(islands):
        at = origin(spot[3], d, islands)
        norm = jnp.sum(norms[pl.ds(at * group, group)], axis=0)[:1, :1]
        scales.append(jnp.minimum(1.0, math.sqrt(entries) / jnp.sqrt(norm + 1e-06)) / islands)
    handed = [m for m in messages[:0:-1] if m.shape[0] > slots]

    def compute(features):
        squares = 0.0
        for m in range(tiles):
            part = slice(m * rows, (m + 1) * rows)
            average = drift_sum[part, :]
            if handed:
                size = handed[0].shape[0] - slots
                n, first = divmod(m * rows, size)
                first += slots
                average = average + handed[n][first : first + rows, :].astype(F32)
            average = average * (1.0 / islands)
            for d in range(islands):
                factor = messages[d][:slots, :]
                average = average + scales[d] * dot(features[d, part, :], factor, ((1,), (0,)))
            total[part, :] = average
            squares = squares + jnp.sum(average * average, axis=0, keepdims=True)
        square[...] = squares

    pl.when(spot[5] == 1)(lambda: compute(own))
    pl.when(spot[5] != 1)(lambda: compute(moved))
    peak = jnp.max(jnp.abs(total[...]))
    unit = jnp.maximum(peak, 1e-30) / 32768
    for n, half in enumerate(halves):
        size = half.shape[0]
        value = total[n * size : (n + 1) * size, :] * (1 / unit)
        spread_out = value * 8193.0
        value = spread_out - (spread_out - value)
        half[...] = jnp.where(jnp.abs(value) < 2.0**-13, 0.0, value)
    sublane = lax.broadcasted_iota(jnp.int32, notes.shape, 1)
    notes[...] = jnp.where(sublane == 0, jnp.sum(square[...]), unit)


def hand_kernel(islands, tails, spot, norms, hidden, *refs):
    features, relays = refs[:islands], refs[islands : islands + len(tails)]
    joined, passed, *messages = refs[islands + len(tails) :]
    across, slots, _ = hidden.shape
    for n in range(islands):
        joined[n] = features[n][...]
    passed[...] = norms[...]
    for d, message in enumerate(messages):
        block = lax.rem(partner(spot[3], d, islands), across)
        message[:slots, :] = hidden[pl.ds(block, 1)][0]
        if d in tails:
            message[slots:, :] = relays[tails.index(d)][...]


def own_kernel(slots, block, slots_out, block_out):
    slots_out[...] = slots[...]
    block_out[...] = block[...]


def update_kernel(entries, pieces, place, notes, momentum, *refs):
    values = refs[: len(pieces)]
    new_momentum, outer_step, moved, step, in_sems, sems = refs[-6:]
    rows, columns = values[0].shape
    spots, loads = [], []
    for n, (d, first) in enumerate(pieces):
        top = pl.multiple_of(pl.multiple_of(place[3 * d], 32) + first, 32)
        left = pl.multiple_of(place[3 * d + 1], columns)
        spots.append((0, pl.ds(top, rows), pl.ds(left, columns)))
        loads.append(pltpu.make_async_copy(momentum.at[spots[n]], moved.at[n], in_sems.at[n]))
        loads[-1].start()
    square = jnp.sum(notes[...], axis=0)[:1, :1]
    clip = jnp.minimum(1.0, 0.25 * math.sqrt(entries) / jnp.sqrt(square + 1e-06))
    stored = []
    for n, (d, first) in enumerate(pieces):
        unit = notes[pl.ds(place[3 * d + 2], 1)][0, 1:2, :1]
        clipped = (clip * unit) * values[n][...]
        loads[n].wait()
        fresh = 0.9 * moved[n] + clipped
        moved[n] = fresh
        step[n] = (0.7 * (clipped + 0.9 * fresh)).astype(BF16)
        for k, (here, out) in enumerate(((moved, new_momentum), (step, outer_step))):
            stored.append(pltpu.make_async_copy(here.at[n], out.at[spots[n]], sems.at[n, k]))
            stored[-1].start()
    for copy in stored:
        copy.wait()


def body(
    tokens,
    token_grads,
    slot_token,
    slot_count,
    slot_prob,
    gate_weight,
    down_weight,
    drift,
    momentum,
):
    islands, experts, parts = (lax.axis_size(a) for a in AXES)
    island, expert, part = (lax.axis_index(a) for a in AXES)
    devices = islands * experts * parts
    features, hidden = gate_weight.shape[2:]
    half = features // parts
    across = islands // parts
    columns = hidden // across
    entries = features * hidden * experts * parts
    slots = slot_token.shape[3]
    routed_rows = experts * slots
    holder = island // across
    spot = jnp.stack(
        [expert, part, island % across, island, jnp.int32(across), (part == holder).astype(jnp.int32)]
    ).astype(jnp.int32)

    handed = half // 2 if islands == 4 else 0
    steps = [0, 1, 2] if handed else list(range(islands))
    pieces = [(d, 0, half, n, 0) for n, d in enumerate(steps)]
    if handed:
        pieces += [(3, 0, handed, 1, half), (3, handed, handed, 2, half)]
    block_rows = [half + (handed if d else 0) for d in steps]
    picked = pl.pallas_call(
        lambda *refs: pick_kernel(experts, *refs),
        in_specs=[SMEM] + [ANY] * 5,
        out_specs=[VMEM] * experts,
        out_shape=[jax.ShapeDtypeStruct((2 * slots, half), BF16)] * experts,
        scratch_shapes=[
            pltpu.VMEM(slot_token.shape, jnp.int32),
            pltpu.SMEM(slot_count.shape, jnp.int32),
            pltpu.VMEM(slot_prob.shape, F32),
            pltpu.VMEM(tokens.shape, BF16),
            pltpu.VMEM(token_grads.shape, BF16),
            pltpu.SemaphoreType.DMA((5,)),
        ],
        compiler_params=params(56),
        name="pick_slots",
    )(spot, slot_token, slot_count, slot_prob, tokens, token_grads)
    blocks = pl.pallas_call(
        lambda *refs: cut_kernel(islands, pieces, *refs),
        in_specs=[SMEM, ANY],
        out_specs=[VMEM] * len(steps),
        out_shape=[jax.ShapeDtypeStruct((rows, columns), BF16) for rows in block_rows],
        scratch_shapes=[pltpu.SemaphoreType.DMA((len(pieces),))],
        compiler_params=params(56),
        name="cut_drift",
    )(spot, drift)
    arrived = [picked[0]] + [swap(picked[d], "expert", d) for d in range(1, experts)]
    drift_in = [blocks[0]] + [swap(blocks[d], "island", d) for d in steps[1:]]
    arrived[0], drift_in[0] = pl.pallas_call(
        own_kernel,
        in_specs=[VMEM] * 2,
        out_specs=[VMEM] * 2,
        out_shape=[
            jax.ShapeDtypeStruct((2 * slots, half), BF16),
            jax.ShapeDtypeStruct((half, columns), BF16),
        ],
        compiler_params=params(6),
        name="own_parts",
    )(arrived[0], drift_in[0])
    joined = pl.pallas_call(
        lambda *refs: gather_kernel(experts, *refs),
        in_specs=[VMEM] * experts,
        out_specs=VMEM,
        out_shape=jax.ShapeDtypeStruct((2 * routed_rows, half), BF16),
        compiler_params=params(6 + routed_rows // 48),
        name="gather_slots",
    )(*arrived)
    turned, drift_sum, *relays = pl.pallas_call(
        lambda *refs: join_kernel(len(steps), *refs),
        in_specs=[VMEM] * (1 + len(steps)),
        out_specs=[VMEM] * (4 if handed else 2),
        out_shape=[
            jax.ShapeDtypeStruct((half, routed_rows), BF16),
            jax.ShapeDtypeStruct((half, columns), F32),
        ]
        + [jax.ShapeDtypeStruct((handed, columns), BF16)] * (2 if handed else 0),
        compiler_params=params(12 + routed_rows // 48),
        name="join_blocks",
    )(joined, *drift_in)

    joined_all = [joined] + [swap(joined, "tensor", t) for t in range(1, parts)]

    def send_features(d):
        pairs = []
        for at in range(islands):
            to = partner(at, d, islands)
            pairs.append((at * parts + to // across, to * parts + to // across))
        return lax.ppermute(turned, ("island", "tensor"), pairs)

    def spread(value):
        result = value
        for t in range(1, parts):
            pairs = []
            for at in range(islands):
                keep = at // across
                pairs.append((at * parts + keep, at * parts + partner(keep, t, parts)))
            moved = lax.ppermute(value, ("island", "tensor"), pairs)
            result = moved if t == 1 else result + moved
        return result

    features_in = [send_features(d) for d in range(1, islands)]

    hidden_out, norms = pl.pallas_call(
        lambda *refs: hidden_kernel(parts, across, *refs),
        in_specs=[SMEM] + [VMEM] * (2 + parts),
        out_specs=[VMEM] * 2,
        out_shape=[
            jax.ShapeDtypeStruct((across, routed_rows, columns), BF16),
            jax.ShapeDtypeStruct((devices, 8, 128), F32),
        ],
        compiler_params=params(16 + routed_rows // 48),
        name="hidden_grads",
    )(spot, gate_weight, down_weight, *joined_all)
    tails = [2, 1] if handed else []
    message_rows = [
        routed_rows + (half - handed if d in tails else 0) for d in range(islands)
    ]
    features_in, norms, *messages = pl.pallas_call(
        lambda *refs: hand_kernel(islands, tails, *refs),
        in_specs=[SMEM] + [VMEM] * (2 + islands + len(relays)),
        out_specs=[VMEM] * (2 + islands),
        out_shape=[
            jax.ShapeDtypeStruct((islands, half, routed_rows), BF16),
            jax.ShapeDtypeStruct(norms.shape, F32),
        ]
        + [jax.ShapeDtypeStruct((rows, columns), BF16) for rows in message_rows],
        compiler_params=params(6 + routed_rows // 48),
        name="hand_on",
    )(spot, norms, hidden_out, turned, *features_in, *relays)
    features_moved = spread(features_in)
    norms = lax.all_to_all(norms, AXES, split_axis=0, concat_axis=0, tiled=True)
    messages_in = [messages[0]] + [swap(messages[d], "island", d) for d in range(1, islands)]

    *halves, notes = pl.pallas_call(
        lambda *refs: average_kernel(islands, entries, 2, *refs),
        in_specs=[SMEM] + [VMEM] * (4 + islands),
        out_specs=[VMEM] * 3,
        out_shape=[jax.ShapeDtypeStruct((half // 2, columns), F32)] * 2
        + [jax.ShapeDtypeStruct((devices, 8, 128), F32)],
        scratch_shapes=[pltpu.VMEM((half, columns), F32), pltpu.VMEM((1, columns), F32)],
        compiler_params=params(8 + routed_rows // 48),
        name="average_block",
    )(spot, norms, drift_sum, features_in, features_moved, *messages_in)
    notes = lax.all_to_all(notes, AXES, split_axis=0, concat_axis=0, tiled=True)

    parted = half // 2
    sent = [v.astype(WIRE) for v in halves]
    values = {(0, 0): halves[0], (0, parted): halves[1]}
    last = {}
    if islands == 4:
        values[2, 0], values[1, parted] = swap(sent[0], "island", 2), swap(sent[1], "island", 1)
        beside, below = swap(sent[0], "island", 1), swap(sent[1], "island", 2)
        values[1, 0], values[2, parted] = beside, below
        last[3, 0], last[3, parted] = swap(beside, "island", 2), swap(below, "island", 1)
    else:
        for d in range(1, islands):
            for n in range(2):
                last[d, n * parted] = swap(sent[n], "island", d)
    place = []
    for d in range(islands):
        at = origin(island, d, islands)
        source = (at * experts + expert) * parts + part
        place += [(at // across) * half, (at % across) * columns, source]
    place = jnp.stack(place).astype(jnp.int32)
    outs = []
    for values, cost in ((values, 12), (last, 3)):
        outs = pl.pallas_call(
            functools.partial(update_kernel, entries, list(values)),
            in_specs=[SMEM, VMEM, ANY] + [VMEM] * len(values) + [ANY] * len(outs),
            out_specs=[ANY, ANY],
            out_shape=[
                jax.ShapeDtypeStruct(momentum.shape, F32),
                jax.ShapeDtypeStruct(momentum.shape, BF16),
            ],
            scratch_shapes=[
                pltpu.VMEM((len(values), parted, columns), F32),
                pltpu.VMEM((len(values), parted, columns), BF16),
                pltpu.SemaphoreType.DMA((len(values),)),
                pltpu.SemaphoreType.DMA((len(values), 2)),
            ],
            input_output_aliases={3 + len(values) + n: n for n in range(len(outs))},
            cost_estimate=pl.CostEstimate(
                flops=0, bytes_accessed=cost * momentum.size, transcendentals=0
            ),
            compiler_params=params(50),
            name="update_pieces",
        )(place, notes, momentum, *[v.astype(F32) for v in values.values()], *outs)
    return tuple(outs)


def solution(mesh):
    return jax.shard_map(
        body,
        mesh=mesh,
        in_specs=(
            P("island", "expert", "tensor"),
            P("island", "expert", "tensor"),
            P("island", "expert", None, None),
            P("island", "expert", None),
            P("island", "expert", None, None),
            P("island", "expert", None, "tensor"),
            P("island", "expert", "tensor", None),
            P("island", "expert", None, "tensor"),
            P("expert", None, "tensor"),
        ),
        out_specs=(P("expert", None, "tensor"), P("expert", None, "tensor")),
        check_vma=False,
    )
```

```python
import functools
import math

import jax
import jax.numpy as jnp
from jax import lax
from jax.experimental import pallas as pl
from jax.experimental.pallas import tpu as pltpu
from jax.sharding import PartitionSpec as P

F32 = jnp.float32
BF16 = jnp.bfloat16
WIRE = jnp.float16
AXES = ("island", "expert", "tensor")

VMEM = pl.BlockSpec(memory_space=pltpu.VMEM)
SMEM = pl.BlockSpec(memory_space=pltpu.SMEM)
ANY = pl.BlockSpec(memory_space=pl.ANY)


def params(mib):
    return pltpu.CompilerParams(vmem_limit_bytes=mib << 20)


def partner(at, step, size):
    return at ^ step if size & (size - 1) == 0 else (at + step) % size


def origin(at, step, size):
    return at ^ step if size & (size - 1) == 0 else (at - step) % size


def swap(value, axis, step):
    size = lax.axis_size(axis)
    return lax.ppermute(value, axis, [(at, partner(at, step, size)) for at in range(size)])


def dot(a, b, contract):
    return lax.dot_general(a, b, (contract, ((), ())), preferred_element_type=F32)


def copy_all(sems, pairs):
    copies = [pltpu.make_async_copy(*pair, sems.at[n]) for n, pair in enumerate(pairs)]
    for copy in copies:
        copy.start()
    return copies


def pick_kernel(experts, spot, *refs):
    sources, outs = refs[:5], refs[5 : 5 + experts]
    table, count, weight, tokens, grads, sems = refs[5 + experts :]
    loads = copy_all(sems, list(zip(sources, refs[5 + experts : -1])))
    for copy in loads:
        copy.wait()
    slots = table.shape[-1]
    rows = lax.broadcasted_iota(jnp.int32, (slots, slots), 0)
    lanes = lax.broadcasted_iota(jnp.int32, (slots, slots), 1)

    def column(row):
        return jnp.sum(jnp.where(rows == lanes, row, 0), axis=1, keepdims=True)

    for d in range(experts):
        to = partner(spot[0], d, experts)
        live = lax.broadcasted_iota(jnp.int32, (slots, 1), 0) < count[0, 0, to]
        token = column(table[0, 0, pl.ds(to, 1), :].astype(F32)).astype(jnp.int32)
        chance = column(weight[0, 0, pl.ds(to, 1), :])
        ids = lax.broadcasted_iota(jnp.int32, (slots, tokens.shape[1]), 1)
        picks = jnp.where((ids == token) & live, 1.0, 0.0).astype(BF16)
        outs[d][:slots, :] = dot(picks, tokens[0], ((1,), (0,))).astype(BF16)
        chosen = dot(picks, grads[0], ((1,), (0,)))
        outs[d][slots:, :] = (chance * chosen).astype(BF16)


def cut_kernel(islands, pieces, spot, drift, *refs):
    *blocks, sems = refs
    rows, columns = blocks[0].shape
    pairs = []
    for d, first, count_rows, target, at_row in pieces:
        at = partner(spot[3], d, islands)
        top = pl.multiple_of(lax.div(at, spot[4]) * rows, rows) + first
        left = pl.multiple_of(lax.rem(at, spot[4]) * columns, columns)
        source = drift.at[0, 0, pl.ds(top, count_rows), pl.ds(left, columns)]
        pairs.append((source, blocks[target].at[pl.ds(at_row, count_rows)]))
    for copy in copy_all(sems, pairs):
        copy.wait()


def gather_kernel(count, *refs):
    arrived, joined = refs[:count], refs[count]
    slots = arrived[0].shape[0] // 2
    for n, piece in enumerate(arrived):
        joined[n * slots : (n + 1) * slots, :] = piece[:slots, :]
        joined[(count + n) * slots : (count + n + 1) * slots, :] = piece[slots:, :]


def join_kernel(blocks, joined, *refs):
    drifts, (turned, drift_sum) = refs[:blocks], refs[blocks : blocks + 2]
    rows = drift_sum.shape[0]
    for n, ref in enumerate(refs[blocks + 2 :]):
        ref[...] = drifts[1 + n][rows:, :]
    turned[...] = joined[: joined.shape[0] // 2, :].T
    added = drifts[0][...].astype(F32)
    for other in drifts[1:]:
        added = added + other[:rows, :].astype(F32)
    drift_sum[...] = added


def hidden_kernel(parts, across, spot, gate, down, *refs):
    joined, out, norms = refs[:parts], refs[parts], refs[-1]
    rows, half = joined[0].shape[0] // 2, joined[0].shape[1]
    columns = out.shape[2]
    starts = [pl.multiple_of(origin(spot[1], t, parts) * half, half) for t in range(parts)]
    hidden_gram = 0.0
    for r in range(across):
        first = r * columns
        value = 0.0
        back = 0.0
        for t in range(parts):
            block = gate[0, 0, pl.ds(starts[t], half), first : first + columns]
            value = value + dot(joined[t][:rows, :], block, ((1,), (0,)))
            block = down[0, 0, first : first + columns, pl.ds(starts[t], half)]
            back = back + dot(joined[t][rows:, :], block, ((1,), (1,)))
        rounded = (back * (value / (1.0 + jnp.exp(-value)))).astype(BF16)
        out[r] = rounded
        hidden_gram = hidden_gram + dot(rounded, rounded, ((1,), (1,)))
    input_gram = 0.0
    for t in range(parts):
        features = joined[t][:rows, :]
        input_gram = input_gram + dot(features, features, ((1,), (1,)))
    norms[...] = jnp.full(norms.shape, jnp.sum(hidden_gram * input_gram), F32)


def average_kernel(islands, entries, tiles, spot, norms, drift_sum, own, moved, *refs):
    messages = refs[:islands]
    *halves, notes, total, square = refs[islands:]
    rows = total.shape[0] // tiles
    slots = own.shape[2]
    group = norms.shape[0] // islands
    scales = []
    for d in range(islands):
        at = origin(spot[3], d, islands)
        norm = jnp.sum(norms[pl.ds(at * group, group)], axis=0)[:1, :1]
        scales.append(jnp.minimum(1.0, math.sqrt(entries) / jnp.sqrt(norm + 1e-06)) / islands)
    handed = [m for m in messages[:0:-1] if m.shape[0] > slots]

    def compute(features):
        squares = 0.0
        for m in range(tiles):
            part = slice(m * rows, (m + 1) * rows)
            average = drift_sum[part, :]
            if handed:
                size = handed[0].shape[0] - slots
                n, first = divmod(m * rows, size)
                first += slots
                average = average + handed[n][first : first + rows, :].astype(F32)
            average = average * (1.0 / islands)
            for d in range(islands):
                factor = messages[d][:slots, :]
                average = average + scales[d] * dot(features[d, part, :], factor, ((1,), (0,)))
            total[part, :] = average
            squares = squares + jnp.sum(average * average, axis=0, keepdims=True)
        square[...] = squares

    pl.when(spot[5] == 1)(lambda: compute(own))
    pl.when(spot[5] != 1)(lambda: compute(moved))
    peak = jnp.max(jnp.abs(total[...]))
    unit = jnp.maximum(peak, 1e-30) / 32768
    for n, half in enumerate(halves):
        size = half.shape[0]
        value = total[n * size : (n + 1) * size, :] * (1 / unit)
        spread_out = value * 8193.0
        value = spread_out - (spread_out - value)
        half[...] = jnp.where(jnp.abs(value) < 2.0**-13, 0.0, value)
    sublane = lax.broadcasted_iota(jnp.int32, notes.shape, 1)
    notes[...] = jnp.where(sublane == 0, jnp.sum(square[...]), unit)


def hand_kernel(islands, tails, spot, norms, hidden, *refs):
    features, relays = refs[:islands], refs[islands : islands + len(tails)]
    joined, passed, *messages = refs[islands + len(tails) :]
    across, slots, _ = hidden.shape
    for n in range(islands):
        joined[n] = features[n][...]
    passed[...] = norms[...]
    for d, message in enumerate(messages):
        block = lax.rem(partner(spot[3], d, islands), across)
        message[:slots, :] = hidden[pl.ds(block, 1)][0]
        if d in tails:
            message[slots:, :] = relays[tails.index(d)][...]


def own_kernel(slots, block, slots_out, block_out):
    slots_out[...] = slots[...]
    block_out[...] = block[...]


def update_kernel(entries, pieces, place, notes, momentum, *refs):
    values = refs[: len(pieces)]
    new_momentum, outer_step, moved, step, in_sems, sems = refs[-6:]
    rows, columns = values[0].shape
    spots, loads = [], []
    for n, (d, first) in enumerate(pieces):
        top = pl.multiple_of(pl.multiple_of(place[3 * d], 32) + first, 32)
        left = pl.multiple_of(place[3 * d + 1], columns)
        spots.append((0, pl.ds(top, rows), pl.ds(left, columns)))
        loads.append(pltpu.make_async_copy(momentum.at[spots[n]], moved.at[n], in_sems.at[n]))
        loads[-1].start()
    square = jnp.sum(notes[...], axis=0)[:1, :1]
    clip = jnp.minimum(1.0, 0.25 * math.sqrt(entries) / jnp.sqrt(square + 1e-06))
    stored = []
    for n, (d, first) in enumerate(pieces):
        unit = notes[pl.ds(place[3 * d + 2], 1)][0, 1:2, :1]
        clipped = (clip * unit) * values[n][...]
        loads[n].wait()
        fresh = 0.9 * moved[n] + clipped
        moved[n] = fresh
        step[n] = (0.7 * (clipped + 0.9 * fresh)).astype(BF16)
        for k, (here, out) in enumerate(((moved, new_momentum), (step, outer_step))):
            stored.append(pltpu.make_async_copy(here.at[n], out.at[spots[n]], sems.at[n, k]))
            stored[-1].start()
    for copy in stored:
        copy.wait()


def body(
    tokens,
    token_grads,
    slot_token,
    slot_count,
    slot_prob,
    gate_weight,
    down_weight,
    drift,
    momentum,
):
    islands, experts, parts = (lax.axis_size(a) for a in AXES)
    island, expert, part = (lax.axis_index(a) for a in AXES)
    features, hidden = gate_weight.shape[2:]
    half = features // parts
    across = islands // parts
    columns = hidden // across
    entries = features * hidden * experts * parts
    slots = slot_token.shape[3]
    routed_rows = experts * slots
    holder = island // across
    spot = jnp.stack(
        [expert, part, island % across, island, jnp.int32(across), (part == holder).astype(jnp.int32)]
    ).astype(jnp.int32)

    handed = half // 2 if islands == 4 else 0
    steps = [0, 1, 2] if handed else list(range(islands))
    pieces = [(d, 0, half, n, 0) for n, d in enumerate(steps)]
    if handed:
        pieces += [(3, 0, handed, 1, half), (3, handed, handed, 2, half)]
    block_rows = [half + (handed if d else 0) for d in steps]
    picked = pl.pallas_call(
        lambda *refs: pick_kernel(experts, *refs),
        in_specs=[SMEM] + [ANY] * 5,
        out_specs=[VMEM] * experts,
        out_shape=[jax.ShapeDtypeStruct((2 * slots, half), BF16)] * experts,
        scratch_shapes=[
            pltpu.VMEM(slot_token.shape, jnp.int32),
            pltpu.SMEM(slot_count.shape, jnp.int32),
            pltpu.VMEM(slot_prob.shape, F32),
            pltpu.VMEM(tokens.shape, BF16),
            pltpu.VMEM(token_grads.shape, BF16),
            pltpu.SemaphoreType.DMA((5,)),
        ],
        compiler_params=params(56),
        name="pick_slots",
    )(spot, slot_token, slot_count, slot_prob, tokens, token_grads)
    blocks = pl.pallas_call(
        lambda *refs: cut_kernel(islands, pieces, *refs),
        in_specs=[SMEM, ANY],
        out_specs=[VMEM] * len(steps),
        out_shape=[jax.ShapeDtypeStruct((rows, columns), BF16) for rows in block_rows],
        scratch_shapes=[pltpu.SemaphoreType.DMA((len(pieces),))],
        compiler_params=params(56),
        name="cut_drift",
    )(spot, drift)
    arrived = [picked[0]] + [swap(picked[d], "expert", d) for d in range(1, experts)]
    drift_in = [blocks[0]] + [swap(blocks[d], "island", d) for d in steps[1:]]
    arrived[0], drift_in[0] = pl.pallas_call(
        own_kernel,
        in_specs=[VMEM] * 2,
        out_specs=[VMEM] * 2,
        out_shape=[
            jax.ShapeDtypeStruct((2 * slots, half), BF16),
            jax.ShapeDtypeStruct((half, columns), BF16),
        ],
        compiler_params=params(6),
        name="own_parts",
    )(arrived[0], drift_in[0])
    joined = pl.pallas_call(
        lambda *refs: gather_kernel(experts, *refs),
        in_specs=[VMEM] * experts,
        out_specs=VMEM,
        out_shape=jax.ShapeDtypeStruct((2 * routed_rows, half), BF16),
        compiler_params=params(6 + routed_rows // 48),
        name="gather_slots",
    )(*arrived)
    turned, drift_sum, *relays = pl.pallas_call(
        lambda *refs: join_kernel(len(steps), *refs),
        in_specs=[VMEM] * (1 + len(steps)),
        out_specs=[VMEM] * (4 if handed else 2),
        out_shape=[
            jax.ShapeDtypeStruct((half, routed_rows), BF16),
            jax.ShapeDtypeStruct((half, columns), F32),
        ]
        + [jax.ShapeDtypeStruct((handed, columns), BF16)] * (2 if handed else 0),
        compiler_params=params(12 + routed_rows // 48),
        name="join_blocks",
    )(joined, *drift_in)

    joined_all = [joined] + [swap(joined, "tensor", t) for t in range(1, parts)]

    def send_features(d):
        pairs = []
        for at in range(islands):
            to = partner(at, d, islands)
            pairs.append((at * parts + to // across, to * parts + to // across))
        return lax.ppermute(turned, ("island", "tensor"), pairs)

    def spread(value):
        result = value
        for t in range(1, parts):
            pairs = []
            for at in range(islands):
                keep = at // across
                pairs.append((at * parts + keep, at * parts + partner(keep, t, parts)))
            moved = lax.ppermute(value, ("island", "tensor"), pairs)
            result = moved if t == 1 else result + moved
        return result

    features_in = [send_features(d) for d in range(1, islands)]

    hidden_out, norms = pl.pallas_call(
        lambda *refs: hidden_kernel(parts, across, *refs),
        in_specs=[SMEM] + [VMEM] * (2 + parts),
        out_specs=[VMEM] * 2,
        out_shape=[
            jax.ShapeDtypeStruct((across, routed_rows, columns), BF16),
            jax.ShapeDtypeStruct((1, 8, 128), F32),
        ],
        compiler_params=params(16 + routed_rows // 48),
        name="hidden_grads",
    )(spot, gate_weight, down_weight, *joined_all)
    tails = [2, 1] if handed else []
    message_rows = [
        routed_rows + (half - handed if d in tails else 0) for d in range(islands)
    ]
    features_in, norms, *messages = pl.pallas_call(
        lambda *refs: hand_kernel(islands, tails, *refs),
        in_specs=[SMEM] + [VMEM] * (2 + islands + len(relays)),
        out_specs=[VMEM] * (2 + islands),
        out_shape=[
            jax.ShapeDtypeStruct((islands, half, routed_rows), BF16),
            jax.ShapeDtypeStruct(norms.shape, F32),
        ]
        + [jax.ShapeDtypeStruct((rows, columns), BF16) for rows in message_rows],
        compiler_params=params(6 + routed_rows // 48),
        name="hand_on",
    )(spot, norms, hidden_out, turned, *features_in, *relays)
    features_moved = spread(features_in)
    norms = lax.all_gather(norms, AXES, axis=0, tiled=True)
    messages_in = [messages[0]] + [swap(messages[d], "island", d) for d in range(1, islands)]

    *halves, notes = pl.pallas_call(
        lambda *refs: average_kernel(islands, entries, 2, *refs),
        in_specs=[SMEM] + [VMEM] * (4 + islands),
        out_specs=[VMEM] * 3,
        out_shape=[jax.ShapeDtypeStruct((half // 2, columns), F32)] * 2
        + [jax.ShapeDtypeStruct((1, 8, 128), F32)],
        scratch_shapes=[pltpu.VMEM((half, columns), F32), pltpu.VMEM((1, columns), F32)],
        compiler_params=params(8 + routed_rows // 48),
        name="average_block",
    )(spot, norms, drift_sum, features_in, features_moved, *messages_in)
    notes = lax.all_gather(notes, AXES, axis=0, tiled=True)

    parted = half // 2
    sent = [v.astype(WIRE) for v in halves]
    values = {(0, 0): halves[0], (0, parted): halves[1]}
    last = {}
    if islands == 4:
        values[2, 0], values[1, parted] = swap(sent[0], "island", 2), swap(sent[1], "island", 1)
        beside, below = swap(sent[0], "island", 1), swap(sent[1], "island", 2)
        values[1, 0], values[2, parted] = beside, below
        last[3, 0], last[3, parted] = swap(beside, "island", 2), swap(below, "island", 1)
    else:
        for d in range(1, islands):
            for n in range(2):
                last[d, n * parted] = swap(sent[n], "island", d)
    place = []
    for d in range(islands):
        at = origin(island, d, islands)
        source = (at * experts + expert) * parts + part
        place += [(at // across) * half, (at % across) * columns, source]
    place = jnp.stack(place).astype(jnp.int32)
    outs = []
    for values, cost in ((values, 12), (last, 3)):
        outs = pl.pallas_call(
            functools.partial(update_kernel, entries, list(values)),
            in_specs=[SMEM, VMEM, ANY] + [VMEM] * len(values) + [ANY] * len(outs),
            out_specs=[ANY, ANY],
            out_shape=[
                jax.ShapeDtypeStruct(momentum.shape, F32),
                jax.ShapeDtypeStruct(momentum.shape, BF16),
            ],
            scratch_shapes=[
                pltpu.VMEM((len(values), parted, columns), F32),
                pltpu.VMEM((len(values), parted, columns), BF16),
                pltpu.SemaphoreType.DMA((len(values),)),
                pltpu.SemaphoreType.DMA((len(values), 2)),
            ],
            input_output_aliases={3 + len(values) + n: n for n in range(len(outs))},
            cost_estimate=pl.CostEstimate(
                flops=0, bytes_accessed=cost * momentum.size, transcendentals=0
            ),
            compiler_params=params(50),
            name="update_pieces",
        )(place, notes, momentum, *[v.astype(F32) for v in values.values()], *outs)
    return tuple(outs)


def solution(mesh):
    return jax.shard_map(
        body,
        mesh=mesh,
        in_specs=(
            P("island", "expert", "tensor"),
            P("island", "expert", "tensor"),
            P("island", "expert", None, None),
            P("island", "expert", None),
            P("island", "expert", None, None),
            P("island", "expert", None, "tensor"),
            P("island", "expert", "tensor", None),
            P("island", "expert", None, "tensor"),
            P("expert", None, "tensor"),
        ),
        out_specs=(P("expert", None, "tensor"), P("expert", None, "tensor")),
        check_vma=False,
    )
```

```python
import functools
import math

import jax
import jax.numpy as jnp
from jax import lax
from jax.experimental import pallas as pl
from jax.experimental.pallas import tpu as pltpu
from jax.sharding import PartitionSpec as P

F32 = jnp.float32
BF16 = jnp.bfloat16
WIRE = jnp.float16
AXES = ("island", "expert", "tensor")

VMEM = pl.BlockSpec(memory_space=pltpu.VMEM)
SMEM = pl.BlockSpec(memory_space=pltpu.SMEM)
ANY = pl.BlockSpec(memory_space=pl.ANY)


def params(mib):
    return pltpu.CompilerParams(vmem_limit_bytes=mib << 20)


def partner(at, step, size):
    return at ^ step if size & (size - 1) == 0 else (at + step) % size


def origin(at, step, size):
    return at ^ step if size & (size - 1) == 0 else (at - step) % size


def swap(value, axis, step):
    size = lax.axis_size(axis)
    return lax.ppermute(value, axis, [(at, partner(at, step, size)) for at in range(size)])


def dot(a, b, contract):
    return lax.dot_general(a, b, (contract, ((), ())), preferred_element_type=F32)


def copy_all(sems, pairs):
    copies = [pltpu.make_async_copy(*pair, sems.at[n]) for n, pair in enumerate(pairs)]
    for copy in copies:
        copy.start()
    return copies


def pick_kernel(experts, spot, *refs):
    sources, outs = refs[:5], refs[5 : 5 + experts]
    table, count, weight, tokens, grads, sems = refs[5 + experts :]
    loads = copy_all(sems, list(zip(sources, refs[5 + experts : -1])))
    for copy in loads:
        copy.wait()
    slots = table.shape[-1]
    rows = lax.broadcasted_iota(jnp.int32, (slots, slots), 0)
    lanes = lax.broadcasted_iota(jnp.int32, (slots, slots), 1)

    def column(row):
        return jnp.sum(jnp.where(rows == lanes, row, 0), axis=1, keepdims=True)

    for d in range(experts):
        to = partner(spot[0], d, experts)
        live = lax.broadcasted_iota(jnp.int32, (slots, 1), 0) < count[0, 0, to]
        token = column(table[0, 0, pl.ds(to, 1), :].astype(F32)).astype(jnp.int32)
        chance = column(weight[0, 0, pl.ds(to, 1), :])
        ids = lax.broadcasted_iota(jnp.int32, (slots, tokens.shape[1]), 1)
        picks = jnp.where((ids == token) & live, 1.0, 0.0).astype(BF16)
        outs[d][:slots, :] = dot(picks, tokens[0], ((1,), (0,))).astype(BF16)
        chosen = dot(picks, grads[0], ((1,), (0,)))
        outs[d][slots:, :] = (chance * chosen).astype(BF16)


def cut_kernel(islands, pieces, spot, drift, *refs):
    *blocks, sems = refs
    rows, columns = blocks[0].shape
    pairs = []
    for d, first, count_rows, target, at_row in pieces:
        at = partner(spot[3], d, islands)
        top = pl.multiple_of(lax.div(at, spot[4]) * rows, rows) + first
        left = pl.multiple_of(lax.rem(at, spot[4]) * columns, columns)
        source = drift.at[0, 0, pl.ds(top, count_rows), pl.ds(left, columns)]
        pairs.append((source, blocks[target].at[pl.ds(at_row, count_rows)]))
    for copy in copy_all(sems, pairs):
        copy.wait()


def gather_kernel(count, *refs):
    arrived, joined = refs[:count], refs[count]
    slots = arrived[0].shape[0] // 2
    for n, piece in enumerate(arrived):
        joined[n * slots : (n + 1) * slots, :] = piece[:slots, :]
        joined[(count + n) * slots : (count + n + 1) * slots, :] = piece[slots:, :]


def join_kernel(blocks, joined, *refs):
    drifts, (turned, drift_sum) = refs[:blocks], refs[blocks : blocks + 2]
    rows = drift_sum.shape[0]
    for n, ref in enumerate(refs[blocks + 2 :]):
        ref[...] = drifts[1 + n][rows:, :]
    turned[...] = joined[: joined.shape[0] // 2, :].T
    added = drifts[0][...].astype(F32)
    for other in drifts[1:]:
        added = added + other[:rows, :].astype(F32)
    drift_sum[...] = added


def hidden_kernel(parts, islands, tails, spot, gate, down, *refs):
    joined, relays = refs[:parts], refs[parts : parts + len(tails)]
    *messages, norms, hidden = refs[parts + len(tails) :]
    across, slots, columns = hidden.shape
    half = joined[0].shape[1]
    starts = [pl.multiple_of(origin(spot[1], t, parts) * half, half) for t in range(parts)]
    hidden_gram = 0.0
    for r in range(across):
        first = r * columns
        value = 0.0
        back = 0.0
        for t in range(parts):
            block = gate[0, 0, pl.ds(starts[t], half), first : first + columns]
            value = value + dot(joined[t][:slots, :], block, ((1,), (0,)))
            block = down[0, 0, first : first + columns, pl.ds(starts[t], half)]
            back = back + dot(joined[t][slots:, :], block, ((1,), (1,)))
        rounded = (back * (value / (1.0 + jnp.exp(-value)))).astype(BF16)
        hidden[r] = rounded
        hidden_gram = hidden_gram + dot(rounded, rounded, ((1,), (1,)))
    for d, message in enumerate(messages):
        block = lax.rem(partner(spot[3], d, islands), across)
        message[:slots, :] = hidden[pl.ds(block, 1)][0]
        if d in tails:
            message[slots:, :] = relays[tails.index(d)][...]
    input_gram = 0.0
    for t in range(parts):
        features = joined[t][:slots, :]
        input_gram = input_gram + dot(features, features, ((1,), (1,)))
    norms[...] = jnp.full(norms.shape, jnp.sum(hidden_gram * input_gram), F32)


def average_kernel(islands, entries, tiles, count, spot, norms, drift_sum, *refs):
    features, messages = refs[:count], refs[count : count + islands]
    *halves, notes, total, square = refs[count + islands :]
    rows = total.shape[0] // tiles
    slots = features[0].shape[1]
    group = norms.shape[0] // islands
    scales = []
    for d in range(islands):
        at = origin(spot[3], d, islands)
        norm = jnp.sum(norms[pl.ds(at * group, group)], axis=0)[:1, :1]
        scales.append(jnp.minimum(1.0, math.sqrt(entries) / jnp.sqrt(norm + 1e-06)) / islands)
    handed = [m for m in messages[:0:-1] if m.shape[0] > slots]

    def compute(blocks):
        squares = 0.0
        for m in range(tiles):
            part = slice(m * rows, (m + 1) * rows)
            average = drift_sum[part, :]
            if handed:
                size = handed[0].shape[0] - slots
                n, first = divmod(m * rows, size)
                first += slots
                average = average + handed[n][first : first + rows, :].astype(F32)
            average = average * (1.0 / islands)
            for d in range(islands):
                size = total.shape[0] // len(blocks[d])
                n, first = divmod(m * rows, size)
                block = blocks[d][n][first : first + rows, :]
                average = average + scales[d] * dot(block, messages[d][:slots, :], ((1,), (0,)))
            total[part, :] = average
            squares = squares + jnp.sum(average * average, axis=0, keepdims=True)
        square[...] = squares

    if count == islands:
        compute([[ref] for ref in features])
    else:
        turned, first, second, other, *others = features
        pl.when(spot[5] == 1)(lambda: compute([[turned], [first], [other], others]))
        pl.when(spot[5] != 1)(lambda: compute([[other], others, [first], [second]]))
    peak = jnp.max(jnp.abs(total[...]))
    unit = jnp.maximum(peak, 1e-30) / 32768
    for n, half in enumerate(halves):
        size = half.shape[0]
        value = total[n * size : (n + 1) * size, :] * (1 / unit)
        spread_out = value * 8193.0
        value = spread_out - (spread_out - value)
        half[...] = jnp.where(jnp.abs(value) < 2.0**-13, 0.0, value)
    sublane = lax.broadcasted_iota(jnp.int32, notes.shape, 1)
    notes[...] = jnp.where(sublane == 0, jnp.sum(square[...]), unit)


def choose_kernel(spot, one, other, out):
    out[...] = jnp.where(spot[5] == 1, one[...], other[...])


def choose_halves_kernel(spot, norms, one, other, earlier, top, bottom, passed):
    size = top.shape[0]
    top[...] = jnp.where(spot[5] == 1, one[:size, :], other[:size, :])
    bottom[...] = jnp.where(spot[5] == 1, one[size:, :], other[size:, :])
    passed[...] = norms[...]


def own_kernel(slots, block, slots_out, block_out):
    slots_out[...] = slots[...]
    block_out[...] = block[...]


def update_kernel(entries, pieces, place, notes, momentum, *refs):
    values = refs[: len(pieces)]
    new_momentum, outer_step, moved, step, in_sems, sems = refs[-6:]
    rows, columns = values[0].shape
    spots, loads = [], []
    for n, (d, first) in enumerate(pieces):
        top = pl.multiple_of(pl.multiple_of(place[3 * d], 32) + first, 32)
        left = pl.multiple_of(place[3 * d + 1], columns)
        spots.append((0, pl.ds(top, rows), pl.ds(left, columns)))
        loads.append(pltpu.make_async_copy(momentum.at[spots[n]], moved.at[n], in_sems.at[n]))
        loads[-1].start()
    square = jnp.sum(notes[...], axis=0)[:1, :1]
    clip = jnp.minimum(1.0, 0.25 * math.sqrt(entries) / jnp.sqrt(square + 1e-06))
    stored = []
    for n, (d, first) in enumerate(pieces):
        unit = notes[pl.ds(place[3 * d + 2], 1)][0, 1:2, :1]
        clipped = (clip * unit) * values[n][...]
        loads[n].wait()
        fresh = 0.9 * moved[n] + clipped
        moved[n] = fresh
        step[n] = (0.7 * (clipped + 0.9 * fresh)).astype(BF16)
        for k, (here, out) in enumerate(((moved, new_momentum), (step, outer_step))):
            stored.append(pltpu.make_async_copy(here.at[n], out.at[spots[n]], sems.at[n, k]))
            stored[-1].start()
    for copy in stored:
        copy.wait()


def body(
    tokens,
    token_grads,
    slot_token,
    slot_count,
    slot_prob,
    gate_weight,
    down_weight,
    drift,
    momentum,
):
    islands, experts, parts = (lax.axis_size(a) for a in AXES)
    island, expert, part = (lax.axis_index(a) for a in AXES)
    devices = islands * experts * parts
    features, hidden = gate_weight.shape[2:]
    half = features // parts
    across = islands // parts
    columns = hidden // across
    entries = features * hidden * experts * parts
    slots = slot_token.shape[3]
    routed_rows = experts * slots
    holder = island // across
    spot = jnp.stack(
        [expert, part, island % across, island, jnp.int32(across), (part == holder).astype(jnp.int32)]
    ).astype(jnp.int32)

    handed = half // 2 if islands == 4 else 0
    steps = [0, 1, 2] if handed else list(range(islands))
    pieces = [(d, 0, half, n, 0) for n, d in enumerate(steps)]
    if handed:
        pieces += [(3, 0, handed, 1, half), (3, handed, handed, 2, half)]
    block_rows = [half + (handed if d else 0) for d in steps]
    picked = pl.pallas_call(
        lambda *refs: pick_kernel(experts, *refs),
        in_specs=[SMEM] + [ANY] * 5,
        out_specs=[VMEM] * experts,
        out_shape=[jax.ShapeDtypeStruct((2 * slots, half), BF16)] * experts,
        scratch_shapes=[
            pltpu.VMEM(slot_token.shape, jnp.int32),
            pltpu.SMEM(slot_count.shape, jnp.int32),
            pltpu.VMEM(slot_prob.shape, F32),
            pltpu.VMEM(tokens.shape, BF16),
            pltpu.VMEM(token_grads.shape, BF16),
            pltpu.SemaphoreType.DMA((5,)),
        ],
        compiler_params=params(56),
        name="pick_slots",
    )(spot, slot_token, slot_count, slot_prob, tokens, token_grads)
    blocks = pl.pallas_call(
        lambda *refs: cut_kernel(islands, pieces, *refs),
        in_specs=[SMEM, ANY],
        out_specs=[VMEM] * len(steps),
        out_shape=[jax.ShapeDtypeStruct((rows, columns), BF16) for rows in block_rows],
        scratch_shapes=[pltpu.SemaphoreType.DMA((len(pieces),))],
        compiler_params=params(56),
        name="cut_drift",
    )(spot, drift)
    arrived = [picked[0]] + [swap(picked[d], "expert", d) for d in range(1, experts)]
    drift_in = [blocks[0]] + [swap(blocks[d], "island", d) for d in steps[1:]]
    arrived[0], drift_in[0] = pl.pallas_call(
        own_kernel,
        in_specs=[VMEM] * 2,
        out_specs=[VMEM] * 2,
        out_shape=[
            jax.ShapeDtypeStruct((2 * slots, half), BF16),
            jax.ShapeDtypeStruct((half, columns), BF16),
        ],
        compiler_params=params(6),
        name="own_parts",
    )(arrived[0], drift_in[0])
    joined = pl.pallas_call(
        lambda *refs: gather_kernel(experts, *refs),
        in_specs=[VMEM] * experts,
        out_specs=VMEM,
        out_shape=jax.ShapeDtypeStruct((2 * routed_rows, half), BF16),
        compiler_params=params(6 + routed_rows // 48),
        name="gather_slots",
    )(*arrived)
    turned, drift_sum, *relays = pl.pallas_call(
        lambda *refs: join_kernel(len(steps), *refs),
        in_specs=[VMEM] * (1 + len(steps)),
        out_specs=[VMEM] * (4 if handed else 2),
        out_shape=[
            jax.ShapeDtypeStruct((half, routed_rows), BF16),
            jax.ShapeDtypeStruct((half, columns), F32),
        ]
        + [jax.ShapeDtypeStruct((handed, columns), BF16)] * (2 if handed else 0),
        compiler_params=params(12 + routed_rows // 48),
        name="join_blocks",
    )(joined, *drift_in)

    joined_all = [joined] + [swap(joined, "tensor", t) for t in range(1, parts)]

    tails = [2, 1] if handed else []
    message_rows = [routed_rows + (half - handed if d in tails else 0) for d in range(islands)]
    *messages, norms = pl.pallas_call(
        lambda *refs: hidden_kernel(parts, islands, tails, *refs),
        in_specs=[SMEM] + [VMEM] * (2 + parts + len(tails)),
        out_specs=[VMEM] * (islands + 1),
        out_shape=[jax.ShapeDtypeStruct((rows, columns), BF16) for rows in message_rows]
        + [jax.ShapeDtypeStruct((devices, 8, 128), F32)],
        scratch_shapes=[pltpu.VMEM((across, routed_rows, columns), BF16)],
        compiler_params=params(18 + routed_rows // 48),
        name="hidden_grads",
    )(spot, gate_weight, down_weight, *joined_all, *relays)
    messages_in = [messages[0]] + [swap(messages[d], "island", d) for d in range(1, islands)]

    if handed and parts == 2:
        pairs, onward = [], []
        for at in range(islands):
            keep = at // across
            pairs += [
                (at * parts + keep, (at ^ 1) * parts + keep),
                (at * parts + 1 - keep, (at ^ 2) * parts + keep),
            ]
            onward.append((at * parts + 1 - keep, (at ^ 1) * parts + 1 - keep))
        first = lax.ppermute(turned, ("island", "tensor"), pairs)
        second = lax.ppermute(first, ("island", "tensor"), onward)
        block = jax.ShapeDtypeStruct((half, routed_rows), BF16)
        part_block = jax.ShapeDtypeStruct((half // 2, routed_rows), BF16)
        chosen = pl.pallas_call(
            choose_kernel,
            in_specs=[SMEM] + [VMEM] * 2,
            out_specs=VMEM,
            out_shape=block,
            compiler_params=params(4 + routed_rows // 48),
            name="choose_features",
        )(spot, turned, first)
        moved = swap(chosen, "tensor", 1)
        *chosen_halves, norms = pl.pallas_call(
            choose_halves_kernel,
            in_specs=[SMEM] + [VMEM] * 3 + [ANY],
            out_specs=[VMEM] * 3,
            out_shape=[part_block] * 2 + [jax.ShapeDtypeStruct(norms.shape, F32)],
            compiler_params=params(4 + routed_rows // 48),
            name="choose_halves",
        )(spot, norms, first, second, moved)
        features_of = [turned, first, second, moved]
        features_of += [swap(v, "tensor", 1) for v in chosen_halves]
    else:
        every = lax.all_gather(turned, ("island", "tensor"))
        features_of = [every[origin(island, d, islands) * parts + holder] for d in range(islands)]
    norms = lax.all_to_all(norms, AXES, split_axis=0, concat_axis=0, tiled=True)

    *halves, notes = pl.pallas_call(
        lambda *refs: average_kernel(islands, entries, 2, len(features_of), *refs),
        in_specs=[SMEM] + [VMEM] * (2 + len(features_of) + islands),
        out_specs=[VMEM] * 3,
        out_shape=[jax.ShapeDtypeStruct((half // 2, columns), F32)] * 2
        + [jax.ShapeDtypeStruct((devices, 8, 128), F32)],
        scratch_shapes=[pltpu.VMEM((half, columns), F32), pltpu.VMEM((1, columns), F32)],
        compiler_params=params(8 + routed_rows // 48),
        name="average_block",
    )(spot, norms, drift_sum, *features_of, *messages_in)
    notes = lax.all_to_all(notes, AXES, split_axis=0, concat_axis=0, tiled=True)

    parted = half // 2
    sent = [v.astype(WIRE) for v in halves]
    values = {(0, 0): halves[0], (0, parted): halves[1]}
    last = {}
    if islands == 4:
        values[2, 0], values[1, parted] = swap(sent[0], "island", 2), swap(sent[1], "island", 1)
        beside, below = swap(sent[0], "island", 1), swap(sent[1], "island", 2)
        values[1, 0], values[2, parted] = beside, below
        last[3, 0], last[3, parted] = swap(beside, "island", 2), swap(below, "island", 1)
    else:
        for d in range(1, islands):
            for n in range(2):
                last[d, n * parted] = swap(sent[n], "island", d)
    place = []
    for d in range(islands):
        at = origin(island, d, islands)
        source = (at * experts + expert) * parts + part
        place += [(at // across) * half, (at % across) * columns, source]
    place = jnp.stack(place).astype(jnp.int32)
    outs = []
    for values, cost in ((values, 12), (last, 3)):
        outs = pl.pallas_call(
            functools.partial(update_kernel, entries, list(values)),
            in_specs=[SMEM, VMEM, ANY] + [VMEM] * len(values) + [ANY] * len(outs),
            out_specs=[ANY, ANY],
            out_shape=[
                jax.ShapeDtypeStruct(momentum.shape, F32),
                jax.ShapeDtypeStruct(momentum.shape, BF16),
            ],
            scratch_shapes=[
                pltpu.VMEM((len(values), parted, columns), F32),
                pltpu.VMEM((len(values), parted, columns), BF16),
                pltpu.SemaphoreType.DMA((len(values),)),
                pltpu.SemaphoreType.DMA((len(values), 2)),
            ],
            input_output_aliases={3 + len(values) + n: n for n in range(len(outs))},
            cost_estimate=pl.CostEstimate(
                flops=0, bytes_accessed=cost * momentum.size, transcendentals=0
            ),
            compiler_params=params(50),
            name="update_pieces",
        )(place, notes, momentum, *[v.astype(F32) for v in values.values()], *outs)
    return tuple(outs)


def solution(mesh):
    return jax.shard_map(
        body,
        mesh=mesh,
        in_specs=(
            P("island", "expert", "tensor"),
            P("island", "expert", "tensor"),
            P("island", "expert", None, None),
            P("island", "expert", None),
            P("island", "expert", None, None),
            P("island", "expert", None, "tensor"),
            P("island", "expert", "tensor", None),
            P("island", "expert", None, "tensor"),
            P("expert", None, "tensor"),
        ),
        out_specs=(P("expert", None, "tensor"), P("expert", None, "tensor")),
        check_vma=False,
    )
```

```python
import functools
import math

import jax
import jax.numpy as jnp
from jax import lax
from jax.experimental import pallas as pl
from jax.experimental.pallas import tpu as pltpu
from jax.sharding import PartitionSpec as P

F32 = jnp.float32
BF16 = jnp.bfloat16
WIRE = jnp.float16
AXES = ("island", "expert", "tensor")

VMEM = pl.BlockSpec(memory_space=pltpu.VMEM)
SMEM = pl.BlockSpec(memory_space=pltpu.SMEM)
ANY = pl.BlockSpec(memory_space=pl.ANY)


def params(mib):
    return pltpu.CompilerParams(vmem_limit_bytes=mib << 20)


def partner(at, step, size):
    return at ^ step if size & (size - 1) == 0 else (at + step) % size


def origin(at, step, size):
    return at ^ step if size & (size - 1) == 0 else (at - step) % size


def swap(value, axis, step):
    size = lax.axis_size(axis)
    return lax.ppermute(value, axis, [(at, partner(at, step, size)) for at in range(size)])


def dot(a, b, contract):
    return lax.dot_general(a, b, (contract, ((), ())), preferred_element_type=F32)


def copy_all(sems, pairs):
    copies = [pltpu.make_async_copy(*pair, sems.at[n]) for n, pair in enumerate(pairs)]
    for copy in copies:
        copy.start()
    return copies


def pick_kernel(experts, spot, *refs):
    sources, outs = refs[:5], refs[5 : 5 + experts]
    table, count, weight, tokens, grads, sems = refs[5 + experts :]
    loads = copy_all(sems, list(zip(sources, refs[5 + experts : -1])))
    for copy in loads:
        copy.wait()
    slots = table.shape[-1]
    rows = lax.broadcasted_iota(jnp.int32, (slots, slots), 0)
    lanes = lax.broadcasted_iota(jnp.int32, (slots, slots), 1)

    def column(row):
        return jnp.sum(jnp.where(rows == lanes, row, 0), axis=1, keepdims=True)

    for d in range(experts):
        to = partner(spot[0], d, experts)
        live = lax.broadcasted_iota(jnp.int32, (slots, 1), 0) < count[0, 0, to]
        token = column(table[0, 0, pl.ds(to, 1), :].astype(F32)).astype(jnp.int32)
        chance = column(weight[0, 0, pl.ds(to, 1), :])
        ids = lax.broadcasted_iota(jnp.int32, (slots, tokens.shape[1]), 1)
        picks = jnp.where((ids == token) & live, 1.0, 0.0).astype(BF16)
        outs[d][:slots, :] = dot(picks, tokens[0], ((1,), (0,))).astype(BF16)
        chosen = dot(picks, grads[0], ((1,), (0,)))
        outs[d][slots:, :] = (chance * chosen).astype(BF16)


def cut_kernel(islands, pieces, spot, drift, *refs):
    *blocks, sems = refs
    rows, columns = blocks[0].shape
    pairs = []
    for d, first, count_rows, target, at_row in pieces:
        at = partner(spot[3], d, islands)
        top = pl.multiple_of(lax.div(at, spot[4]) * rows, rows) + first
        left = pl.multiple_of(lax.rem(at, spot[4]) * columns, columns)
        source = drift.at[0, 0, pl.ds(top, count_rows), pl.ds(left, columns)]
        pairs.append((source, blocks[target].at[pl.ds(at_row, count_rows)]))
    for copy in copy_all(sems, pairs):
        copy.wait()


def gather_kernel(count, *refs):
    arrived, joined = refs[:count], refs[count]
    slots = arrived[0].shape[0] // 2
    for n, piece in enumerate(arrived):
        joined[n * slots : (n + 1) * slots, :] = piece[:slots, :]
        joined[(count + n) * slots : (count + n + 1) * slots, :] = piece[slots:, :]


def join_kernel(blocks, joined, *refs):
    drifts, (turned, drift_sum) = refs[:blocks], refs[blocks : blocks + 2]
    rows = drift_sum.shape[0]
    for n, ref in enumerate(refs[blocks + 2 :]):
        ref[...] = drifts[1 + n][rows:, :]
    turned[...] = joined[: joined.shape[0] // 2, :].T
    added = drifts[0][...].astype(F32)
    for other in drifts[1:]:
        added = added + other[:rows, :].astype(F32)
    drift_sum[...] = added


def hidden_kernel(parts, across, spot, gate, down, *refs):
    joined, out, norms = refs[:parts], refs[parts], refs[-1]
    rows, half = joined[0].shape[0] // 2, joined[0].shape[1]
    columns = out.shape[2]
    starts = [pl.multiple_of(origin(spot[1], t, parts) * half, half) for t in range(parts)]
    hidden_gram = 0.0
    for r in range(across):
        first = r * columns
        value = 0.0
        back = 0.0
        for t in range(parts):
            block = gate[0, 0, pl.ds(starts[t], half), first : first + columns]
            value = value + dot(joined[t][:rows, :], block, ((1,), (0,)))
            block = down[0, 0, first : first + columns, pl.ds(starts[t], half)]
            back = back + dot(joined[t][rows:, :], block, ((1,), (1,)))
        rounded = (back * (value / (1.0 + jnp.exp(-value)))).astype(BF16)
        out[r] = rounded
        hidden_gram = hidden_gram + dot(rounded, rounded, ((1,), (1,)))
    input_gram = 0.0
    for t in range(parts):
        features = joined[t][:rows, :]
        input_gram = input_gram + dot(features, features, ((1,), (1,)))
    norms[...] = jnp.full(norms.shape, jnp.sum(hidden_gram * input_gram), F32)


def average_kernel(islands, entries, tiles, spot, norms, drift_sum, own, moved, *refs):
    messages = refs[:islands]
    scaled, notes, total, square = refs[islands:]
    rows = total.shape[0] // tiles
    slots = own.shape[2]
    group = norms.shape[0] // islands
    scales = []
    for d in range(islands):
        at = origin(spot[3], d, islands)
        norm = jnp.sum(norms[pl.ds(at * group, group)], axis=0)[:1, :1]
        scales.append(jnp.minimum(1.0, math.sqrt(entries) / jnp.sqrt(norm + 1e-06)) / islands)
    handed = [m for m in messages[:0:-1] if m.shape[0] > slots]

    def compute(features):
        squares = 0.0
        for m in range(tiles):
            part = slice(m * rows, (m + 1) * rows)
            average = drift_sum[part, :]
            if handed:
                size = handed[0].shape[0] - slots
                n, first = divmod(m * rows, size)
                first += slots
                average = average + handed[n][first : first + rows, :].astype(F32)
            average = average * (1.0 / islands)
            for d in range(islands):
                factor = messages[d][:slots, :]
                average = average + scales[d] * dot(features[d, part, :], factor, ((1,), (0,)))
            total[part, :] = average
            squares = squares + jnp.sum(average * average, axis=0, keepdims=True)
        square[...] = squares

    pl.when(spot[5] == 1)(lambda: compute(own))
    pl.when(spot[5] != 1)(lambda: compute(moved))
    peak = jnp.max(jnp.abs(total[...]))
    unit = jnp.maximum(peak, 1e-30) / 32768
    value = total[...] * (1 / unit)
    spread_out = value * 8193.0
    value = spread_out - (spread_out - value)
    scaled[...] = jnp.where(jnp.abs(value) < 2.0**-13, 0.0, value)
    sublane = lax.broadcasted_iota(jnp.int32, notes.shape, 1)
    notes[...] = jnp.where(sublane == 0, jnp.sum(square[...]), unit)


def hand_kernel(islands, tails, spot, norms, hidden, *refs):
    features, relays = refs[:islands], refs[islands : islands + len(tails)]
    joined, passed, *messages = refs[islands + len(tails) :]
    across, slots, _ = hidden.shape
    for n in range(islands):
        joined[n] = features[n][...]
    passed[...] = norms[...]
    for d, message in enumerate(messages):
        block = lax.rem(partner(spot[3], d, islands), across)
        message[:slots, :] = hidden[pl.ds(block, 1)][0]
        if d in tails:
            message[slots:, :] = relays[tails.index(d)][...]


def own_kernel(slots, block, slots_out, block_out):
    slots_out[...] = slots[...]
    block_out[...] = block[...]


def update_kernel(entries, pieces, place, notes, momentum, *refs):
    values = refs[: len(pieces)]
    new_momentum, outer_step, moved, step, in_sems, sems = refs[-6:]
    rows, columns = values[0].shape
    spots, loads = [], []
    for n, (d, first) in enumerate(pieces):
        top = pl.multiple_of(pl.multiple_of(place[3 * d], 32) + first, 32)
        left = pl.multiple_of(place[3 * d + 1], columns)
        spots.append((0, pl.ds(top, rows), pl.ds(left, columns)))
        loads.append(pltpu.make_async_copy(momentum.at[spots[n]], moved.at[n], in_sems.at[n]))
        loads[-1].start()
    square = jnp.sum(notes[...], axis=0)[:1, :1]
    clip = jnp.minimum(1.0, 0.25 * math.sqrt(entries) / jnp.sqrt(square + 1e-06))
    stored = []
    for n, (d, first) in enumerate(pieces):
        unit = notes[pl.ds(place[3 * d + 2], 1)][0, 1:2, :1]
        clipped = (clip * unit) * values[n][...]
        loads[n].wait()
        fresh = 0.9 * moved[n] + clipped
        moved[n] = fresh
        step[n] = (0.7 * (clipped + 0.9 * fresh)).astype(BF16)
        for k, (here, out) in enumerate(((moved, new_momentum), (step, outer_step))):
            stored.append(pltpu.make_async_copy(here.at[n], out.at[spots[n]], sems.at[n, k]))
            stored[-1].start()
    for copy in stored:
        copy.wait()


def body(
    tokens,
    token_grads,
    slot_token,
    slot_count,
    slot_prob,
    gate_weight,
    down_weight,
    drift,
    momentum,
):
    islands, experts, parts = (lax.axis_size(a) for a in AXES)
    island, expert, part = (lax.axis_index(a) for a in AXES)
    devices = islands * experts * parts
    features, hidden = gate_weight.shape[2:]
    half = features // parts
    across = islands // parts
    columns = hidden // across
    entries = features * hidden * experts * parts
    slots = slot_token.shape[3]
    routed_rows = experts * slots
    holder = island // across
    spot = jnp.stack(
        [expert, part, island % across, island, jnp.int32(across), (part == holder).astype(jnp.int32)]
    ).astype(jnp.int32)

    handed = half // 2 if islands == 4 else 0
    steps = [0, 1, 2] if handed else list(range(islands))
    pieces = [(d, 0, half, n, 0) for n, d in enumerate(steps)]
    if handed:
        pieces += [(3, 0, handed, 1, half), (3, handed, handed, 2, half)]
    block_rows = [half + (handed if d else 0) for d in steps]
    picked = pl.pallas_call(
        lambda *refs: pick_kernel(experts, *refs),
        in_specs=[SMEM] + [ANY] * 5,
        out_specs=[VMEM] * experts,
        out_shape=[jax.ShapeDtypeStruct((2 * slots, half), BF16)] * experts,
        scratch_shapes=[
            pltpu.VMEM(slot_token.shape, jnp.int32),
            pltpu.SMEM(slot_count.shape, jnp.int32),
            pltpu.VMEM(slot_prob.shape, F32),
            pltpu.VMEM(tokens.shape, BF16),
            pltpu.VMEM(token_grads.shape, BF16),
            pltpu.SemaphoreType.DMA((5,)),
        ],
        compiler_params=params(56),
        name="pick_slots",
    )(spot, slot_token, slot_count, slot_prob, tokens, token_grads)
    blocks = pl.pallas_call(
        lambda *refs: cut_kernel(islands, pieces, *refs),
        in_specs=[SMEM, ANY],
        out_specs=[VMEM] * len(steps),
        out_shape=[jax.ShapeDtypeStruct((rows, columns), BF16) for rows in block_rows],
        scratch_shapes=[pltpu.SemaphoreType.DMA((len(pieces),))],
        compiler_params=params(56),
        name="cut_drift",
    )(spot, drift)
    arrived = [picked[0]] + [swap(picked[d], "expert", d) for d in range(1, experts)]
    drift_in = [blocks[0]] + [swap(blocks[d], "island", d) for d in steps[1:]]
    arrived[0], drift_in[0] = pl.pallas_call(
        own_kernel,
        in_specs=[VMEM] * 2,
        out_specs=[VMEM] * 2,
        out_shape=[
            jax.ShapeDtypeStruct((2 * slots, half), BF16),
            jax.ShapeDtypeStruct((half, columns), BF16),
        ],
        compiler_params=params(6),
        name="own_parts",
    )(arrived[0], drift_in[0])
    joined = pl.pallas_call(
        lambda *refs: gather_kernel(experts, *refs),
        in_specs=[VMEM] * experts,
        out_specs=VMEM,
        out_shape=jax.ShapeDtypeStruct((2 * routed_rows, half), BF16),
        compiler_params=params(6 + routed_rows // 48),
        name="gather_slots",
    )(*arrived)
    turned, drift_sum, *relays = pl.pallas_call(
        lambda *refs: join_kernel(len(steps), *refs),
        in_specs=[VMEM] * (1 + len(steps)),
        out_specs=[VMEM] * (4 if handed else 2),
        out_shape=[
            jax.ShapeDtypeStruct((half, routed_rows), BF16),
            jax.ShapeDtypeStruct((half, columns), F32),
        ]
        + [jax.ShapeDtypeStruct((handed, columns), BF16)] * (2 if handed else 0),
        compiler_params=params(12 + routed_rows // 48),
        name="join_blocks",
    )(joined, *drift_in)

    joined_all = [joined] + [swap(joined, "tensor", t) for t in range(1, parts)]

    def send_features(d):
        pairs = []
        for at in range(islands):
            to = partner(at, d, islands)
            pairs.append((at * parts + to // across, to * parts + to // across))
        return lax.ppermute(turned, ("island", "tensor"), pairs)

    def spread(value):
        result = value
        for t in range(1, parts):
            pairs = []
            for at in range(islands):
                keep = at // across
                pairs.append((at * parts + keep, at * parts + partner(keep, t, parts)))
            moved = lax.ppermute(value, ("island", "tensor"), pairs)
            result = moved if t == 1 else result + moved
        return result

    features_in = [send_features(d) for d in range(1, islands)]

    hidden_out, norms = pl.pallas_call(
        lambda *refs: hidden_kernel(parts, across, *refs),
        in_specs=[SMEM] + [VMEM] * (2 + parts),
        out_specs=[VMEM] * 2,
        out_shape=[
            jax.ShapeDtypeStruct((across, routed_rows, columns), BF16),
            jax.ShapeDtypeStruct((devices, 8, 128), F32),
        ],
        compiler_params=params(16 + routed_rows // 48),
        name="hidden_grads",
    )(spot, gate_weight, down_weight, *joined_all)
    tails = [2, 1] if handed else []
    message_rows = [
        routed_rows + (half - handed if d in tails else 0) for d in range(islands)
    ]
    features_in, norms, *messages = pl.pallas_call(
        lambda *refs: hand_kernel(islands, tails, *refs),
        in_specs=[SMEM] + [VMEM] * (2 + islands + len(relays)),
        out_specs=[VMEM] * (2 + islands),
        out_shape=[
            jax.ShapeDtypeStruct((islands, half, routed_rows), BF16),
            jax.ShapeDtypeStruct(norms.shape, F32),
        ]
        + [jax.ShapeDtypeStruct((rows, columns), BF16) for rows in message_rows],
        compiler_params=params(6 + routed_rows // 48),
        name="hand_on",
    )(spot, norms, hidden_out, turned, *features_in, *relays)
    features_moved = spread(features_in)
    norms = lax.all_to_all(norms, AXES, split_axis=0, concat_axis=0, tiled=True)
    messages_in = [messages[0]] + [swap(messages[d], "island", d) for d in range(1, islands)]

    scaled, notes = pl.pallas_call(
        lambda *refs: average_kernel(islands, entries, 2, *refs),
        in_specs=[SMEM] + [VMEM] * (4 + islands),
        out_specs=[VMEM] * 2,
        out_shape=[
            jax.ShapeDtypeStruct((half, columns), F32),
            jax.ShapeDtypeStruct((devices, 8, 128), F32),
        ],
        scratch_shapes=[pltpu.VMEM((half, columns), F32), pltpu.VMEM((1, columns), F32)],
        compiler_params=params(8 + routed_rows // 48),
        name="average_block",
    )(spot, norms, drift_sum, features_in, features_moved, *messages_in)
    notes = lax.all_to_all(notes, AXES, split_axis=0, concat_axis=0, tiled=True)

    sent = scaled.astype(WIRE)
    values, last = {(0, 0): scaled}, {}
    steps = [1, 2] if handed else range(1, islands)
    for d in steps:
        values[d, 0] = swap(sent, "island", d)
    if handed:
        nothing = jnp.minimum(notes[0, 1, 0], 0.0).astype(WIRE)
        last[3, 0] = swap(values[1, 0][:handed] + nothing, "island", 2)
        last[3, handed] = swap(values[2, 0][handed:] + nothing, "island", 1)
    place = []
    for d in range(islands):
        at = origin(island, d, islands)
        source = (at * experts + expert) * parts + part
        place += [(at // across) * half, (at % across) * columns, source]
    place = jnp.stack(place).astype(jnp.int32)
    outs = []
    for values, cost in ((values, 12), (last, 3)):
        if not values:
            continue
        outs = pl.pallas_call(
            functools.partial(update_kernel, entries, list(values)),
            in_specs=[SMEM, VMEM, ANY] + [VMEM] * len(values) + [ANY] * len(outs),
            out_specs=[ANY, ANY],
            out_shape=[
                jax.ShapeDtypeStruct(momentum.shape, F32),
                jax.ShapeDtypeStruct(momentum.shape, BF16),
            ],
            scratch_shapes=[
                pltpu.VMEM((len(values), *next(iter(values.values())).shape), F32),
                pltpu.VMEM((len(values), *next(iter(values.values())).shape), BF16),
                pltpu.SemaphoreType.DMA((len(values),)),
                pltpu.SemaphoreType.DMA((len(values), 2)),
            ],
            input_output_aliases={3 + len(values) + n: n for n in range(len(outs))},
            cost_estimate=pl.CostEstimate(
                flops=0, bytes_accessed=cost * momentum.size, transcendentals=0
            ),
            compiler_params=params(50),
            name="update_pieces",
        )(place, notes, momentum, *[v.astype(F32) for v in values.values()], *outs)
    return tuple(outs)


def solution(mesh):
    return jax.shard_map(
        body,
        mesh=mesh,
        in_specs=(
            P("island", "expert", "tensor"),
            P("island", "expert", "tensor"),
            P("island", "expert", None, None),
            P("island", "expert", None),
            P("island", "expert", None, None),
            P("island", "expert", None, "tensor"),
            P("island", "expert", "tensor", None),
            P("island", "expert", None, "tensor"),
            P("expert", None, "tensor"),
        ),
        out_specs=(P("expert", None, "tensor"), P("expert", None, "tensor")),
        check_vma=False,
    )
```

```python
import functools
import math

import jax
import jax.numpy as jnp
from jax import lax
from jax.experimental import pallas as pl
from jax.experimental.pallas import tpu as pltpu
from jax.sharding import PartitionSpec as P

F32 = jnp.float32
BF16 = jnp.bfloat16
WIRE = jnp.float16
AXES = ("island", "expert", "tensor")

VMEM = pl.BlockSpec(memory_space=pltpu.VMEM)
SMEM = pl.BlockSpec(memory_space=pltpu.SMEM)
ANY = pl.BlockSpec(memory_space=pl.ANY)


def params(mib):
    return pltpu.CompilerParams(vmem_limit_bytes=mib << 20)


def partner(at, step, size):
    return at ^ step if size & (size - 1) == 0 else (at + step) % size


def origin(at, step, size):
    return at ^ step if size & (size - 1) == 0 else (at - step) % size


def swap(value, axis, step):
    size = lax.axis_size(axis)
    return lax.ppermute(value, axis, [(at, partner(at, step, size)) for at in range(size)])


def dot(a, b, contract):
    return lax.dot_general(a, b, (contract, ((), ())), preferred_element_type=F32)


def copy_all(sems, pairs):
    copies = [pltpu.make_async_copy(*pair, sems.at[n]) for n, pair in enumerate(pairs)]
    for copy in copies:
        copy.start()
    return copies


def pick_kernel(experts, spot, *refs):
    sources, outs = refs[:5], refs[5 : 5 + experts]
    table, count, weight, tokens, grads, sems = refs[5 + experts :]
    loads = copy_all(sems, list(zip(sources, refs[5 + experts : -1])))
    for copy in loads:
        copy.wait()
    slots = table.shape[-1]
    rows = lax.broadcasted_iota(jnp.int32, (slots, slots), 0)
    lanes = lax.broadcasted_iota(jnp.int32, (slots, slots), 1)

    def column(row):
        return jnp.sum(jnp.where(rows == lanes, row, 0), axis=1, keepdims=True)

    for d in range(experts):
        to = partner(spot[0], d, experts)
        live = lax.broadcasted_iota(jnp.int32, (slots, 1), 0) < count[0, 0, to]
        token = column(table[0, 0, pl.ds(to, 1), :].astype(F32)).astype(jnp.int32)
        chance = column(weight[0, 0, pl.ds(to, 1), :])
        ids = lax.broadcasted_iota(jnp.int32, (slots, tokens.shape[1]), 1)
        picks = jnp.where((ids == token) & live, 1.0, 0.0).astype(BF16)
        outs[d][:slots, :] = dot(picks, tokens[0], ((1,), (0,))).astype(BF16)
        chosen = dot(picks, grads[0], ((1,), (0,)))
        outs[d][slots:, :] = (chance * chosen).astype(BF16)


def cut_kernel(islands, pieces, spot, drift, *refs):
    *blocks, sems = refs
    rows, columns = blocks[0].shape
    pairs = []
    for d, first, count_rows, target, at_row in pieces:
        at = partner(spot[3], d, islands)
        top = pl.multiple_of(lax.div(at, spot[4]) * rows, rows) + first
        left = pl.multiple_of(lax.rem(at, spot[4]) * columns, columns)
        source = drift.at[0, 0, pl.ds(top, count_rows), pl.ds(left, columns)]
        pairs.append((source, blocks[target].at[pl.ds(at_row, count_rows)]))
    for copy in copy_all(sems, pairs):
        copy.wait()


def gather_kernel(count, *refs):
    arrived, joined = refs[:count], refs[count]
    slots = arrived[0].shape[0] // 2
    for n, piece in enumerate(arrived):
        joined[n * slots : (n + 1) * slots, :] = piece[:slots, :]
        joined[(count + n) * slots : (count + n + 1) * slots, :] = piece[slots:, :]


def join_kernel(blocks, joined, *refs):
    drifts, (turned, drift_sum) = refs[:blocks], refs[blocks : blocks + 2]
    rows = drift_sum.shape[0]
    for n, ref in enumerate(refs[blocks + 2 :]):
        ref[...] = drifts[1 + n][rows:, :]
    turned[...] = joined[: joined.shape[0] // 2, :].T
    added = drifts[0][...].astype(F32)
    for other in drifts[1:]:
        added = added + other[:rows, :].astype(F32)
    drift_sum[...] = added


def hidden_kernel(parts, islands, tails, spot, gate, down, *refs):
    joined, relays = refs[:parts], refs[parts : parts + len(tails)]
    *messages, norms, hidden = refs[parts + len(tails) :]
    across, slots, columns = hidden.shape
    half = joined[0].shape[1]
    starts = [pl.multiple_of(origin(spot[1], t, parts) * half, half) for t in range(parts)]
    hidden_gram = 0.0
    for r in range(across):
        first = r * columns
        value = 0.0
        back = 0.0
        for t in range(parts):
            block = gate[0, 0, pl.ds(starts[t], half), first : first + columns]
            value = value + dot(joined[t][:slots, :], block, ((1,), (0,)))
            block = down[0, 0, first : first + columns, pl.ds(starts[t], half)]
            back = back + dot(joined[t][slots:, :], block, ((1,), (1,)))
        rounded = (back * (value / (1.0 + jnp.exp(-value)))).astype(BF16)
        hidden[r] = rounded
        hidden_gram = hidden_gram + dot(rounded, rounded, ((1,), (1,)))
    for d, message in enumerate(messages):
        block = lax.rem(partner(spot[3], d, islands), across)
        message[:slots, :] = hidden[pl.ds(block, 1)][0]
        if d in tails:
            message[slots:, :] = relays[tails.index(d)][...]
    input_gram = 0.0
    for t in range(parts):
        features = joined[t][:slots, :]
        input_gram = input_gram + dot(features, features, ((1,), (1,)))
    norms[...] = jnp.full(norms.shape, jnp.sum(hidden_gram * input_gram), F32)


def average_kernel(islands, entries, tiles, count, spot, norms, drift_sum, *refs):
    features, messages = refs[:count], refs[count : count + islands]
    scaled, notes, total, square = refs[count + islands :]
    rows = total.shape[0] // tiles
    slots = features[0].shape[-1]
    group = norms.shape[0] // islands
    scales = []
    for d in range(islands):
        at = origin(spot[3], d, islands)
        norm = jnp.sum(norms[pl.ds(at * group, group)], axis=0)[:1, :1]
        scales.append(jnp.minimum(1.0, math.sqrt(entries) / jnp.sqrt(norm + 1e-06)) / islands)
    handed = [m for m in messages[:0:-1] if m.shape[0] > slots]

    def compute(blocks):
        squares = 0.0
        for m in range(tiles):
            part = slice(m * rows, (m + 1) * rows)
            average = drift_sum[part, :]
            if handed:
                size = handed[0].shape[0] - slots
                n, first = divmod(m * rows, size)
                first += slots
                average = average + handed[n][first : first + rows, :].astype(F32)
            average = average * (1.0 / islands)
            for d in range(islands):
                size = total.shape[0] // len(blocks[d])
                n, first = divmod(m * rows, size)
                ref, *lead = blocks[d][n]
                block = ref[(*lead, slice(first, first + rows), slice(None))]
                average = average + scales[d] * dot(block, messages[d][:slots, :], ((1,), (0,)))
            total[part, :] = average
            squares = squares + jnp.sum(average * average, axis=0, keepdims=True)
        square[...] = squares

    if len(features[0].shape) == 2:
        compute([[(ref,)] for ref in features])
    else:
        pair, moved, *halves = features
        held = [[(pair, 0)], [(pair, 1)]]
        others = [[(moved,)], [(ref,) for ref in halves]]
        pl.when(spot[5] == 1)(lambda: compute(held + others))
        pl.when(spot[5] != 1)(lambda: compute(others + held))
    peak = jnp.max(jnp.abs(total[...]))
    unit = jnp.maximum(peak, 1e-30) / 32768
    value = total[...] * (1 / unit)
    spread_out = value * 8193.0
    value = spread_out - (spread_out - value)
    scaled[...] = jnp.where(jnp.abs(value) < 2.0**-13, 0.0, value)
    sublane = lax.broadcasted_iota(jnp.int32, notes.shape, 1)
    notes[...] = jnp.where(sublane == 0, jnp.sum(square[...]), unit)


def choose_kernel(spot, norms, turned, first, chosen, passed):
    chosen[...] = jnp.where(spot[5] == 1, turned[...], first[...])
    passed[...] = first[...]


def hold_kernel(spot, norms, turned, first, second, earlier, pair, top, bottom, passed):
    holder = spot[5] == 1
    size = top.shape[0]
    pair[0] = jnp.where(holder, turned[...], first[...])
    pair[1] = jnp.where(holder, first[...], second[...])
    top[...] = pair[1, :size, :]
    bottom[...] = pair[1, size:, :]
    passed[...] = norms[...]


def own_kernel(slots, block, slots_out, block_out):
    slots_out[...] = slots[...]
    block_out[...] = block[...]


def update_kernel(entries, pieces, place, notes, momentum, *refs):
    values = refs[: len(pieces)]
    new_momentum, outer_step, moved, step, in_sems, sems = refs[-6:]
    rows, columns = values[0].shape
    spots, loads = [], []
    for n, (d, first) in enumerate(pieces):
        top = pl.multiple_of(pl.multiple_of(place[3 * d], 32) + first, 32)
        left = pl.multiple_of(place[3 * d + 1], columns)
        spots.append((0, pl.ds(top, rows), pl.ds(left, columns)))
        loads.append(pltpu.make_async_copy(momentum.at[spots[n]], moved.at[n], in_sems.at[n]))
        loads[-1].start()
    square = jnp.sum(notes[...], axis=0)[:1, :1]
    clip = jnp.minimum(1.0, 0.25 * math.sqrt(entries) / jnp.sqrt(square + 1e-06))
    stored = []
    for n, (d, first) in enumerate(pieces):
        unit = notes[pl.ds(place[3 * d + 2], 1)][0, 1:2, :1]
        clipped = (clip * unit) * values[n][...]
        loads[n].wait()
        fresh = 0.9 * moved[n] + clipped
        moved[n] = fresh
        step[n] = (0.7 * (clipped + 0.9 * fresh)).astype(BF16)
        for k, (here, out) in enumerate(((moved, new_momentum), (step, outer_step))):
            stored.append(pltpu.make_async_copy(here.at[n], out.at[spots[n]], sems.at[n, k]))
            stored[-1].start()
    for copy in stored:
        copy.wait()


def body(
    tokens,
    token_grads,
    slot_token,
    slot_count,
    slot_prob,
    gate_weight,
    down_weight,
    drift,
    momentum,
):
    islands, experts, parts = (lax.axis_size(a) for a in AXES)
    island, expert, part = (lax.axis_index(a) for a in AXES)
    devices = islands * experts * parts
    features, hidden = gate_weight.shape[2:]
    half = features // parts
    across = islands // parts
    columns = hidden // across
    entries = features * hidden * experts * parts
    slots = slot_token.shape[3]
    routed_rows = experts * slots
    holder = island // across
    spot = jnp.stack(
        [expert, part, island % across, island, jnp.int32(across), (part == holder).astype(jnp.int32)]
    ).astype(jnp.int32)

    handed = half // 2 if islands == 4 else 0
    steps = [0, 1, 2] if handed else list(range(islands))
    pieces = [(d, 0, half, n, 0) for n, d in enumerate(steps)]
    if handed:
        pieces += [(3, 0, handed, 1, half), (3, handed, handed, 2, half)]
    block_rows = [half + (handed if d else 0) for d in steps]
    picked = pl.pallas_call(
        lambda *refs: pick_kernel(experts, *refs),
        in_specs=[SMEM] + [ANY] * 5,
        out_specs=[VMEM] * experts,
        out_shape=[jax.ShapeDtypeStruct((2 * slots, half), BF16)] * experts,
        scratch_shapes=[
            pltpu.VMEM(slot_token.shape, jnp.int32),
            pltpu.SMEM(slot_count.shape, jnp.int32),
            pltpu.VMEM(slot_prob.shape, F32),
            pltpu.VMEM(tokens.shape, BF16),
            pltpu.VMEM(token_grads.shape, BF16),
            pltpu.SemaphoreType.DMA((5,)),
        ],
        compiler_params=params(56),
        name="pick_slots",
    )(spot, slot_token, slot_count, slot_prob, tokens, token_grads)
    blocks = pl.pallas_call(
        lambda *refs: cut_kernel(islands, pieces, *refs),
        in_specs=[SMEM, ANY],
        out_specs=[VMEM] * len(steps),
        out_shape=[jax.ShapeDtypeStruct((rows, columns), BF16) for rows in block_rows],
        scratch_shapes=[pltpu.SemaphoreType.DMA((len(pieces),))],
        compiler_params=params(56),
        name="cut_drift",
    )(spot, drift)
    arrived = [picked[0]] + [swap(picked[d], "expert", d) for d in range(1, experts)]
    drift_in = [blocks[0]] + [swap(blocks[d], "island", d) for d in steps[1:]]
    arrived[0], drift_in[0] = pl.pallas_call(
        own_kernel,
        in_specs=[VMEM] * 2,
        out_specs=[VMEM] * 2,
        out_shape=[
            jax.ShapeDtypeStruct((2 * slots, half), BF16),
            jax.ShapeDtypeStruct((half, columns), BF16),
        ],
        compiler_params=params(6),
        name="own_parts",
    )(arrived[0], drift_in[0])
    joined = pl.pallas_call(
        lambda *refs: gather_kernel(experts, *refs),
        in_specs=[VMEM] * experts,
        out_specs=VMEM,
        out_shape=jax.ShapeDtypeStruct((2 * routed_rows, half), BF16),
        compiler_params=params(6 + routed_rows // 48),
        name="gather_slots",
    )(*arrived)
    turned, drift_sum, *relays = pl.pallas_call(
        lambda *refs: join_kernel(len(steps), *refs),
        in_specs=[VMEM] * (1 + len(steps)),
        out_specs=[VMEM] * (4 if handed else 2),
        out_shape=[
            jax.ShapeDtypeStruct((half, routed_rows), BF16),
            jax.ShapeDtypeStruct((half, columns), F32),
        ]
        + [jax.ShapeDtypeStruct((handed, columns), BF16)] * (2 if handed else 0),
        compiler_params=params(12 + routed_rows // 48),
        name="join_blocks",
    )(joined, *drift_in)

    joined_all = [joined] + [swap(joined, "tensor", t) for t in range(1, parts)]

    tails = [2, 1] if handed else []
    message_rows = [routed_rows + (half - handed if d in tails else 0) for d in range(islands)]
    *messages, norms = pl.pallas_call(
        lambda *refs: hidden_kernel(parts, islands, tails, *refs),
        in_specs=[SMEM] + [VMEM] * (2 + parts + len(tails)),
        out_specs=[VMEM] * (islands + 1),
        out_shape=[jax.ShapeDtypeStruct((rows, columns), BF16) for rows in message_rows]
        + [jax.ShapeDtypeStruct((devices, 8, 128), F32)],
        scratch_shapes=[pltpu.VMEM((across, routed_rows, columns), BF16)],
        compiler_params=params(18 + routed_rows // 48),
        name="hidden_grads",
    )(spot, gate_weight, down_weight, *joined_all, *relays)
    messages_in = [messages[0]] + [swap(messages[d], "island", d) for d in range(1, islands)]

    if handed and parts == 2:
        pairs, onward = [], []
        for at in range(islands):
            keep = at // across
            pairs += [
                (at * parts + keep, (at ^ 1) * parts + keep),
                (at * parts + 1 - keep, (at ^ 2) * parts + keep),
            ]
            onward.append((at * parts + 1 - keep, (at ^ 1) * parts + 1 - keep))
        first = lax.ppermute(turned, ("island", "tensor"), pairs)
        block = jax.ShapeDtypeStruct((half, routed_rows), BF16)
        half_block = jax.ShapeDtypeStruct((half // 2, routed_rows), BF16)
        chosen, first = pl.pallas_call(
            choose_kernel,
            in_specs=[SMEM, ANY] + [VMEM] * 2,
            out_specs=[VMEM] * 2,
            out_shape=[block] * 2,
            compiler_params=params(4 + routed_rows // 48),
            name="choose_features",
        )(spot, norms, turned, first)
        second = lax.ppermute(first, ("island", "tensor"), onward)
        moved = swap(chosen, "tensor", 1)
        pair, *halves, norms = pl.pallas_call(
            hold_kernel,
            in_specs=[SMEM] + [VMEM] * 4 + [ANY],
            out_specs=[VMEM] * 4,
            out_shape=[
                jax.ShapeDtypeStruct((2, half, routed_rows), BF16),
                half_block,
                half_block,
                jax.ShapeDtypeStruct(norms.shape, F32),
            ],
            compiler_params=params(4 + routed_rows // 48),
            name="hold_features",
        )(spot, norms, turned, first, second, moved)
        features_of = [pair, moved] + [swap(v, "tensor", 1) for v in halves]
    else:
        every = lax.all_gather(turned, ("island", "tensor"))
        features_of = [every[origin(island, d, islands) * parts + holder] for d in range(islands)]
    norms = lax.all_to_all(norms, AXES, split_axis=0, concat_axis=0, tiled=True)

    scaled, notes = pl.pallas_call(
        lambda *refs: average_kernel(islands, entries, 2, len(features_of), *refs),
        in_specs=[SMEM] + [VMEM] * (2 + len(features_of) + islands),
        out_specs=[VMEM] * 2,
        out_shape=[
            jax.ShapeDtypeStruct((half, columns), F32),
            jax.ShapeDtypeStruct((devices, 8, 128), F32),
        ],
        scratch_shapes=[pltpu.VMEM((half, columns), F32), pltpu.VMEM((1, columns), F32)],
        compiler_params=params(8 + routed_rows // 48),
        name="average_block",
    )(spot, norms, drift_sum, *features_of, *messages_in)
    notes = lax.all_to_all(notes, AXES, split_axis=0, concat_axis=0, tiled=True)

    sent = scaled.astype(WIRE)
    values, last = {(0, 0): scaled}, {}
    steps = [1, 2] if handed else range(1, islands)
    for d in steps:
        values[d, 0] = swap(sent, "island", d)
    if handed:
        nothing = jnp.minimum(notes[0, 1, 0], 0.0).astype(WIRE)
        last[3, 0] = swap(values[1, 0][:handed] + nothing, "island", 2)
        last[3, handed] = swap(values[2, 0][handed:] + nothing, "island", 1)
    place = []
    for d in range(islands):
        at = origin(island, d, islands)
        source = (at * experts + expert) * parts + part
        place += [(at // across) * half, (at % across) * columns, source]
    place = jnp.stack(place).astype(jnp.int32)
    outs = []
    for values, cost in ((values, 12), (last, 3)):
        if not values:
            continue
        outs = pl.pallas_call(
            functools.partial(update_kernel, entries, list(values)),
            in_specs=[SMEM, VMEM, ANY] + [VMEM] * len(values) + [ANY] * len(outs),
            out_specs=[ANY, ANY],
            out_shape=[
                jax.ShapeDtypeStruct(momentum.shape, F32),
                jax.ShapeDtypeStruct(momentum.shape, BF16),
            ],
            scratch_shapes=[
                pltpu.VMEM((len(values), *next(iter(values.values())).shape), F32),
                pltpu.VMEM((len(values), *next(iter(values.values())).shape), BF16),
                pltpu.SemaphoreType.DMA((len(values),)),
                pltpu.SemaphoreType.DMA((len(values), 2)),
            ],
            input_output_aliases={3 + len(values) + n: n for n in range(len(outs))},
            cost_estimate=pl.CostEstimate(
                flops=0, bytes_accessed=cost * momentum.size, transcendentals=0
            ),
            compiler_params=params(50),
            name="update_pieces",
        )(place, notes, momentum, *[v.astype(F32) for v in values.values()], *outs)
    return tuple(outs)


def solution(mesh):
    return jax.shard_map(
        body,
        mesh=mesh,
        in_specs=(
            P("island", "expert", "tensor"),
            P("island", "expert", "tensor"),
            P("island", "expert", None, None),
            P("island", "expert", None),
            P("island", "expert", None, None),
            P("island", "expert", None, "tensor"),
            P("island", "expert", "tensor", None),
            P("island", "expert", None, "tensor"),
            P("expert", None, "tensor"),
        ),
        out_specs=(P("expert", None, "tensor"), P("expert", None, "tensor")),
        check_vma=False,
    )
```

```python
import functools
import math

import jax
import jax.numpy as jnp
from jax import lax
from jax.experimental import pallas as pl
from jax.experimental.pallas import tpu as pltpu
from jax.sharding import PartitionSpec as P

F32 = jnp.float32
BF16 = jnp.bfloat16
WIRE = jnp.float16
AXES = ("island", "expert", "tensor")

VMEM = pl.BlockSpec(memory_space=pltpu.VMEM)
SMEM = pl.BlockSpec(memory_space=pltpu.SMEM)
ANY = pl.BlockSpec(memory_space=pl.ANY)


def params(mib):
    return pltpu.CompilerParams(vmem_limit_bytes=mib << 20)


def partner(at, step, size):
    return at ^ step if size & (size - 1) == 0 else (at + step) % size


def origin(at, step, size):
    return at ^ step if size & (size - 1) == 0 else (at - step) % size


def swap(value, axis, step):
    size = lax.axis_size(axis)
    return lax.ppermute(value, axis, [(at, partner(at, step, size)) for at in range(size)])


def dot(a, b, contract):
    return lax.dot_general(a, b, (contract, ((), ())), preferred_element_type=F32)


def copy_all(sems, pairs):
    copies = [pltpu.make_async_copy(*pair, sems.at[n]) for n, pair in enumerate(pairs)]
    for copy in copies:
        copy.start()
    return copies


def pick_kernel(experts, spot, *refs):
    sources, outs = refs[:5], refs[5 : 5 + experts]
    table, count, weight, tokens, grads, sems = refs[5 + experts :]
    loads = copy_all(sems, list(zip(sources, refs[5 + experts : -1])))
    for copy in loads:
        copy.wait()
    slots = table.shape[-1]
    rows = lax.broadcasted_iota(jnp.int32, (slots, slots), 0)
    lanes = lax.broadcasted_iota(jnp.int32, (slots, slots), 1)

    def column(row):
        return jnp.sum(jnp.where(rows == lanes, row, 0), axis=1, keepdims=True)

    for d in range(experts):
        to = partner(spot[0], d, experts)
        live = lax.broadcasted_iota(jnp.int32, (slots, 1), 0) < count[0, 0, to]
        token = column(table[0, 0, pl.ds(to, 1), :].astype(F32)).astype(jnp.int32)
        chance = column(weight[0, 0, pl.ds(to, 1), :])
        ids = lax.broadcasted_iota(jnp.int32, (slots, tokens.shape[1]), 1)
        picks = jnp.where((ids == token) & live, 1.0, 0.0).astype(BF16)
        outs[d][:slots, :] = dot(picks, tokens[0], ((1,), (0,))).astype(BF16)
        chosen = dot(picks, grads[0], ((1,), (0,)))
        outs[d][slots:, :] = (chance * chosen).astype(BF16)


def cut_kernel(islands, pieces, spot, drift, *blocks):
    rows, columns = blocks[0].shape
    for d, first, count_rows, target, at_row in pieces:
        at = partner(spot[3], d, islands)
        top = pl.multiple_of(lax.div(at, spot[4]) * rows + first, 32)
        left = pl.multiple_of(lax.rem(at, spot[4]) * columns, columns)
        source = drift[0, 0, pl.ds(top, count_rows), pl.ds(left, columns)]
        blocks[target][at_row : at_row + count_rows, :] = source


def gather_kernel(count, *refs):
    arrived, joined = refs[:count], refs[count]
    slots = arrived[0].shape[0] // 2
    for n, piece in enumerate(arrived):
        joined[n * slots : (n + 1) * slots, :] = piece[:slots, :]
        joined[(count + n) * slots : (count + n + 1) * slots, :] = piece[slots:, :]


def join_kernel(blocks, joined, *refs):
    drifts, (turned, drift_sum) = refs[:blocks], refs[blocks : blocks + 2]
    rows = drift_sum.shape[0]
    for n, ref in enumerate(refs[blocks + 2 :]):
        ref[...] = drifts[1 + n][rows:, :]
    turned[...] = joined[: joined.shape[0] // 2, :].T
    added = drifts[0][...].astype(F32)
    for other in drifts[1:]:
        added = added + other[:rows, :].astype(F32)
    drift_sum[...] = added


def hidden_kernel(parts, across, spot, gate, down, *refs):
    joined, out, norms = refs[:parts], refs[parts], refs[-1]
    rows, half = joined[0].shape[0] // 2, joined[0].shape[1]
    columns = out.shape[2]
    starts = [pl.multiple_of(origin(spot[1], t, parts) * half, half) for t in range(parts)]
    hidden_gram = 0.0
    for r in range(across):
        first = r * columns
        value = 0.0
        back = 0.0
        for t in range(parts):
            block = gate[0, 0, pl.ds(starts[t], half), first : first + columns]
            value = value + dot(joined[t][:rows, :], block, ((1,), (0,)))
            block = down[0, 0, first : first + columns, pl.ds(starts[t], half)]
            back = back + dot(joined[t][rows:, :], block, ((1,), (1,)))
        rounded = (back * (value / (1.0 + jnp.exp(-value)))).astype(BF16)
        out[r] = rounded
        hidden_gram = hidden_gram + dot(rounded, rounded, ((1,), (1,)))
    input_gram = 0.0
    for t in range(parts):
        features = joined[t][:rows, :]
        input_gram = input_gram + dot(features, features, ((1,), (1,)))
    norms[...] = jnp.full(norms.shape, jnp.sum(hidden_gram * input_gram), F32)


def average_kernel(islands, entries, tiles, spot, norms, drift_sum, own, moved, *refs):
    messages = refs[:islands]
    scaled, notes, total, square = refs[islands:]
    rows = total.shape[0] // tiles
    slots = own.shape[2]
    group = norms.shape[0] // islands
    scales = []
    for d in range(islands):
        at = origin(spot[3], d, islands)
        norm = jnp.sum(norms[pl.ds(at * group, group)], axis=0)[:1, :1]
        scales.append(jnp.minimum(1.0, math.sqrt(entries) / jnp.sqrt(norm + 1e-06)) / islands)
    handed = [m for m in messages[:0:-1] if m.shape[0] > slots]

    def compute(features):
        squares = 0.0
        for m in range(tiles):
            part = slice(m * rows, (m + 1) * rows)
            average = drift_sum[part, :]
            if handed:
                size = handed[0].shape[0] - slots
                n, first = divmod(m * rows, size)
                first += slots
                average = average + handed[n][first : first + rows, :].astype(F32)
            average = average * (1.0 / islands)
            for d in range(islands):
                factor = messages[d][:slots, :]
                average = average + scales[d] * dot(features[d, part, :], factor, ((1,), (0,)))
            total[part, :] = average
            squares = squares + jnp.sum(average * average, axis=0, keepdims=True)
        square[...] = squares

    pl.when(spot[5] == 1)(lambda: compute(own))
    pl.when(spot[5] != 1)(lambda: compute(moved))
    peak = jnp.max(jnp.abs(total[...]))
    unit = jnp.maximum(peak, 1e-30) / 32768
    value = total[...] * (1 / unit)
    spread_out = value * 8193.0
    value = spread_out - (spread_out - value)
    scaled[...] = jnp.where(jnp.abs(value) < 2.0**-13, 0.0, value)
    sublane = lax.broadcasted_iota(jnp.int32, notes.shape, 1)
    notes[...] = jnp.where(sublane == 0, jnp.sum(square[...]), unit)


def hand_kernel(islands, tails, spot, norms, hidden, *refs):
    features, relays = refs[:islands], refs[islands : islands + len(tails)]
    joined, passed, *messages = refs[islands + len(tails) :]
    across, slots, _ = hidden.shape
    for n in range(islands):
        joined[n] = features[n][...]
    passed[...] = norms[...]
    for d, message in enumerate(messages):
        block = lax.rem(partner(spot[3], d, islands), across)
        message[:slots, :] = hidden[pl.ds(block, 1)][0]
        if d in tails:
            message[slots:, :] = relays[tails.index(d)][...]


def own_kernel(slots, block, slots_out, block_out):
    slots_out[...] = slots[...]
    block_out[...] = block[...]


def update_kernel(entries, pieces, cuts, place, notes, momentum, *refs):
    values = refs[: len(pieces)]
    new_momentum, outer_step, moved, step, in_sems, sems = refs[-6:]
    rows, columns = values[0].shape
    size = rows // cuts
    parts = [(n, m) for n in range(len(pieces)) for m in range(cuts)]
    spots, loads = [], []
    for i, (n, m) in enumerate(parts):
        d, first = pieces[n]
        top = pl.multiple_of(pl.multiple_of(place[3 * d], 32) + first + m * size, 32)
        left = pl.multiple_of(place[3 * d + 1], columns)
        spots.append((0, pl.ds(top, size), pl.ds(left, columns)))
        here = moved.at[n, pl.ds(m * size, size)]
        loads.append(pltpu.make_async_copy(momentum.at[spots[i]], here, in_sems.at[i]))
        loads[-1].start()
    square = jnp.sum(notes[...], axis=0)[:1, :1]
    clip = jnp.minimum(1.0, 0.25 * math.sqrt(entries) / jnp.sqrt(square + 1e-06))
    stored = []
    for i, (n, m) in enumerate(parts):
        unit = notes[pl.ds(place[3 * pieces[n][0] + 2], 1)][0, 1:2, :1]
        here = slice(m * size, (m + 1) * size)
        clipped = (clip * unit) * values[n][here, :]
        loads[i].wait()
        fresh = 0.9 * moved[n, here, :] + clipped
        moved[n, here, :] = fresh
        step[n, here, :] = (0.7 * (clipped + 0.9 * fresh)).astype(BF16)
        for k, (held, out) in enumerate(((moved, new_momentum), (step, outer_step))):
            held = held.at[n, pl.ds(m * size, size)]
            stored.append(pltpu.make_async_copy(held, out.at[spots[i]], sems.at[i, k]))
            stored[-1].start()
    for copy in stored:
        copy.wait()


def body(
    tokens,
    token_grads,
    slot_token,
    slot_count,
    slot_prob,
    gate_weight,
    down_weight,
    drift,
    momentum,
):
    islands, experts, parts = (lax.axis_size(a) for a in AXES)
    island, expert, part = (lax.axis_index(a) for a in AXES)
    devices = islands * experts * parts
    features, hidden = gate_weight.shape[2:]
    half = features // parts
    across = islands // parts
    columns = hidden // across
    entries = features * hidden * experts * parts
    slots = slot_token.shape[3]
    routed_rows = experts * slots
    holder = island // across
    spot = jnp.stack(
        [expert, part, island % across, island, jnp.int32(across), (part == holder).astype(jnp.int32)]
    ).astype(jnp.int32)

    handed = half // 2 if islands == 4 else 0
    steps = [0, 1, 2] if handed else list(range(islands))
    pieces = [(d, 0, half, n, 0) for n, d in enumerate(steps)]
    if handed:
        pieces += [(3, 0, handed, 1, half), (3, handed, handed, 2, half)]
    block_rows = [half + (handed if d else 0) for d in steps]
    picked = pl.pallas_call(
        lambda *refs: pick_kernel(experts, *refs),
        in_specs=[SMEM] + [ANY] * 5,
        out_specs=[VMEM] * experts,
        out_shape=[jax.ShapeDtypeStruct((2 * slots, half), BF16)] * experts,
        scratch_shapes=[
            pltpu.VMEM(slot_token.shape, jnp.int32),
            pltpu.SMEM(slot_count.shape, jnp.int32),
            pltpu.VMEM(slot_prob.shape, F32),
            pltpu.VMEM(tokens.shape, BF16),
            pltpu.VMEM(token_grads.shape, BF16),
            pltpu.SemaphoreType.DMA((5,)),
        ],
        compiler_params=params(56),
        name="pick_slots",
    )(spot, slot_token, slot_count, slot_prob, tokens, token_grads)
    blocks = pl.pallas_call(
        lambda *refs: cut_kernel(islands, pieces, *refs),
        in_specs=[SMEM, VMEM],
        out_specs=[VMEM] * len(steps),
        out_shape=[jax.ShapeDtypeStruct((rows, columns), BF16) for rows in block_rows],
        compiler_params=params(16),
        name="cut_drift",
    )(spot, drift)
    arrived = [picked[0]] + [swap(picked[d], "expert", d) for d in range(1, experts)]
    drift_in = [blocks[0]] + [swap(blocks[d], "island", d) for d in steps[1:]]
    arrived[0], drift_in[0] = pl.pallas_call(
        own_kernel,
        in_specs=[VMEM] * 2,
        out_specs=[VMEM] * 2,
        out_shape=[
            jax.ShapeDtypeStruct((2 * slots, half), BF16),
            jax.ShapeDtypeStruct((half, columns), BF16),
        ],
        compiler_params=params(6),
        name="own_parts",
    )(arrived[0], drift_in[0])
    joined = pl.pallas_call(
        lambda *refs: gather_kernel(experts, *refs),
        in_specs=[VMEM] * experts,
        out_specs=VMEM,
        out_shape=jax.ShapeDtypeStruct((2 * routed_rows, half), BF16),
        compiler_params=params(6 + routed_rows // 48),
        name="gather_slots",
    )(*arrived)
    turned, drift_sum, *relays = pl.pallas_call(
        lambda *refs: join_kernel(len(steps), *refs),
        in_specs=[VMEM] * (1 + len(steps)),
        out_specs=[VMEM] * (4 if handed else 2),
        out_shape=[
            jax.ShapeDtypeStruct((half, routed_rows), BF16),
            jax.ShapeDtypeStruct((half, columns), F32),
        ]
        + [jax.ShapeDtypeStruct((handed, columns), BF16)] * (2 if handed else 0),
        compiler_params=params(12 + routed_rows // 48),
        name="join_blocks",
    )(joined, *drift_in)

    joined_all = [joined] + [swap(joined, "tensor", t) for t in range(1, parts)]

    def send_features(d):
        pairs = []
        for at in range(islands):
            to = partner(at, d, islands)
            pairs.append((at * parts + to // across, to * parts + to // across))
        return lax.ppermute(turned, ("island", "tensor"), pairs)

    def spread(value):
        result = value
        for t in range(1, parts):
            pairs = []
            for at in range(islands):
                keep = at // across
                pairs.append((at * parts + keep, at * parts + partner(keep, t, parts)))
            moved = lax.ppermute(value, ("island", "tensor"), pairs)
            result = moved if t == 1 else result + moved
        return result

    features_in = [send_features(d) for d in range(1, islands)]

    hidden_out, norms = pl.pallas_call(
        lambda *refs: hidden_kernel(parts, across, *refs),
        in_specs=[SMEM] + [VMEM] * (2 + parts),
        out_specs=[VMEM] * 2,
        out_shape=[
            jax.ShapeDtypeStruct((across, routed_rows, columns), BF16),
            jax.ShapeDtypeStruct((devices, 8, 128), F32),
        ],
        compiler_params=params(16 + routed_rows // 48),
        name="hidden_grads",
    )(spot, gate_weight, down_weight, *joined_all)
    tails = [2, 1] if handed else []
    message_rows = [
        routed_rows + (half - handed if d in tails else 0) for d in range(islands)
    ]
    features_in, norms, *messages = pl.pallas_call(
        lambda *refs: hand_kernel(islands, tails, *refs),
        in_specs=[SMEM] + [VMEM] * (2 + islands + len(relays)),
        out_specs=[VMEM] * (2 + islands),
        out_shape=[
            jax.ShapeDtypeStruct((islands, half, routed_rows), BF16),
            jax.ShapeDtypeStruct(norms.shape, F32),
        ]
        + [jax.ShapeDtypeStruct((rows, columns), BF16) for rows in message_rows],
        compiler_params=params(6 + routed_rows // 48),
        name="hand_on",
    )(spot, norms, hidden_out, turned, *features_in, *relays)
    features_moved = spread(features_in)
    norms = lax.all_to_all(norms, AXES, split_axis=0, concat_axis=0, tiled=True)
    messages_in = [messages[0]] + [swap(messages[d], "island", d) for d in range(1, islands)]

    scaled, notes = pl.pallas_call(
        lambda *refs: average_kernel(islands, entries, 2, *refs),
        in_specs=[SMEM] + [VMEM] * (4 + islands),
        out_specs=[VMEM] * 2,
        out_shape=[
            jax.ShapeDtypeStruct((half, columns), F32),
            jax.ShapeDtypeStruct((devices, 8, 128), F32),
        ],
        scratch_shapes=[pltpu.VMEM((half, columns), F32), pltpu.VMEM((1, columns), F32)],
        compiler_params=params(8 + routed_rows // 48),
        name="average_block",
    )(spot, norms, drift_sum, features_in, features_moved, *messages_in)
    notes = lax.all_to_all(notes, AXES, split_axis=0, concat_axis=0, tiled=True)

    sent = scaled.astype(WIRE)
    values, last = {(0, 0): scaled}, {}
    steps = [1, 2] if handed else range(1, islands)
    for d in steps:
        values[d, 0] = swap(sent, "island", d)
    if handed:
        nothing = jnp.minimum(notes[0, 1, 0], 0.0).astype(WIRE)
        last[3, 0] = swap(values[1, 0][:handed] + nothing, "island", 2)
        last[3, handed] = swap(values[2, 0][handed:] + nothing, "island", 1)
    place = []
    for d in range(islands):
        at = origin(island, d, islands)
        source = (at * experts + expert) * parts + part
        place += [(at // across) * half, (at % across) * columns, source]
    place = jnp.stack(place).astype(jnp.int32)
    outs = []
    for values, cost, cuts in ((values, 12, 2), (last, 3, 2)):
        if not values:
            continue
        outs = pl.pallas_call(
            functools.partial(update_kernel, entries, list(values), cuts),
            in_specs=[SMEM, VMEM, ANY] + [VMEM] * len(values) + [ANY] * len(outs),
            out_specs=[ANY, ANY],
            out_shape=[
                jax.ShapeDtypeStruct(momentum.shape, F32),
                jax.ShapeDtypeStruct(momentum.shape, BF16),
            ],
            scratch_shapes=[
                pltpu.VMEM((len(values), *next(iter(values.values())).shape), F32),
                pltpu.VMEM((len(values), *next(iter(values.values())).shape), BF16),
                pltpu.SemaphoreType.DMA((len(values) * cuts,)),
                pltpu.SemaphoreType.DMA((len(values) * cuts, 2)),
            ],
            input_output_aliases={3 + len(values) + n: n for n in range(len(outs))},
            cost_estimate=pl.CostEstimate(
                flops=0, bytes_accessed=cost * momentum.size, transcendentals=0
            ),
            compiler_params=params(50),
            name="update_pieces",
        )(place, notes, momentum, *[v.astype(F32) for v in values.values()], *outs)
    return tuple(outs)


def solution(mesh):
    return jax.shard_map(
        body,
        mesh=mesh,
        in_specs=(
            P("island", "expert", "tensor"),
            P("island", "expert", "tensor"),
            P("island", "expert", None, None),
            P("island", "expert", None),
            P("island", "expert", None, None),
            P("island", "expert", None, "tensor"),
            P("island", "expert", "tensor", None),
            P("island", "expert", None, "tensor"),
            P("expert", None, "tensor"),
        ),
        out_specs=(P("expert", None, "tensor"), P("expert", None, "tensor")),
        check_vma=False,
    )
```

```python
import functools
import math

import jax
import jax.numpy as jnp
from jax import lax
from jax.experimental import pallas as pl
from jax.experimental.pallas import tpu as pltpu
from jax.sharding import PartitionSpec as P

F32 = jnp.float32
BF16 = jnp.bfloat16
WIRE = jnp.float16
AXES = ("island", "expert", "tensor")

VMEM = pl.BlockSpec(memory_space=pltpu.VMEM)
SMEM = pl.BlockSpec(memory_space=pltpu.SMEM)
ANY = pl.BlockSpec(memory_space=pl.ANY)


def params(mib):
    return pltpu.CompilerParams(vmem_limit_bytes=mib << 20)


def partner(at, step, size):
    return at ^ step if size & (size - 1) == 0 else (at + step) % size


def origin(at, step, size):
    return at ^ step if size & (size - 1) == 0 else (at - step) % size


def swap(value, axis, step):
    size = lax.axis_size(axis)
    return lax.ppermute(value, axis, [(at, partner(at, step, size)) for at in range(size)])


def dot(a, b, contract):
    return lax.dot_general(a, b, (contract, ((), ())), preferred_element_type=F32)


def copy_all(sems, pairs):
    copies = [pltpu.make_async_copy(*pair, sems.at[n]) for n, pair in enumerate(pairs)]
    for copy in copies:
        copy.start()
    return copies


def pick_kernel(experts, spot, *refs):
    sources, outs = refs[:5], refs[5 : 5 + experts]
    table, count, weight, tokens, grads, sems = refs[5 + experts :]
    loads = copy_all(sems, list(zip(sources, refs[5 + experts : -1])))
    for copy in loads:
        copy.wait()
    slots = table.shape[-1]
    rows = lax.broadcasted_iota(jnp.int32, (slots, slots), 0)
    lanes = lax.broadcasted_iota(jnp.int32, (slots, slots), 1)

    def column(row):
        return jnp.sum(jnp.where(rows == lanes, row, 0), axis=1, keepdims=True)

    for d in range(experts):
        to = partner(spot[0], d, experts)
        live = lax.broadcasted_iota(jnp.int32, (slots, 1), 0) < count[0, 0, to]
        token = column(table[0, 0, pl.ds(to, 1), :].astype(F32)).astype(jnp.int32)
        chance = column(weight[0, 0, pl.ds(to, 1), :])
        ids = lax.broadcasted_iota(jnp.int32, (slots, tokens.shape[1]), 1)
        picks = jnp.where((ids == token) & live, 1.0, 0.0).astype(BF16)
        outs[d][:slots, :] = dot(picks, tokens[0], ((1,), (0,))).astype(BF16)
        chosen = dot(picks, grads[0], ((1,), (0,)))
        outs[d][slots:, :] = (chance * chosen).astype(BF16)


def cut_kernel(islands, pieces, spot, drift, *refs):
    *blocks, sems = refs
    rows, columns = blocks[0].shape
    pairs = []
    for d, first, count_rows, target, at_row in pieces:
        at = partner(spot[3], d, islands)
        top = pl.multiple_of(lax.div(at, spot[4]) * rows + first, 32)
        left = pl.multiple_of(lax.rem(at, spot[4]) * columns, columns)
        source = drift.at[0, 0, pl.ds(top, count_rows), pl.ds(left, columns)]
        pairs.append((source, blocks[target].at[pl.ds(at_row, count_rows)]))
    for copy in copy_all(sems, pairs):
        copy.wait()


def gather_kernel(count, *refs):
    arrived, joined = refs[:count], refs[count]
    slots = arrived[0].shape[0] // 2
    for n, piece in enumerate(arrived):
        joined[n * slots : (n + 1) * slots, :] = piece[:slots, :]
        joined[(count + n) * slots : (count + n + 1) * slots, :] = piece[slots:, :]


def join_kernel(blocks, joined, *refs):
    drifts, (turned, drift_sum) = refs[:blocks], refs[blocks : blocks + 2]
    rows = drift_sum.shape[0]
    for n, ref in enumerate(refs[blocks + 2 :]):
        ref[...] = drifts[1 + n][rows:, :]
    turned[...] = joined[: joined.shape[0] // 2, :].T
    added = drifts[0][...].astype(F32)
    for other in drifts[1:]:
        added = added + other[:rows, :].astype(F32)
    drift_sum[...] = added


def hidden_kernel(parts, across, spot, gate, down, *refs):
    joined, out, norms = refs[:parts], refs[parts], refs[-1]
    rows, half = joined[0].shape[0] // 2, joined[0].shape[1]
    columns = out.shape[2]
    starts = [pl.multiple_of(origin(spot[1], t, parts) * half, half) for t in range(parts)]
    hidden_gram = 0.0
    for r in range(across):
        first = r * columns
        value = 0.0
        back = 0.0
        for t in range(parts):
            block = gate[0, 0, pl.ds(starts[t], half), first : first + columns]
            value = value + dot(joined[t][:rows, :], block, ((1,), (0,)))
            block = down[0, 0, first : first + columns, pl.ds(starts[t], half)]
            back = back + dot(joined[t][rows:, :], block, ((1,), (1,)))
        rounded = (back * (value / (1.0 + jnp.exp(-value)))).astype(BF16)
        out[r] = rounded
        hidden_gram = hidden_gram + dot(rounded, rounded, ((1,), (1,)))
    input_gram = 0.0
    for t in range(parts):
        features = joined[t][:rows, :]
        input_gram = input_gram + dot(features, features, ((1,), (1,)))
    norms[...] = jnp.full(norms.shape, jnp.sum(hidden_gram * input_gram), F32)


def average_kernel(islands, entries, tiles, spot, norms, drift_sum, own, moved, *refs):
    messages = refs[:islands]
    scaled, notes, total, square = refs[islands:]
    rows = total.shape[0] // tiles
    slots = own.shape[2]
    group = norms.shape[0] // islands
    scales = []
    for d in range(islands):
        at = origin(spot[3], d, islands)
        norm = jnp.sum(norms[pl.ds(at * group, group)], axis=0)[:1, :1]
        scales.append(jnp.minimum(1.0, math.sqrt(entries) / jnp.sqrt(norm + 1e-06)) / islands)
    handed = [m for m in messages[:0:-1] if m.shape[0] > slots]

    def compute(features):
        squares = 0.0
        for m in range(tiles):
            part = slice(m * rows, (m + 1) * rows)
            average = drift_sum[part, :]
            if handed:
                size = handed[0].shape[0] - slots
                n, first = divmod(m * rows, size)
                first += slots
                average = average + handed[n][first : first + rows, :].astype(F32)
            average = average * (1.0 / islands)
            for d in range(islands):
                factor = messages[d][:slots, :]
                average = average + scales[d] * dot(features[d, part, :], factor, ((1,), (0,)))
            total[part, :] = average
            squares = squares + jnp.sum(average * average, axis=0, keepdims=True)
        square[...] = squares

    pl.when(spot[5] == 1)(lambda: compute(own))
    pl.when(spot[5] != 1)(lambda: compute(moved))
    peak = jnp.max(jnp.abs(total[...]))
    unit = jnp.maximum(peak, 1e-30) / 32768
    value = total[...] * (1 / unit)
    spread_out = value * 8193.0
    value = spread_out - (spread_out - value)
    scaled[...] = jnp.where(jnp.abs(value) < 2.0**-13, 0.0, value)
    sublane = lax.broadcasted_iota(jnp.int32, notes.shape, 1)
    notes[...] = jnp.where(sublane == 0, jnp.sum(square[...]), unit)


def hand_kernel(islands, tails, spot, norms, hidden, *refs):
    features, relays = refs[:islands], refs[islands : islands + len(tails)]
    joined, passed, *messages = refs[islands + len(tails) :]
    across, slots, _ = hidden.shape
    for n in range(islands):
        joined[n] = features[n][...]
    passed[...] = norms[...]
    for d, message in enumerate(messages):
        block = lax.rem(partner(spot[3], d, islands), across)
        message[:slots, :] = hidden[pl.ds(block, 1)][0]
        if d in tails:
            message[slots:, :] = relays[tails.index(d)][...]


def own_kernel(slots, block, slots_out, block_out):
    slots_out[...] = slots[...]
    block_out[...] = block[...]


def update_kernel(entries, pieces, cuts, place, notes, momentum, *refs):
    values = refs[: len(pieces)]
    new_momentum, outer_step, moved, step, in_sems, sems = refs[-6:]
    rows, columns = values[0].shape
    size = rows // cuts
    parts = [(n, m) for n in range(len(pieces)) for m in range(cuts)]
    spots, loads = [], []
    for i, (n, m) in enumerate(parts):
        d, first = pieces[n]
        top = pl.multiple_of(pl.multiple_of(place[3 * d], 32) + first + m * size, 32)
        left = pl.multiple_of(place[3 * d + 1], columns)
        spots.append((0, pl.ds(top, size), pl.ds(left, columns)))
        here = moved.at[n, pl.ds(m * size, size)]
        loads.append(pltpu.make_async_copy(momentum.at[spots[i]], here, in_sems.at[i]))
        loads[-1].start()
    square = jnp.sum(notes[...], axis=0)[:1, :1]
    clip = jnp.minimum(1.0, 0.25 * math.sqrt(entries) / jnp.sqrt(square + 1e-06))
    stored = []
    for i, (n, m) in enumerate(parts):
        unit = notes[pl.ds(place[3 * pieces[n][0] + 2], 1)][0, 1:2, :1]
        here = slice(m * size, (m + 1) * size)
        clipped = (clip * unit) * values[n][here, :]
        loads[i].wait()
        fresh = 0.9 * moved[n, here, :] + clipped
        moved[n, here, :] = fresh
        step[n, here, :] = (0.7 * (clipped + 0.9 * fresh)).astype(BF16)
        for k, (held, out) in enumerate(((moved, new_momentum), (step, outer_step))):
            held = held.at[n, pl.ds(m * size, size)]
            stored.append(pltpu.make_async_copy(held, out.at[spots[i]], sems.at[i, k]))
            stored[-1].start()
    for copy in stored:
        copy.wait()


def body(
    tokens,
    token_grads,
    slot_token,
    slot_count,
    slot_prob,
    gate_weight,
    down_weight,
    drift,
    momentum,
):
    islands, experts, parts = (lax.axis_size(a) for a in AXES)
    island, expert, part = (lax.axis_index(a) for a in AXES)
    devices = islands * experts * parts
    features, hidden = gate_weight.shape[2:]
    half = features // parts
    across = islands // parts
    columns = hidden // across
    entries = features * hidden * experts * parts
    slots = slot_token.shape[3]
    routed_rows = experts * slots
    holder = island // across
    spot = jnp.stack(
        [expert, part, island % across, island, jnp.int32(across), (part == holder).astype(jnp.int32)]
    ).astype(jnp.int32)

    handed = half // 2 if islands == 4 else 0
    steps = [0, 1, 2] if handed else list(range(islands))
    pieces = [(d, 0, half, n, 0) for n, d in enumerate(steps)]
    if handed:
        pieces += [(3, 0, handed, 1, half), (3, handed, handed, 2, half)]
    block_rows = [half + (handed if d else 0) for d in steps]
    picked = pl.pallas_call(
        lambda *refs: pick_kernel(experts, *refs),
        in_specs=[SMEM] + [ANY] * 5,
        out_specs=[VMEM] * experts,
        out_shape=[jax.ShapeDtypeStruct((2 * slots, half), BF16)] * experts,
        scratch_shapes=[
            pltpu.VMEM(slot_token.shape, jnp.int32),
            pltpu.SMEM(slot_count.shape, jnp.int32),
            pltpu.VMEM(slot_prob.shape, F32),
            pltpu.VMEM(tokens.shape, BF16),
            pltpu.VMEM(token_grads.shape, BF16),
            pltpu.SemaphoreType.DMA((5,)),
        ],
        compiler_params=params(56),
        name="pick_slots",
    )(spot, slot_token, slot_count, slot_prob, tokens, token_grads)
    blocks = pl.pallas_call(
        lambda *refs: cut_kernel(islands, pieces, *refs),
        in_specs=[SMEM, ANY],
        out_specs=[VMEM] * len(steps),
        out_shape=[jax.ShapeDtypeStruct((rows, columns), BF16) for rows in block_rows],
        scratch_shapes=[pltpu.SemaphoreType.DMA((len(pieces),))],
        compiler_params=params(50),
        name="cut_drift",
    )(spot, drift)
    arrived = [picked[0]] + [swap(picked[d], "expert", d) for d in range(1, experts)]
    drift_in = [blocks[0]] + [swap(blocks[d], "island", d) for d in steps[1:]]
    arrived[0], drift_in[0] = pl.pallas_call(
        own_kernel,
        in_specs=[VMEM] * 2,
        out_specs=[VMEM] * 2,
        out_shape=[
            jax.ShapeDtypeStruct((2 * slots, half), BF16),
            jax.ShapeDtypeStruct((half, columns), BF16),
        ],
        compiler_params=params(6),
        name="own_parts",
    )(arrived[0], drift_in[0])
    joined = pl.pallas_call(
        lambda *refs: gather_kernel(experts, *refs),
        in_specs=[VMEM] * experts,
        out_specs=VMEM,
        out_shape=jax.ShapeDtypeStruct((2 * routed_rows, half), BF16),
        compiler_params=params(6 + routed_rows // 48),
        name="gather_slots",
    )(*arrived)
    turned, drift_sum, *relays = pl.pallas_call(
        lambda *refs: join_kernel(len(steps), *refs),
        in_specs=[VMEM] * (1 + len(steps)),
        out_specs=[VMEM] * (4 if handed else 2),
        out_shape=[
            jax.ShapeDtypeStruct((half, routed_rows), BF16),
            jax.ShapeDtypeStruct((half, columns), F32),
        ]
        + [jax.ShapeDtypeStruct((handed, columns), BF16)] * (2 if handed else 0),
        compiler_params=params(12 + routed_rows // 48),
        name="join_blocks",
    )(joined, *drift_in)

    joined_all = [joined] + [swap(joined, "tensor", t) for t in range(1, parts)]

    def send_features(d):
        pairs = []
        for at in range(islands):
            to = partner(at, d, islands)
            pairs.append((at * parts + to // across, to * parts + to // across))
        return lax.ppermute(turned, ("island", "tensor"), pairs)

    def spread(value):
        result = value
        for t in range(1, parts):
            pairs = []
            for at in range(islands):
                keep = at // across
                pairs.append((at * parts + keep, at * parts + partner(keep, t, parts)))
            moved = lax.ppermute(value, ("island", "tensor"), pairs)
            result = moved if t == 1 else result + moved
        return result

    features_in = [send_features(d) for d in range(1, islands)]

    hidden_out, norms = pl.pallas_call(
        lambda *refs: hidden_kernel(parts, across, *refs),
        in_specs=[SMEM] + [VMEM] * (2 + parts),
        out_specs=[VMEM] * 2,
        out_shape=[
            jax.ShapeDtypeStruct((across, routed_rows, columns), BF16),
            jax.ShapeDtypeStruct((devices, 8, 128), F32),
        ],
        compiler_params=params(16 + routed_rows // 48),
        name="hidden_grads",
    )(spot, gate_weight, down_weight, *joined_all)
    tails = [2, 1] if handed else []
    message_rows = [
        routed_rows + (half - handed if d in tails else 0) for d in range(islands)
    ]
    features_in, norms, *messages = pl.pallas_call(
        lambda *refs: hand_kernel(islands, tails, *refs),
        in_specs=[SMEM] + [VMEM] * (2 + islands + len(relays)),
        out_specs=[VMEM] * (2 + islands),
        out_shape=[
            jax.ShapeDtypeStruct((islands, half, routed_rows), BF16),
            jax.ShapeDtypeStruct(norms.shape, F32),
        ]
        + [jax.ShapeDtypeStruct((rows, columns), BF16) for rows in message_rows],
        compiler_params=params(6 + routed_rows // 48),
        name="hand_on",
    )(spot, norms, hidden_out, turned, *features_in, *relays)
    features_moved = spread(features_in)
    norms = lax.all_to_all(norms, AXES, split_axis=0, concat_axis=0, tiled=True)
    messages_in = [messages[0]] + [swap(messages[d], "island", d) for d in range(1, islands)]

    scaled, notes = pl.pallas_call(
        lambda *refs: average_kernel(islands, entries, 2, *refs),
        in_specs=[SMEM] + [VMEM] * (4 + islands),
        out_specs=[VMEM] * 2,
        out_shape=[
            jax.ShapeDtypeStruct((half, columns), F32),
            jax.ShapeDtypeStruct((devices, 8, 128), F32),
        ],
        scratch_shapes=[pltpu.VMEM((half, columns), F32), pltpu.VMEM((1, columns), F32)],
        compiler_params=params(8 + routed_rows // 48),
        name="average_block",
    )(spot, norms, drift_sum, features_in, features_moved, *messages_in)
    notes = lax.all_to_all(notes, AXES, split_axis=0, concat_axis=0, tiled=True)

    sent = scaled.astype(WIRE)
    values, last = {(0, 0): scaled}, {}
    steps = [1, 2] if handed else range(1, islands)
    for d in steps:
        values[d, 0] = swap(sent, "island", d)
    if handed:
        nothing = jnp.where(notes[0, 1, 0] < 0, handed, 0)

        def rows_of(value, first):
            return lax.dynamic_slice(value, (first + nothing, 0), (handed, columns))

        last[3, 0] = swap(rows_of(values[1, 0], 0), "island", 2)
        last[3, handed] = swap(rows_of(values[2, 0], handed), "island", 1)
    place = []
    for d in range(islands):
        at = origin(island, d, islands)
        source = (at * experts + expert) * parts + part
        place += [(at // across) * half, (at % across) * columns, source]
    place = jnp.stack(place).astype(jnp.int32)
    outs = []
    for values, cost, cuts in ((values, 12, 2), (last, 3, 2)):
        if not values:
            continue
        outs = pl.pallas_call(
            functools.partial(update_kernel, entries, list(values), cuts),
            in_specs=[SMEM, VMEM, ANY] + [VMEM] * len(values) + [ANY] * len(outs),
            out_specs=[ANY, ANY],
            out_shape=[
                jax.ShapeDtypeStruct(momentum.shape, F32),
                jax.ShapeDtypeStruct(momentum.shape, BF16),
            ],
            scratch_shapes=[
                pltpu.VMEM((len(values), *next(iter(values.values())).shape), F32),
                pltpu.VMEM((len(values), *next(iter(values.values())).shape), BF16),
                pltpu.SemaphoreType.DMA((len(values) * cuts,)),
                pltpu.SemaphoreType.DMA((len(values) * cuts, 2)),
            ],
            input_output_aliases={3 + len(values) + n: n for n in range(len(outs))},
            cost_estimate=pl.CostEstimate(
                flops=0, bytes_accessed=cost * momentum.size, transcendentals=0
            ),
            compiler_params=params(50),
            name="update_pieces",
        )(place, notes, momentum, *[v.astype(F32) for v in values.values()], *outs)
    return tuple(outs)


def solution(mesh):
    return jax.shard_map(
        body,
        mesh=mesh,
        in_specs=(
            P("island", "expert", "tensor"),
            P("island", "expert", "tensor"),
            P("island", "expert", None, None),
            P("island", "expert", None),
            P("island", "expert", None, None),
            P("island", "expert", None, "tensor"),
            P("island", "expert", "tensor", None),
            P("island", "expert", None, "tensor"),
            P("expert", None, "tensor"),
        ),
        out_specs=(P("expert", None, "tensor"), P("expert", None, "tensor")),
        check_vma=False,
    )
```

```python
import functools
import math

import jax
import jax.numpy as jnp
from jax import lax
from jax.experimental import pallas as pl
from jax.experimental.pallas import tpu as pltpu
from jax.sharding import PartitionSpec as P

F32 = jnp.float32
BF16 = jnp.bfloat16
WIRE = jnp.float16
AXES = ("island", "expert", "tensor")

VMEM = pl.BlockSpec(memory_space=pltpu.VMEM)
SMEM = pl.BlockSpec(memory_space=pltpu.SMEM)
ANY = pl.BlockSpec(memory_space=pl.ANY)


def params(mib):
    return pltpu.CompilerParams(vmem_limit_bytes=mib << 20)


def partner(at, step, size):
    return at ^ step if size & (size - 1) == 0 else (at + step) % size


def origin(at, step, size):
    return at ^ step if size & (size - 1) == 0 else (at - step) % size


def swap(value, axis, step):
    size = lax.axis_size(axis)
    return lax.ppermute(value, axis, [(at, partner(at, step, size)) for at in range(size)])


def dot(a, b, contract):
    return lax.dot_general(a, b, (contract, ((), ())), preferred_element_type=F32)


def copy_all(sems, pairs):
    copies = [pltpu.make_async_copy(*pair, sems.at[n]) for n, pair in enumerate(pairs)]
    for copy in copies:
        copy.start()
    return copies


def pick_kernel(experts, spot, *refs):
    sources, outs = refs[:5], refs[5 : 5 + experts]
    table, count, weight, tokens, grads, sems = refs[5 + experts :]
    loads = copy_all(sems, list(zip(sources, refs[5 + experts : -1])))
    for copy in loads:
        copy.wait()
    slots = table.shape[-1]
    rows = lax.broadcasted_iota(jnp.int32, (slots, slots), 0)
    lanes = lax.broadcasted_iota(jnp.int32, (slots, slots), 1)

    def column(row):
        return jnp.sum(jnp.where(rows == lanes, row, 0), axis=1, keepdims=True)

    for d in range(experts):
        to = partner(spot[0], d, experts)
        live = lax.broadcasted_iota(jnp.int32, (slots, 1), 0) < count[0, 0, to]
        token = column(table[0, 0, pl.ds(to, 1), :].astype(F32)).astype(jnp.int32)
        chance = column(weight[0, 0, pl.ds(to, 1), :])
        ids = lax.broadcasted_iota(jnp.int32, (slots, tokens.shape[1]), 1)
        picks = jnp.where((ids == token) & live, 1.0, 0.0).astype(BF16)
        outs[d][:slots, :] = dot(picks, tokens[0], ((1,), (0,))).astype(BF16)
        chosen = dot(picks, grads[0], ((1,), (0,)))
        outs[d][slots:, :] = (chance * chosen).astype(BF16)


def cut_kernel(islands, pieces, spot, drift, *blocks):
    rows, columns = blocks[0].shape
    for d, first, count_rows, target, at_row in pieces:
        at = partner(spot[3], d, islands)
        top = pl.multiple_of(lax.div(at, spot[4]) * rows + first, 32)
        left = pl.multiple_of(lax.rem(at, spot[4]) * columns, columns)
        source = drift[0, 0, pl.ds(top, count_rows), pl.ds(left, columns)]
        blocks[target][at_row : at_row + count_rows, :] = source


def gather_kernel(count, *refs):
    arrived, (inputs, grads) = refs[:count], refs[count:]
    slots = arrived[0].shape[0] // 2
    for n, piece in enumerate(arrived):
        inputs[n * slots : (n + 1) * slots, :] = piece[:slots, :]
        grads[n * slots : (n + 1) * slots, :] = piece[slots:, :]


def join_kernel(parts, blocks, spot, *refs):
    joined, drifts = refs[:parts], refs[parts : parts + blocks]
    shares, (drift_sum, *relays) = refs[parts + blocks :][:parts], refs[parts + blocks :][parts:]
    rows = drift_sum.shape[0]
    for n, ref in enumerate(relays):
        ref[...] = drifts[1 + n][rows:, :]
    size = shares[0].shape[0]
    first = pl.multiple_of(spot[1] * size, size)

    def take(share, source):
        share[...] = source[:, pl.ds(first, size)].T

    for r in range(parts):
        for t in range(parts):
            pl.when(partner(spot[5], r, parts) == t)(functools.partial(take, shares[r], joined[t]))
    added = drifts[0][...].astype(F32)
    for other in drifts[1:]:
        added = added + other[:rows, :].astype(F32)
    drift_sum[...] = added


def hidden_kernel(parts, across, spot, gate, down, *refs):
    inputs, grads, (out, norms) = refs[:parts], refs[parts : 2 * parts], refs[2 * parts :]
    half = inputs[0].shape[1]
    columns = out.shape[2]
    starts = [pl.multiple_of(origin(spot[1], t, parts) * half, half) for t in range(parts)]
    hidden_gram = 0.0
    for r in range(across):
        first = r * columns
        value = 0.0
        back = 0.0
        for t in range(parts):
            block = gate[0, 0, pl.ds(starts[t], half), first : first + columns]
            value = value + dot(inputs[t][...], block, ((1,), (0,)))
            block = down[0, 0, first : first + columns, pl.ds(starts[t], half)]
            back = back + dot(grads[t][...], block, ((1,), (1,)))
        rounded = (back * (value / (1.0 + jnp.exp(-value)))).astype(BF16)
        out[r] = rounded
        hidden_gram = hidden_gram + dot(rounded, rounded, ((1,), (1,)))
    input_gram = 0.0
    for t in range(parts):
        features = inputs[t][...]
        input_gram = input_gram + dot(features, features, ((1,), (1,)))
    norms[...] = jnp.full(norms.shape, jnp.sum(hidden_gram * input_gram), F32)


def average_kernel(islands, entries, parts, spot, norms, drift_sum, *refs):
    features, messages = refs[:parts], refs[parts : parts + islands]
    scaled, notes, total, square = refs[parts + islands :]
    rows = total.shape[0] // parts
    slots = features[0].shape[2]
    group = norms.shape[0] // islands
    scales = []
    for d in range(islands):
        at = origin(spot[3], d, islands)
        norm = jnp.sum(norms[pl.ds(at * group, group)], axis=0)[:1, :1]
        scales.append(jnp.minimum(1.0, math.sqrt(entries) / jnp.sqrt(norm + 1e-06)) / islands)
    handed = [m for m in messages[:0:-1] if m.shape[0] > slots]

    def compute(at):
        squares = 0.0
        for m in range(parts):
            part = slice(m * rows, (m + 1) * rows)
            average = drift_sum[part, :]
            if handed:
                size = handed[0].shape[0] - slots
                n, first = divmod(m * rows, size)
                first += slots
                average = average + handed[n][first : first + rows, :].astype(F32)
            average = average * (1.0 / islands)
            for d in range(islands):
                factor = messages[d][:slots, :]
                average = average + scales[d] * dot(features[partner(at, m, parts)][d], factor, ((1,), (0,)))
            total[part, :] = average
            squares = squares + jnp.sum(average * average, axis=0, keepdims=True)
        square[...] = squares

    for at in range(parts):
        pl.when(spot[1] == at)(functools.partial(compute, at))
    peak = jnp.max(jnp.abs(total[...]))
    unit = jnp.maximum(peak, 1e-30) / 32768
    value = total[...] * (1 / unit)
    spread_out = value * 8193.0
    value = spread_out - (spread_out - value)
    scaled[...] = jnp.where(jnp.abs(value) < 2.0**-13, 0.0, value)
    sublane = lax.broadcasted_iota(jnp.int32, notes.shape, 1)
    notes[...] = jnp.where(sublane == 0, jnp.sum(square[...]), unit)


def hand_kernel(islands, tails, spot, norms, hidden, *refs):
    features, relays = refs[:islands], refs[islands : islands + len(tails)]
    joined, passed, *messages = refs[islands + len(tails) :]
    across, slots, _ = hidden.shape
    for n in range(islands):
        joined[n] = features[n][...]
    passed[...] = norms[...]
    for d, message in enumerate(messages):
        block = lax.rem(partner(spot[3], d, islands), across)
        message[:slots, :] = hidden[pl.ds(block, 1)][0]
        if d in tails:
            message[slots:, :] = relays[tails.index(d)][...]


def own_kernel(slots, block, slots_out, block_out):
    slots_out[...] = slots[...]
    block_out[...] = block[...]


def update_kernel(entries, pieces, cuts, place, notes, momentum, *refs):
    values = refs[: len(pieces)]
    new_momentum, outer_step, moved, step, in_sems, sems = refs[-6:]
    rows, columns = values[0].shape
    size = rows // cuts
    parts = [(n, m) for n in range(len(pieces)) for m in range(cuts)]
    spots, loads = [], []
    for i, (n, m) in enumerate(parts):
        d, first = pieces[n]
        top = pl.multiple_of(pl.multiple_of(place[3 * d], 32) + first + m * size, 32)
        left = pl.multiple_of(place[3 * d + 1], columns)
        spots.append((0, pl.ds(top, size), pl.ds(left, columns)))
        here = moved.at[n, pl.ds(m * size, size)]
        loads.append(pltpu.make_async_copy(momentum.at[spots[i]], here, in_sems.at[i]))
        loads[-1].start()
    square = jnp.sum(notes[...], axis=0)[:1, :1]
    clip = jnp.minimum(1.0, 0.25 * math.sqrt(entries) / jnp.sqrt(square + 1e-06))
    stored = []
    for i, (n, m) in enumerate(parts):
        unit = notes[pl.ds(place[3 * pieces[n][0] + 2], 1)][0, 1:2, :1]
        here = slice(m * size, (m + 1) * size)
        clipped = (clip * unit) * values[n][here, :]
        loads[i].wait()
        fresh = 0.9 * moved[n, here, :] + clipped
        moved[n, here, :] = fresh
        step[n, here, :] = (0.7 * (clipped + 0.9 * fresh)).astype(BF16)
        for k, (held, out) in enumerate(((moved, new_momentum), (step, outer_step))):
            held = held.at[n, pl.ds(m * size, size)]
            stored.append(pltpu.make_async_copy(held, out.at[spots[i]], sems.at[i, k]))
            stored[-1].start()
    for copy in stored:
        copy.wait()


def body(
    tokens,
    token_grads,
    slot_token,
    slot_count,
    slot_prob,
    gate_weight,
    down_weight,
    drift,
    momentum,
):
    islands, experts, parts = (lax.axis_size(a) for a in AXES)
    island, expert, part = (lax.axis_index(a) for a in AXES)
    devices = islands * experts * parts
    features, hidden = gate_weight.shape[2:]
    half = features // parts
    across = islands // parts
    columns = hidden // across
    entries = features * hidden * experts * parts
    slots = slot_token.shape[3]
    routed_rows = experts * slots
    holder = island // across
    spot = jnp.stack(
        [expert, part, island % across, island, jnp.int32(across), part ^ holder]
    ).astype(jnp.int32)

    handed = half // 2 if islands == 4 else 0
    steps = [0, 1, 2] if handed else list(range(islands))
    pieces = [(d, 0, half, n, 0) for n, d in enumerate(steps)]
    if handed:
        pieces += [(3, 0, handed, 1, half), (3, handed, handed, 2, half)]
    block_rows = [half + (handed if d else 0) for d in steps]
    picked = pl.pallas_call(
        lambda *refs: pick_kernel(experts, *refs),
        in_specs=[SMEM] + [ANY] * 5,
        out_specs=[VMEM] * experts,
        out_shape=[jax.ShapeDtypeStruct((2 * slots, half), BF16)] * experts,
        scratch_shapes=[
            pltpu.VMEM(slot_token.shape, jnp.int32),
            pltpu.SMEM(slot_count.shape, jnp.int32),
            pltpu.VMEM(slot_prob.shape, F32),
            pltpu.VMEM(tokens.shape, BF16),
            pltpu.VMEM(token_grads.shape, BF16),
            pltpu.SemaphoreType.DMA((5,)),
        ],
        compiler_params=params(56),
        name="pick_slots",
    )(spot, slot_token, slot_count, slot_prob, tokens, token_grads)
    blocks = pl.pallas_call(
        lambda *refs: cut_kernel(islands, pieces, *refs),
        in_specs=[SMEM, VMEM],
        out_specs=[VMEM] * len(steps),
        out_shape=[jax.ShapeDtypeStruct((rows, columns), BF16) for rows in block_rows],
        compiler_params=params(16),
        name="cut_drift",
    )(spot, drift)
    arrived = [picked[0]] + [swap(picked[d], "expert", d) for d in range(1, experts)]
    drift_in = [blocks[0]] + [swap(blocks[d], "island", d) for d in steps[1:]]
    arrived[0], drift_in[0] = pl.pallas_call(
        own_kernel,
        in_specs=[VMEM] * 2,
        out_specs=[VMEM] * 2,
        out_shape=[
            jax.ShapeDtypeStruct((2 * slots, half), BF16),
            jax.ShapeDtypeStruct((half, columns), BF16),
        ],
        compiler_params=params(6),
        name="own_parts",
    )(arrived[0], drift_in[0])
    rows_block = jax.ShapeDtypeStruct((routed_rows, half), BF16)
    inputs, grads = pl.pallas_call(
        lambda *refs: gather_kernel(experts, *refs),
        in_specs=[VMEM] * experts,
        out_specs=[VMEM] * 2,
        out_shape=[rows_block] * 2,
        compiler_params=params(6 + routed_rows // 48),
        name="gather_slots",
    )(*arrived)

    inputs_all = [inputs] + [swap(inputs, "tensor", t) for t in range(1, parts)]
    grads_all = [grads] + [swap(grads, "tensor", t) for t in range(1, parts)]
    share = jax.ShapeDtypeStruct((half // parts, routed_rows), BF16)
    outputs = pl.pallas_call(
        lambda *refs: join_kernel(parts, len(steps), *refs),
        in_specs=[SMEM] + [VMEM] * (parts + len(steps)),
        out_specs=[VMEM] * (parts + (3 if handed else 1)),
        out_shape=[share] * parts
        + [jax.ShapeDtypeStruct((half, columns), F32)]
        + [jax.ShapeDtypeStruct((handed, columns), BF16)] * (2 if handed else 0),
        compiler_params=params(14 + routed_rows // 48),
        name="join_blocks",
    )(spot, *inputs_all, *drift_in)
    shares, (drift_sum, *relays) = outputs[:parts], outputs[parts:]

    features_in = [swap(shares[d // across], "island", d) for d in range(1, islands)]

    hidden_out, norms = pl.pallas_call(
        lambda *refs: hidden_kernel(parts, across, *refs),
        in_specs=[SMEM] + [VMEM] * (2 + 2 * parts),
        out_specs=[VMEM] * 2,
        out_shape=[
            jax.ShapeDtypeStruct((across, routed_rows, columns), BF16),
            jax.ShapeDtypeStruct((devices, 8, 128), F32),
        ],
        compiler_params=params(16 + routed_rows // 48),
        name="hidden_grads",
    )(spot, gate_weight, down_weight, *inputs_all, *grads_all)
    tails = [2, 1] if handed else []
    message_rows = [
        routed_rows + (half - handed if d in tails else 0) for d in range(islands)
    ]
    features_in, norms, *messages = pl.pallas_call(
        lambda *refs: hand_kernel(islands, tails, *refs),
        in_specs=[SMEM] + [VMEM] * (2 + islands + len(relays)),
        out_specs=[VMEM] * (2 + islands),
        out_shape=[
            jax.ShapeDtypeStruct((islands, half // parts, routed_rows), BF16),
            jax.ShapeDtypeStruct(norms.shape, F32),
        ]
        + [jax.ShapeDtypeStruct((rows, columns), BF16) for rows in message_rows],
        compiler_params=params(6 + routed_rows // 48),
        name="hand_on",
    )(spot, norms, hidden_out, shares[0], *features_in, *relays)
    features_of = [features_in] + [swap(features_in, "tensor", t) for t in range(1, parts)]
    norms = lax.all_to_all(norms, AXES, split_axis=0, concat_axis=0, tiled=True)
    messages_in = [messages[0]] + [swap(messages[d], "island", d) for d in range(1, islands)]

    scaled, notes = pl.pallas_call(
        lambda *refs: average_kernel(islands, entries, parts, *refs),
        in_specs=[SMEM] + [VMEM] * (2 + parts + islands),
        out_specs=[VMEM] * 2,
        out_shape=[
            jax.ShapeDtypeStruct((half, columns), F32),
            jax.ShapeDtypeStruct((devices, 8, 128), F32),
        ],
        scratch_shapes=[pltpu.VMEM((half, columns), F32), pltpu.VMEM((1, columns), F32)],
        compiler_params=params(8 + routed_rows // 48),
        name="average_block",
    )(spot, norms, drift_sum, *features_of, *messages_in)
    notes = lax.all_to_all(notes, AXES, split_axis=0, concat_axis=0, tiled=True)

    sent = scaled.astype(WIRE)
    values, last = {(0, 0): scaled}, {}
    steps = [1, 2] if handed else range(1, islands)
    for d in steps:
        values[d, 0] = swap(sent, "island", d)
    if handed:
        nothing = jnp.minimum(notes[0, 1, 0], 0.0).astype(WIRE)
        last[3, 0] = swap(values[1, 0][:handed] + nothing, "island", 2)
        last[3, handed] = swap(values[2, 0][handed:] + nothing, "island", 1)
    place = []
    for d in range(islands):
        at = origin(island, d, islands)
        source = (at * experts + expert) * parts + part
        place += [(at // across) * half, (at % across) * columns, source]
    place = jnp.stack(place).astype(jnp.int32)
    outs = []
    for values, cost, cuts in ((values, 12, 2), (last, 3, 2)):
        if not values:
            continue
        outs = pl.pallas_call(
            functools.partial(update_kernel, entries, list(values), cuts),
            in_specs=[SMEM, VMEM, ANY] + [VMEM] * len(values) + [ANY] * len(outs),
            out_specs=[ANY, ANY],
            out_shape=[
                jax.ShapeDtypeStruct(momentum.shape, F32),
                jax.ShapeDtypeStruct(momentum.shape, BF16),
            ],
            scratch_shapes=[
                pltpu.VMEM((len(values), *next(iter(values.values())).shape), F32),
                pltpu.VMEM((len(values), *next(iter(values.values())).shape), BF16),
                pltpu.SemaphoreType.DMA((len(values) * cuts,)),
                pltpu.SemaphoreType.DMA((len(values) * cuts, 2)),
            ],
            input_output_aliases={3 + len(values) + n: n for n in range(len(outs))},
            cost_estimate=pl.CostEstimate(
                flops=0, bytes_accessed=cost * momentum.size, transcendentals=0
            ),
            compiler_params=params(50),
            name="update_pieces",
        )(place, notes, momentum, *[v.astype(F32) for v in values.values()], *outs)
    return tuple(outs)


def solution(mesh):
    return jax.shard_map(
        body,
        mesh=mesh,
        in_specs=(
            P("island", "expert", "tensor"),
            P("island", "expert", "tensor"),
            P("island", "expert", None, None),
            P("island", "expert", None),
            P("island", "expert", None, None),
            P("island", "expert", None, "tensor"),
            P("island", "expert", "tensor", None),
            P("island", "expert", None, "tensor"),
            P("expert", None, "tensor"),
        ),
        out_specs=(P("expert", None, "tensor"), P("expert", None, "tensor")),
        check_vma=False,
    )
```

```python
import functools
import math

import jax
import jax.numpy as jnp
from jax import lax
from jax.experimental import pallas as pl
from jax.experimental.pallas import tpu as pltpu
from jax.sharding import PartitionSpec as P

F32 = jnp.float32
BF16 = jnp.bfloat16
WIRE = jnp.float16
AXES = ("island", "expert", "tensor")

VMEM = pl.BlockSpec(memory_space=pltpu.VMEM)
ANY = pl.BlockSpec(memory_space=pl.ANY)


def params(mib):
    return pltpu.CompilerParams(vmem_limit_bytes=mib << 20)


def partner(at, step, size):
    return at ^ step if size & (size - 1) == 0 else (at + step) % size


def origin(at, step, size):
    return at ^ step if size & (size - 1) == 0 else (at - step) % size


def swap(value, axis, step):
    size = lax.axis_size(axis)
    return lax.ppermute(value, axis, [(at, partner(at, step, size)) for at in range(size)])


def position():
    island, expert, part = (lax.axis_index(a) for a in AXES)
    across = lax.axis_size("island") // lax.axis_size("tensor")
    return expert, part, lax.rem(island, across), island, across, part == lax.div(island, across)


def dot(a, b, contract):
    return lax.dot_general(a, b, (contract, ((), ())), preferred_element_type=F32)


def copy_all(sems, pairs):
    copies = [pltpu.make_async_copy(*pair, sems.at[n]) for n, pair in enumerate(pairs)]
    for copy in copies:
        copy.start()
    return copies


def pick_kernel(experts, *refs):
    spot = position()
    sources, outs = refs[:5], refs[5 : 5 + experts]
    table, count, weight, tokens, grads, sems = refs[5 + experts :]
    loads = copy_all(sems, list(zip(sources, refs[5 + experts : -1])))
    for copy in loads:
        copy.wait()
    slots = table.shape[-1]
    rows = lax.broadcasted_iota(jnp.int32, (slots, slots), 0)
    lanes = lax.broadcasted_iota(jnp.int32, (slots, slots), 1)

    def column(row):
        return jnp.sum(jnp.where(rows == lanes, row, 0), axis=1, keepdims=True)

    for d in range(experts):
        to = partner(spot[0], d, experts)
        live = lax.broadcasted_iota(jnp.int32, (slots, 1), 0) < count[0, 0, to]
        token = column(table[0, 0, pl.ds(to, 1), :].astype(F32)).astype(jnp.int32)
        chance = column(weight[0, 0, pl.ds(to, 1), :])
        ids = lax.broadcasted_iota(jnp.int32, (slots, tokens.shape[1]), 1)
        picks = jnp.where((ids == token) & live, 1.0, 0.0).astype(BF16)
        outs[d][:slots, :] = dot(picks, tokens[0], ((1,), (0,))).astype(BF16)
        chosen = dot(picks, grads[0], ((1,), (0,)))
        outs[d][slots:, :] = (chance * chosen).astype(BF16)


def cut_kernel(islands, pieces, drift, *refs):
    spot = position()
    *blocks, sems = refs
    rows, columns = blocks[0].shape
    pairs = []
    for d, first, count_rows, target, at_row in pieces:
        at = partner(spot[3], d, islands)
        top = pl.multiple_of(lax.div(at, spot[4]) * rows + first, 32)
        left = pl.multiple_of(lax.rem(at, spot[4]) * columns, columns)
        source = drift.at[0, 0, pl.ds(top, count_rows), pl.ds(left, columns)]
        pairs.append((source, blocks[target].at[pl.ds(at_row, count_rows)]))
    for copy in copy_all(sems, pairs):
        copy.wait()


def gather_kernel(count, *refs):
    arrived, joined = refs[:count], refs[count]
    slots = arrived[0].shape[0] // 2
    for n, piece in enumerate(arrived):
        joined[n * slots : (n + 1) * slots, :] = piece[:slots, :]
        joined[(count + n) * slots : (count + n + 1) * slots, :] = piece[slots:, :]


def join_kernel(blocks, joined, *refs):
    drifts, (turned, drift_sum) = refs[:blocks], refs[blocks : blocks + 2]
    rows = drift_sum.shape[0]
    for n, ref in enumerate(refs[blocks + 2 :]):
        ref[...] = drifts[1 + n][rows:, :]
    turned[...] = joined[: joined.shape[0] // 2, :].T
    added = drifts[0][...].astype(F32)
    for other in drifts[1:]:
        added = added + other[:rows, :].astype(F32)
    drift_sum[...] = added


def hidden_kernel(parts, across, gate, down, *refs):
    spot = position()
    joined, out, norms = refs[:parts], refs[parts], refs[-1]
    rows, half = joined[0].shape[0] // 2, joined[0].shape[1]
    columns = out.shape[2]
    starts = [pl.multiple_of(origin(spot[1], t, parts) * half, half) for t in range(parts)]
    hidden_gram = 0.0
    for r in range(across):
        first = r * columns
        value = 0.0
        back = 0.0
        for t in range(parts):
            block = gate[0, 0, pl.ds(starts[t], half), first : first + columns]
            value = value + dot(joined[t][:rows, :], block, ((1,), (0,)))
            block = down[0, 0, first : first + columns, pl.ds(starts[t], half)]
            back = back + dot(joined[t][rows:, :], block, ((1,), (1,)))
        rounded = (back * (value / (1.0 + jnp.exp(-value)))).astype(BF16)
        out[r] = rounded
        hidden_gram = hidden_gram + dot(rounded, rounded, ((1,), (1,)))
    input_gram = 0.0
    for t in range(parts):
        features = joined[t][:rows, :]
        input_gram = input_gram + dot(features, features, ((1,), (1,)))
    norms[...] = jnp.full(norms.shape, jnp.sum(hidden_gram * input_gram), F32)


def average_kernel(islands, entries, tiles, norms, drift_sum, own, moved, *refs):
    spot = position()
    messages = refs[:islands]
    scaled, notes, total, square = refs[islands:]
    rows = total.shape[0] // tiles
    slots = own.shape[2]
    group = norms.shape[0] // islands
    scales = []
    for d in range(islands):
        at = origin(spot[3], d, islands)
        norm = jnp.sum(norms[pl.ds(at * group, group)], axis=0)[:1, :1]
        scales.append(jnp.minimum(1.0, math.sqrt(entries) / jnp.sqrt(norm + 1e-06)) / islands)
    handed = [m for m in messages[:0:-1] if m.shape[0] > slots]

    def compute(features):
        squares = 0.0
        for m in range(tiles):
            part = slice(m * rows, (m + 1) * rows)
            average = drift_sum[part, :]
            if handed:
                size = handed[0].shape[0] - slots
                n, first = divmod(m * rows, size)
                first += slots
                average = average + handed[n][first : first + rows, :].astype(F32)
            average = average * (1.0 / islands)
            for d in range(islands):
                factor = messages[d][:slots, :]
                average = average + scales[d] * dot(features[d, part, :], factor, ((1,), (0,)))
            total[part, :] = average
            squares = squares + jnp.sum(average * average, axis=0, keepdims=True)
        square[...] = squares

    pl.when(spot[5])(lambda: compute(own))
    pl.when(jnp.logical_not(spot[5]))(lambda: compute(moved))
    peak = jnp.max(jnp.abs(total[...]))
    unit = jnp.maximum(peak, 1e-30) / 32768
    value = total[...] * (1 / unit)
    spread_out = value * 8193.0
    value = spread_out - (spread_out - value)
    scaled[...] = jnp.where(jnp.abs(value) < 2.0**-13, 0.0, value)
    sublane = lax.broadcasted_iota(jnp.int32, notes.shape, 1)
    notes[...] = jnp.where(sublane == 0, jnp.sum(square[...]), unit)


def hand_kernel(islands, tails, norms, hidden, *refs):
    spot = position()
    features, relays = refs[:islands], refs[islands : islands + len(tails)]
    joined, passed, *messages = refs[islands + len(tails) :]
    across, slots, _ = hidden.shape
    for n in range(islands):
        joined[n] = features[n][...]
    passed[...] = norms[...]
    for d, message in enumerate(messages):
        block = lax.rem(partner(spot[3], d, islands), across)
        message[:slots, :] = hidden[pl.ds(block, 1)][0]
        if d in tails:
            message[slots:, :] = relays[tails.index(d)][...]


def own_kernel(slots, block, slots_out, block_out):
    slots_out[...] = slots[...]
    block_out[...] = block[...]


def update_kernel(entries, pieces, cuts, notes, momentum, *refs):
    values = refs[: len(pieces)]
    new_momentum, outer_step, moved, step, in_sems, sems = refs[-6:]
    expert, part, _, island, across, _ = position()
    islands, experts, devices = (lax.axis_size(a) for a in AXES)
    rows, columns = values[0].shape
    half = momentum.shape[1] // devices
    size = rows // cuts
    parts = [(n, m) for n in range(len(pieces)) for m in range(cuts)]
    spots, loads = [], []
    for i, (n, m) in enumerate(parts):
        d, first = pieces[n]
        at = origin(island, d, islands)
        top = pl.multiple_of(lax.div(at, across) * half + first + m * size, 32)
        left = pl.multiple_of(lax.rem(at, across) * columns, columns)
        spots.append((0, pl.ds(top, size), pl.ds(left, columns)))
        here = moved.at[n, pl.ds(m * size, size)]
        loads.append(pltpu.make_async_copy(momentum.at[spots[i]], here, in_sems.at[i]))
        loads[-1].start()
    square = jnp.sum(notes[...], axis=0)[:1, :1]
    clip = jnp.minimum(1.0, 0.25 * math.sqrt(entries) / jnp.sqrt(square + 1e-06))
    stored = []
    for i, (n, m) in enumerate(parts):
        at = (origin(island, pieces[n][0], islands) * experts + expert) * devices + part
        unit = notes[pl.ds(at, 1)][0, 1:2, :1]
        here = slice(m * size, (m + 1) * size)
        clipped = (clip * unit) * values[n][here, :]
        loads[i].wait()
        fresh = 0.9 * moved[n, here, :] + clipped
        moved[n, here, :] = fresh
        step[n, here, :] = (0.7 * (clipped + 0.9 * fresh)).astype(BF16)
        for k, (held, out) in enumerate(((moved, new_momentum), (step, outer_step))):
            held = held.at[n, pl.ds(m * size, size)]
            stored.append(pltpu.make_async_copy(held, out.at[spots[i]], sems.at[i, k]))
            stored[-1].start()
    for copy in stored:
        copy.wait()


def body(
    tokens,
    token_grads,
    slot_token,
    slot_count,
    slot_prob,
    gate_weight,
    down_weight,
    drift,
    momentum,
):
    islands, experts, parts = (lax.axis_size(a) for a in AXES)
    devices = islands * experts * parts
    features, hidden = gate_weight.shape[2:]
    half = features // parts
    across = islands // parts
    columns = hidden // across
    entries = features * hidden * experts * parts
    slots = slot_token.shape[3]
    routed_rows = experts * slots
    holder = lax.axis_index("island") // across
    handed = half // 2 if islands == 4 else 0
    steps = [0, 1, 2] if handed else list(range(islands))
    pieces = [(d, 0, half, n, 0) for n, d in enumerate(steps)]
    if handed:
        pieces += [(3, 0, handed, 1, half), (3, handed, handed, 2, half)]
    block_rows = [half + (handed if d else 0) for d in steps]
    picked = pl.pallas_call(
        lambda *refs: pick_kernel(experts, *refs),
        in_specs=[ANY] * 5,
        out_specs=[VMEM] * experts,
        out_shape=[jax.ShapeDtypeStruct((2 * slots, half), BF16)] * experts,
        scratch_shapes=[
            pltpu.VMEM(slot_token.shape, jnp.int32),
            pltpu.SMEM(slot_count.shape, jnp.int32),
            pltpu.VMEM(slot_prob.shape, F32),
            pltpu.VMEM(tokens.shape, BF16),
            pltpu.VMEM(token_grads.shape, BF16),
            pltpu.SemaphoreType.DMA((5,)),
        ],
        compiler_params=params(56),
        name="pick_slots",
    )(slot_token, slot_count, slot_prob, tokens, token_grads)
    blocks = pl.pallas_call(
        lambda *refs: cut_kernel(islands, pieces, *refs),
        in_specs=[ANY],
        out_specs=[VMEM] * len(steps),
        out_shape=[jax.ShapeDtypeStruct((rows, columns), BF16) for rows in block_rows],
        scratch_shapes=[pltpu.SemaphoreType.DMA((len(pieces),))],
        compiler_params=params(50),
        name="cut_drift",
    )(drift)
    arrived = [picked[0]] + [swap(picked[d], "expert", d) for d in range(experts - 1, 0, -1)]
    drift_in = [blocks[0]] + [swap(blocks[d], "island", d) for d in steps[1:]]
    arrived[0], drift_in[0] = pl.pallas_call(
        own_kernel,
        in_specs=[VMEM] * 2,
        out_specs=[VMEM] * 2,
        out_shape=[
            jax.ShapeDtypeStruct((2 * slots, half), BF16),
            jax.ShapeDtypeStruct((half, columns), BF16),
        ],
        compiler_params=params(6),
        name="own_parts",
    )(arrived[0], drift_in[0])
    joined = pl.pallas_call(
        lambda *refs: gather_kernel(experts, *refs),
        in_specs=[VMEM] * experts,
        out_specs=VMEM,
        out_shape=jax.ShapeDtypeStruct((2 * routed_rows, half), BF16),
        compiler_params=params(6 + routed_rows // 48),
        name="gather_slots",
    )(*arrived)
    turned, drift_sum, *relays = pl.pallas_call(
        lambda *refs: join_kernel(len(steps), *refs),
        in_specs=[VMEM] * (1 + len(steps)),
        out_specs=[VMEM] * (4 if handed else 2),
        out_shape=[
            jax.ShapeDtypeStruct((half, routed_rows), BF16),
            jax.ShapeDtypeStruct((half, columns), F32),
        ]
        + [jax.ShapeDtypeStruct((handed, columns), BF16)] * (2 if handed else 0),
        compiler_params=params(12 + routed_rows // 48),
        name="join_blocks",
    )(joined, *drift_in)

    joined_all = [joined] + [swap(joined, "tensor", t) for t in range(1, parts)]

    def send_features(d):
        pairs = []
        for at in range(islands):
            to = partner(at, d, islands)
            pairs.append((at * parts + to // across, to * parts + to // across))
        return lax.ppermute(turned, ("island", "tensor"), pairs)

    def spread(value):
        result = value
        for t in range(1, parts):
            pairs = []
            for at in range(islands):
                keep = at // across
                pairs.append((at * parts + keep, at * parts + partner(keep, t, parts)))
            moved = lax.ppermute(value, ("island", "tensor"), pairs)
            result = moved if t == 1 else result + moved
        return result

    features_in = [send_features(d) for d in range(1, islands)]

    hidden_out, norms = pl.pallas_call(
        lambda *refs: hidden_kernel(parts, across, *refs),
        in_specs=[VMEM] * (2 + parts),
        out_specs=[VMEM] * 2,
        out_shape=[
            jax.ShapeDtypeStruct((across, routed_rows, columns), BF16),
            jax.ShapeDtypeStruct((devices, 8, 128), F32),
        ],
        compiler_params=params(16 + routed_rows // 48),
        name="hidden_grads",
    )(gate_weight, down_weight, *joined_all)
    tails = [2, 1] if handed else []
    message_rows = [
        routed_rows + (half - handed if d in tails else 0) for d in range(islands)
    ]
    features_in, norms, *messages = pl.pallas_call(
        lambda *refs: hand_kernel(islands, tails, *refs),
        in_specs=[VMEM] * (2 + islands + len(relays)),
        out_specs=[VMEM] * (2 + islands),
        out_shape=[
            jax.ShapeDtypeStruct((islands, half, routed_rows), BF16),
            jax.ShapeDtypeStruct(norms.shape, F32),
        ]
        + [jax.ShapeDtypeStruct((rows, columns), BF16) for rows in message_rows],
        compiler_params=params(6 + routed_rows // 48),
        name="hand_on",
    )(norms, hidden_out, turned, *features_in, *relays)
    features_moved = spread(features_in)
    norms = lax.all_to_all(norms, AXES, split_axis=0, concat_axis=0, tiled=True)
    messages_in = [messages[0]] + [swap(messages[d], "island", d) for d in range(1, islands)]

    scaled, notes = pl.pallas_call(
        lambda *refs: average_kernel(islands, entries, 2, *refs),
        in_specs=[VMEM] * (4 + islands),
        out_specs=[VMEM] * 2,
        out_shape=[
            jax.ShapeDtypeStruct((half, columns), F32),
            jax.ShapeDtypeStruct((devices, 8, 128), F32),
        ],
        scratch_shapes=[pltpu.VMEM((half, columns), F32), pltpu.VMEM((1, columns), F32)],
        compiler_params=params(8 + routed_rows // 48),
        name="average_block",
    )(norms, drift_sum, features_in, features_moved, *messages_in)
    notes = lax.all_to_all(notes, AXES, split_axis=0, concat_axis=0, tiled=True)

    sent = scaled.astype(WIRE)
    values, last = {(0, 0): scaled}, {}
    steps = [1, 2] if handed else range(1, islands)
    for d in steps:
        values[d, 0] = swap(sent, "island", d)
    if handed:
        nothing = jnp.minimum(notes[0, 1, 0], 0.0).astype(WIRE)
        last[3, 0] = swap(values[1, 0][:handed] + nothing, "island", 2)
        last[3, handed] = swap(values[2, 0][handed:] + nothing, "island", 1)
    outs = []
    for values, cost, cuts in ((values, 12, 2), (last, 3, 2)):
        if not values:
            continue
        outs = pl.pallas_call(
            functools.partial(update_kernel, entries, list(values), cuts),
            in_specs=[VMEM, ANY] + [VMEM] * len(values) + [ANY] * len(outs),
            out_specs=[ANY, ANY],
            out_shape=[
                jax.ShapeDtypeStruct(momentum.shape, F32),
                jax.ShapeDtypeStruct(momentum.shape, BF16),
            ],
            scratch_shapes=[
                pltpu.VMEM((len(values), *next(iter(values.values())).shape), F32),
                pltpu.VMEM((len(values), *next(iter(values.values())).shape), BF16),
                pltpu.SemaphoreType.DMA((len(values) * cuts,)),
                pltpu.SemaphoreType.DMA((len(values) * cuts, 2)),
            ],
            input_output_aliases={2 + len(values) + n: n for n in range(len(outs))},
            cost_estimate=pl.CostEstimate(
                flops=0, bytes_accessed=cost * momentum.size, transcendentals=0
            ),
            compiler_params=params(50),
            name="update_pieces",
        )(notes, momentum, *[v.astype(F32) for v in values.values()], *outs)
    return tuple(outs)


def solution(mesh):
    return jax.shard_map(
        body,
        mesh=mesh,
        in_specs=(
            P("island", "expert", "tensor"),
            P("island", "expert", "tensor"),
            P("island", "expert", None, None),
            P("island", "expert", None),
            P("island", "expert", None, None),
            P("island", "expert", None, "tensor"),
            P("island", "expert", "tensor", None),
            P("island", "expert", None, "tensor"),
            P("expert", None, "tensor"),
        ),
        out_specs=(P("expert", None, "tensor"), P("expert", None, "tensor")),
        check_vma=False,
    )
```

```python
import functools
import math

import jax
import jax.numpy as jnp
from jax import lax
from jax.experimental import pallas as pl
from jax.experimental.pallas import tpu as pltpu
from jax.sharding import PartitionSpec as P

F32 = jnp.float32
BF16 = jnp.bfloat16
WIRE = jnp.float16
AXES = ("island", "expert", "tensor")

VMEM = pl.BlockSpec(memory_space=pltpu.VMEM)
ANY = pl.BlockSpec(memory_space=pl.ANY)


def params(mib):
    return pltpu.CompilerParams(vmem_limit_bytes=mib << 20)


def partner(at, step, size):
    return at ^ step if size & (size - 1) == 0 else (at + step) % size


def origin(at, step, size):
    return at ^ step if size & (size - 1) == 0 else (at - step) % size


def swap(value, axis, step):
    size = lax.axis_size(axis)
    return lax.ppermute(value, axis, [(at, partner(at, step, size)) for at in range(size)])


def position():
    island, expert, part = (lax.axis_index(a) for a in AXES)
    across = lax.axis_size("island") // lax.axis_size("tensor")
    return expert, part, lax.rem(island, across), island, across, part == lax.div(island, across)


def dot(a, b, contract):
    return lax.dot_general(a, b, (contract, ((), ())), preferred_element_type=F32)


def copy_all(sems, pairs):
    copies = [pltpu.make_async_copy(*pair, sems.at[n]) for n, pair in enumerate(pairs)]
    for copy in copies:
        copy.start()
    return copies


def pick_kernel(experts, *refs):
    spot = position()
    sources, outs = refs[:5], refs[5 : 5 + experts]
    table, count, weight, tokens, grads, sems = refs[5 + experts :]
    loads = copy_all(sems, list(zip(sources, refs[5 + experts : -1])))
    for copy in loads:
        copy.wait()
    slots = table.shape[-1]
    rows = lax.broadcasted_iota(jnp.int32, (slots, slots), 0)
    lanes = lax.broadcasted_iota(jnp.int32, (slots, slots), 1)

    def column(row):
        return jnp.sum(jnp.where(rows == lanes, row, 0), axis=1, keepdims=True)

    for d in range(experts):
        to = partner(spot[0], d, experts)
        live = lax.broadcasted_iota(jnp.int32, (slots, 1), 0) < count[0, 0, to]
        token = column(table[0, 0, pl.ds(to, 1), :].astype(F32)).astype(jnp.int32)
        chance = column(weight[0, 0, pl.ds(to, 1), :])
        ids = lax.broadcasted_iota(jnp.int32, (slots, tokens.shape[1]), 1)
        picks = jnp.where((ids == token) & live, 1.0, 0.0).astype(BF16)
        outs[d][:slots, :] = dot(picks, tokens[0], ((1,), (0,))).astype(BF16)
        chosen = dot(picks, grads[0], ((1,), (0,)))
        outs[d][slots:, :] = (chance * chosen).astype(BF16)


def cut_kernel(islands, pieces, drift, *refs):
    spot = position()
    *blocks, sems = refs
    rows, columns = blocks[0].shape
    pairs = []
    for d, first, count_rows, target, at_row in pieces:
        at = partner(spot[3], d, islands)
        top = pl.multiple_of(lax.div(at, spot[4]) * rows + first, 32)
        left = pl.multiple_of(lax.rem(at, spot[4]) * columns, columns)
        source = drift.at[0, 0, pl.ds(top, count_rows), pl.ds(left, columns)]
        pairs.append((source, blocks[target].at[pl.ds(at_row, count_rows)]))
    for copy in copy_all(sems, pairs):
        copy.wait()


def gather_kernel(count, *refs):
    arrived, (inputs, grads) = refs[:count], refs[count:]
    slots = arrived[0].shape[0] // 2
    for n, piece in enumerate(arrived):
        inputs[n * slots : (n + 1) * slots, :] = piece[:slots, :]
        grads[n * slots : (n + 1) * slots, :] = piece[slots:, :]


def join_kernel(parts, blocks, *refs):
    spot = position()
    away = spot[1] ^ lax.div(spot[3], spot[4])
    joined, drifts = refs[:parts], refs[parts : parts + blocks]
    shares, (drift_sum, *relays) = refs[parts + blocks :][:parts], refs[parts + blocks :][parts:]
    rows = drift_sum.shape[0]
    for n, ref in enumerate(relays):
        ref[...] = drifts[1 + n][rows:, :]
    size = shares[0].shape[0]
    first = pl.multiple_of(spot[1] * size, size)

    def take(share, source):
        share[...] = source[:, pl.ds(first, size)].T

    for r in range(parts):
        for t in range(parts):
            pl.when(partner(away, r, parts) == t)(functools.partial(take, shares[r], joined[t]))
    added = drifts[0][...].astype(F32)
    for other in drifts[1:]:
        added = added + other[:rows, :].astype(F32)
    drift_sum[...] = added


def hidden_kernel(parts, islands, tails, gate, down, *refs):
    spot = position()
    inputs, grads, refs = refs[:parts], refs[parts : 2 * parts], refs[2 * parts :]
    relays, (*messages, norms, hidden) = refs[: len(tails)], refs[len(tails) :]
    across, slots, columns = hidden.shape
    half = inputs[0].shape[1]
    starts = [pl.multiple_of(origin(spot[1], t, parts) * half, half) for t in range(parts)]
    hidden_gram = 0.0
    for r in range(across):
        first = r * columns
        value = 0.0
        back = 0.0
        for t in range(parts):
            block = gate[0, 0, pl.ds(starts[t], half), first : first + columns]
            value = value + dot(inputs[t][...], block, ((1,), (0,)))
            block = down[0, 0, first : first + columns, pl.ds(starts[t], half)]
            back = back + dot(grads[t][...], block, ((1,), (1,)))
        rounded = (back * (value / (1.0 + jnp.exp(-value)))).astype(BF16)
        hidden[r] = rounded
        hidden_gram = hidden_gram + dot(rounded, rounded, ((1,), (1,)))
    for d, message in enumerate(messages):
        block = lax.rem(partner(spot[3], d, islands), across)
        message[:slots, :] = hidden[pl.ds(block, 1)][0]
        if d in tails:
            message[slots:, :] = relays[tails.index(d)][...]
    input_gram = 0.0
    for t in range(parts):
        features = inputs[t][...]
        input_gram = input_gram + dot(features, features, ((1,), (1,)))
    norms[...] = jnp.full(norms.shape, jnp.sum(hidden_gram * input_gram), F32)


def average_kernel(islands, entries, norms, drift_sum, *refs):
    spot = position()
    mine, other, messages = refs[:islands], refs[islands : islands + 3], refs[islands + 3 : 2 * islands + 3]
    scaled, notes, total, square = refs[2 * islands + 3 :]
    rows, slots = mine[0].shape
    group = norms.shape[0] // islands

    def moved(d):
        if d == 0:
            return other[0][...]
        split = other[1].shape[0]
        first, last = (d - 1) * rows, d * rows
        above = other[1][first : min(last, split), :] if first < split else None
        below = other[2][max(first - split, 0) : last - split, :] if last > split else None
        found = [v for v in (above, below) if v is not None]
        return found[0] if len(found) == 1 else jnp.concatenate(found)

    scales = []
    for d in range(islands):
        at = origin(spot[3], d, islands)
        norm = jnp.sum(norms[pl.ds(at * group, group)], axis=0)[:1, :1]
        scales.append(jnp.minimum(1.0, math.sqrt(entries) / jnp.sqrt(norm + 1e-06)) / islands)
    handed = [m for m in messages[:0:-1] if m.shape[0] > slots]

    def compute(at):
        squares = 0.0
        for m in range(2):
            part = slice(m * rows, (m + 1) * rows)
            average = drift_sum[part, :]
            if handed:
                size = handed[0].shape[0] - slots
                n, first = divmod(m * rows, size)
                first += slots
                average = average + handed[n][first : first + rows, :].astype(F32)
            average = average * (1.0 / islands)
            for d in range(islands):
                factor = messages[d][:slots, :]
                average = average + scales[d] * dot(mine[d][...] if m == at else moved(d), factor, ((1,), (0,)))
            total[part, :] = average
            squares = squares + jnp.sum(average * average, axis=0, keepdims=True)
        square[...] = squares

    for at in range(2):
        pl.when(spot[1] == at)(functools.partial(compute, at))
    peak = jnp.max(jnp.abs(total[...]))
    unit = jnp.maximum(peak, 1e-30) / 32768
    value = total[...] * (1 / unit)
    spread_out = value * 8193.0
    value = spread_out - (spread_out - value)
    scaled[...] = jnp.where(jnp.abs(value) < 2.0**-13, 0.0, value)
    sublane = lax.broadcasted_iota(jnp.int32, notes.shape, 1)
    notes[...] = jnp.where(sublane == 0, jnp.sum(square[...]), unit)


def hand_kernel(count, norms, *refs):
    shares, (_, top, bottom, passed) = refs[:count], refs[count:]
    passed[...] = norms[...]
    size = shares[0].shape[0]
    split = top.shape[0]
    for n, share in enumerate(shares):
        cut = min(max(split - n * size, 0), size)
        if cut:
            top[n * size : n * size + cut, :] = share[:cut, :]
        if cut < size:
            first = n * size + cut - split
            bottom[first : first + size - cut, :] = share[cut:, :]


def own_kernel(slots, block, slots_out, block_out):
    slots_out[...] = slots[...]
    block_out[...] = block[...]


def update_kernel(entries, pieces, cuts, notes, momentum, *refs):
    values = refs[: len(pieces)]
    new_momentum, outer_step, moved, step, in_sems, sems = refs[-6:]
    expert, part, _, island, across, _ = position()
    islands, experts, devices = (lax.axis_size(a) for a in AXES)
    rows, columns = values[0].shape
    half = momentum.shape[1] // devices
    size = rows // cuts
    parts = [(n, m) for n in range(len(pieces)) for m in range(cuts)]
    spots, loads = [], []
    for i, (n, m) in enumerate(parts):
        d, first = pieces[n]
        at = origin(island, d, islands)
        top = pl.multiple_of(lax.div(at, across) * half + first + m * size, 32)
        left = pl.multiple_of(lax.rem(at, across) * columns, columns)
        spots.append((0, pl.ds(top, size), pl.ds(left, columns)))
        here = moved.at[n, pl.ds(m * size, size)]
        loads.append(pltpu.make_async_copy(momentum.at[spots[i]], here, in_sems.at[i]))
        loads[-1].start()
    square = jnp.sum(notes[...], axis=0)[:1, :1]
    clip = jnp.minimum(1.0, 0.25 * math.sqrt(entries) / jnp.sqrt(square + 1e-06))
    stored = []
    for i, (n, m) in enumerate(parts):
        at = (origin(island, pieces[n][0], islands) * experts + expert) * devices + part
        unit = notes[pl.ds(at, 1)][0, 1:2, :1]
        here = slice(m * size, (m + 1) * size)
        clipped = (clip * unit) * values[n][here, :]
        loads[i].wait()
        fresh = 0.9 * moved[n, here, :] + clipped
        moved[n, here, :] = fresh
        step[n, here, :] = (0.7 * (clipped + 0.9 * fresh)).astype(BF16)
        for k, (held, out) in enumerate(((moved, new_momentum), (step, outer_step))):
            held = held.at[n, pl.ds(m * size, size)]
            stored.append(pltpu.make_async_copy(held, out.at[spots[i]], sems.at[i, k]))
            stored[-1].start()
    for copy in stored:
        copy.wait()


def body(
    tokens,
    token_grads,
    slot_token,
    slot_count,
    slot_prob,
    gate_weight,
    down_weight,
    drift,
    momentum,
):
    islands, experts, parts = (lax.axis_size(a) for a in AXES)
    devices = islands * experts * parts
    features, hidden = gate_weight.shape[2:]
    half = features // parts
    across = islands // parts
    columns = hidden // across
    entries = features * hidden * experts * parts
    slots = slot_token.shape[3]
    routed_rows = experts * slots
    holder = lax.axis_index("island") // across
    handed = half // 2 if islands == 4 else 0
    steps = [0, 1, 2] if handed else list(range(islands))
    pieces = [(d, 0, half, n, 0) for n, d in enumerate(steps)]
    if handed:
        pieces += [(3, 0, handed, 1, half), (3, handed, handed, 2, half)]
    block_rows = [half + (handed if d else 0) for d in steps]
    picked = pl.pallas_call(
        lambda *refs: pick_kernel(experts, *refs),
        in_specs=[ANY] * 5,
        out_specs=[VMEM] * experts,
        out_shape=[jax.ShapeDtypeStruct((2 * slots, half), BF16)] * experts,
        scratch_shapes=[
            pltpu.VMEM(slot_token.shape, jnp.int32),
            pltpu.SMEM(slot_count.shape, jnp.int32),
            pltpu.VMEM(slot_prob.shape, F32),
            pltpu.VMEM(tokens.shape, BF16),
            pltpu.VMEM(token_grads.shape, BF16),
            pltpu.SemaphoreType.DMA((5,)),
        ],
        compiler_params=params(56),
        name="pick_slots",
    )(slot_token, slot_count, slot_prob, tokens, token_grads)
    blocks = pl.pallas_call(
        lambda *refs: cut_kernel(islands, pieces, *refs),
        in_specs=[ANY],
        out_specs=[VMEM] * len(steps),
        out_shape=[jax.ShapeDtypeStruct((rows, columns), BF16) for rows in block_rows],
        scratch_shapes=[pltpu.SemaphoreType.DMA((len(pieces),))],
        compiler_params=params(50),
        name="cut_drift",
    )(drift)
    arrived = [picked[0]] + [swap(picked[d], "expert", d) for d in range(experts - 1, 0, -1)]
    drift_in = [blocks[0]] + [swap(blocks[d], "island", d) for d in steps[1:]]
    arrived[0], drift_in[0] = pl.pallas_call(
        own_kernel,
        in_specs=[VMEM] * 2,
        out_specs=[VMEM] * 2,
        out_shape=[
            jax.ShapeDtypeStruct((2 * slots, half), BF16),
            jax.ShapeDtypeStruct((half, columns), BF16),
        ],
        compiler_params=params(6),
        name="own_parts",
    )(arrived[0], drift_in[0])
    rows_block = jax.ShapeDtypeStruct((routed_rows, half), BF16)
    inputs, grads = pl.pallas_call(
        lambda *refs: gather_kernel(experts, *refs),
        in_specs=[VMEM] * experts,
        out_specs=[VMEM] * 2,
        out_shape=[rows_block] * 2,
        compiler_params=params(6 + routed_rows // 48),
        name="gather_slots",
    )(*arrived)

    inputs_all = [inputs] + [swap(inputs, "tensor", t) for t in range(1, parts)]
    grads_all = [grads] + [swap(grads, "tensor", t) for t in range(1, parts)]
    share = jax.ShapeDtypeStruct((half // parts, routed_rows), BF16)
    outputs = pl.pallas_call(
        lambda *refs: join_kernel(parts, len(steps), *refs),
        in_specs=[VMEM] * (parts + len(steps)),
        out_specs=[VMEM] * (parts + (3 if handed else 1)),
        out_shape=[share] * parts
        + [jax.ShapeDtypeStruct((half, columns), F32)]
        + [jax.ShapeDtypeStruct((handed, columns), BF16)] * (2 if handed else 0),
        compiler_params=params(14 + routed_rows // 48),
        name="join_blocks",
    )(*inputs_all, *drift_in)
    shares, (drift_sum, *relays) = outputs[:parts], outputs[parts:]

    own_moved = swap(shares[0], "tensor", 1)
    features_in = [swap(shares[d // across], "island", d) for d in range(1, islands)]

    tails = [2, 1] if handed else []
    message_rows = [routed_rows + (half - handed if d in tails else 0) for d in range(islands)]
    *messages, norms = pl.pallas_call(
        lambda *refs: hidden_kernel(parts, islands, tails, *refs),
        in_specs=[VMEM] * (2 + 2 * parts + len(tails)),
        out_specs=[VMEM] * (islands + 1),
        out_shape=[jax.ShapeDtypeStruct((rows, columns), BF16) for rows in message_rows]
        + [jax.ShapeDtypeStruct((devices, 8, 128), F32)],
        scratch_shapes=[pltpu.VMEM((across, routed_rows, columns), BF16)],
        compiler_params=params(18 + routed_rows // 48),
        name="hidden_grads",
    )(gate_weight, down_weight, *inputs_all, *grads_all, *relays)
    messages_in = [messages[0]] + [swap(messages[d], "island", d) for d in range(1, islands)]

    middle = (islands - 1) * (half // parts) // 2
    *halves, norms = pl.pallas_call(
        lambda *refs: hand_kernel(islands - 1, *refs),
        in_specs=[VMEM] * islands + [ANY],
        out_specs=[VMEM] * 3,
        out_shape=[jax.ShapeDtypeStruct((middle, routed_rows), BF16)] * 2
        + [jax.ShapeDtypeStruct(norms.shape, F32)],
        compiler_params=params(4 + routed_rows // 48),
        name="hand_on",
    )(norms, *features_in, own_moved)
    halves_moved = [swap(v, "tensor", 1) for v in halves]
    norms = lax.all_to_all(norms, AXES, split_axis=0, concat_axis=0, tiled=True)

    scaled, notes = pl.pallas_call(
        lambda *refs: average_kernel(islands, entries, *refs),
        in_specs=[VMEM] * (5 + 2 * islands),
        out_specs=[VMEM] * 2,
        out_shape=[
            jax.ShapeDtypeStruct((half, columns), F32),
            jax.ShapeDtypeStruct((devices, 8, 128), F32),
        ],
        scratch_shapes=[pltpu.VMEM((half, columns), F32), pltpu.VMEM((1, columns), F32)],
        compiler_params=params(8 + routed_rows // 48),
        name="average_block",
    )(norms, drift_sum, shares[0], *features_in, own_moved, *halves_moved, *messages_in)
    notes = lax.all_to_all(notes, AXES, split_axis=0, concat_axis=0, tiled=True)

    sent = scaled.astype(WIRE)
    values, last = {(0, 0): scaled}, {}
    steps = [1, 2] if handed else range(1, islands)
    for d in steps:
        values[d, 0] = swap(sent, "island", d)
    if handed:
        nothing = jnp.minimum(notes[0, 1, 0], 0.0).astype(WIRE)
        last[3, 0] = swap(values[1, 0][:handed] + nothing, "island", 2)
        last[3, handed] = swap(values[2, 0][handed:] + nothing, "island", 1)
    outs = []
    for values, cost, cuts in ((values, 12, 2), (last, 3, 2)):
        if not values:
            continue
        outs = pl.pallas_call(
            functools.partial(update_kernel, entries, list(values), cuts),
            in_specs=[VMEM, ANY] + [VMEM] * len(values) + [ANY] * len(outs),
            out_specs=[ANY, ANY],
            out_shape=[
                jax.ShapeDtypeStruct(momentum.shape, F32),
                jax.ShapeDtypeStruct(momentum.shape, BF16),
            ],
            scratch_shapes=[
                pltpu.VMEM((len(values), *next(iter(values.values())).shape), F32),
                pltpu.VMEM((len(values), *next(iter(values.values())).shape), BF16),
                pltpu.SemaphoreType.DMA((len(values) * cuts,)),
                pltpu.SemaphoreType.DMA((len(values) * cuts, 2)),
            ],
            input_output_aliases={2 + len(values) + n: n for n in range(len(outs))},
            cost_estimate=pl.CostEstimate(
                flops=0, bytes_accessed=cost * momentum.size, transcendentals=0
            ),
            compiler_params=params(50),
            name="update_pieces",
        )(notes, momentum, *[v.astype(F32) for v in values.values()], *outs)
    return tuple(outs)


def solution(mesh):
    return jax.shard_map(
        body,
        mesh=mesh,
        in_specs=(
            P("island", "expert", "tensor"),
            P("island", "expert", "tensor"),
            P("island", "expert", None, None),
            P("island", "expert", None),
            P("island", "expert", None, None),
            P("island", "expert", None, "tensor"),
            P("island", "expert", "tensor", None),
            P("island", "expert", None, "tensor"),
            P("expert", None, "tensor"),
        ),
        out_specs=(P("expert", None, "tensor"), P("expert", None, "tensor")),
        check_vma=False,
    )
```

```python
import functools
import math

import jax
import jax.numpy as jnp
from jax import lax
from jax.experimental import pallas as pl
from jax.experimental.pallas import tpu as pltpu
from jax.sharding import PartitionSpec as P

F32 = jnp.float32
BF16 = jnp.bfloat16
WIRE = jnp.float16
AXES = ("island", "expert", "tensor")

VMEM = pl.BlockSpec(memory_space=pltpu.VMEM)
ANY = pl.BlockSpec(memory_space=pl.ANY)


def params(mib):
    return pltpu.CompilerParams(vmem_limit_bytes=mib << 20)


def partner(at, step, size):
    return at ^ step if size & (size - 1) == 0 else (at + step) % size


def origin(at, step, size):
    return at ^ step if size & (size - 1) == 0 else (at - step) % size


def swap(value, axis, step):
    size = lax.axis_size(axis)
    return lax.ppermute(value, axis, [(at, partner(at, step, size)) for at in range(size)])


def position():
    island, expert, part = (lax.axis_index(a) for a in AXES)
    across = lax.axis_size("island") // lax.axis_size("tensor")
    return expert, part, lax.rem(island, across), island, across, part == lax.div(island, across)


def dot(a, b, contract):
    return lax.dot_general(a, b, (contract, ((), ())), preferred_element_type=F32)


def copy_all(sems, pairs):
    copies = [pltpu.make_async_copy(*pair, sems.at[n]) for n, pair in enumerate(pairs)]
    for copy in copies:
        copy.start()
    return copies


def pick_kernel(experts, *refs):
    spot = position()
    sources, outs = refs[:5], refs[5 : 5 + experts]
    table, count, weight, tokens, grads, sems = refs[5 + experts :]
    loads = copy_all(sems, list(zip(sources, refs[5 + experts : -1])))
    for copy in loads:
        copy.wait()
    slots = table.shape[-1]
    rows = lax.broadcasted_iota(jnp.int32, (slots, slots), 0)
    lanes = lax.broadcasted_iota(jnp.int32, (slots, slots), 1)

    def column(row):
        return jnp.sum(jnp.where(rows == lanes, row, 0), axis=1, keepdims=True)

    for d in range(experts):
        to = partner(spot[0], d, experts)
        live = lax.broadcasted_iota(jnp.int32, (slots, 1), 0) < count[0, 0, to]
        token = column(table[0, 0, pl.ds(to, 1), :].astype(F32)).astype(jnp.int32)
        chance = column(weight[0, 0, pl.ds(to, 1), :])
        ids = lax.broadcasted_iota(jnp.int32, (slots, tokens.shape[1]), 1)
        picks = jnp.where((ids == token) & live, 1.0, 0.0).astype(BF16)
        outs[d][:slots, :] = dot(picks, tokens[0], ((1,), (0,))).astype(BF16)
        chosen = dot(picks, grads[0], ((1,), (0,)))
        outs[d][slots:, :] = (chance * chosen).astype(BF16)


def cut_kernel(islands, pieces, drift, *refs):
    spot = position()
    *blocks, sems = refs
    rows, columns = blocks[0].shape
    pairs = []
    for d, first, count_rows, target, at_row in pieces:
        at = partner(spot[3], d, islands)
        top = pl.multiple_of(lax.div(at, spot[4]) * rows + first, 32)
        left = pl.multiple_of(lax.rem(at, spot[4]) * columns, columns)
        source = drift.at[0, 0, pl.ds(top, count_rows), pl.ds(left, columns)]
        pairs.append((source, blocks[target].at[pl.ds(at_row, count_rows)]))
    for copy in copy_all(sems, pairs):
        copy.wait()


def gather_kernel(count, *refs):
    arrived, (inputs, grads) = refs[:count], refs[count:]
    slots = arrived[0].shape[0] // 2
    for n, piece in enumerate(arrived):
        inputs[n * slots : (n + 1) * slots, :] = piece[:slots, :]
        grads[n * slots : (n + 1) * slots, :] = piece[slots:, :]


def join_kernel(parts, blocks, *refs):
    spot = position()
    away = spot[1] ^ lax.div(spot[3], spot[4])
    joined, drifts = refs[:parts], refs[parts : parts + blocks]
    shares, (drift_sum, *relays) = refs[parts + blocks :][:parts], refs[parts + blocks :][parts:]
    rows = drift_sum.shape[0]
    for n, ref in enumerate(relays):
        ref[...] = drifts[1 + n][rows:, :]
    size = shares[0].shape[0]
    first = pl.multiple_of(spot[1] * size, size)

    def take(share, source):
        share[...] = source[:, pl.ds(first, size)].T

    for r in range(parts):
        for t in range(parts):
            pl.when(partner(away, r, parts) == t)(functools.partial(take, shares[r], joined[t]))
    added = drifts[0][...].astype(F32)
    for other in drifts[1:]:
        added = added + other[:rows, :].astype(F32)
    drift_sum[...] = added


def hidden_kernel(parts, islands, tails, gate, down, *refs):
    spot = position()
    inputs, grads, refs = refs[:parts], refs[parts : 2 * parts], refs[2 * parts :]
    relays, (*messages, norms, hidden) = refs[: len(tails)], refs[len(tails) :]
    across, slots, columns = hidden.shape
    half = inputs[0].shape[1]
    starts = [pl.multiple_of(origin(spot[1], t, parts) * half, half) for t in range(parts)]
    hidden_gram = 0.0
    for r in range(across):
        first = r * columns
        value = 0.0
        back = 0.0
        for t in range(parts):
            block = gate[0, 0, pl.ds(starts[t], half), first : first + columns]
            value = value + dot(inputs[t][...], block, ((1,), (0,)))
            block = down[0, 0, first : first + columns, pl.ds(starts[t], half)]
            back = back + dot(grads[t][...], block, ((1,), (1,)))
        rounded = (back * (value / (1.0 + jnp.exp(-value)))).astype(BF16)
        hidden[r] = rounded
        hidden_gram = hidden_gram + dot(rounded, rounded, ((1,), (1,)))
    for d, message in enumerate(messages):
        block = lax.rem(partner(spot[3], d, islands), across)
        message[:slots, :] = hidden[pl.ds(block, 1)][0]
        if d in tails:
            message[slots:, :] = relays[tails.index(d)][...]
    input_gram = 0.0
    for t in range(parts):
        features = inputs[t][...]
        input_gram = input_gram + dot(features, features, ((1,), (1,)))
    norms[...] = jnp.full(norms.shape, jnp.sum(hidden_gram * input_gram), F32)


def average_kernel(islands, entries, norms, drift_sum, *refs):
    spot = position()
    mine, other, messages = refs[:islands], refs[islands : islands + 3], refs[islands + 3 : 2 * islands + 3]
    scaled, notes, total, square, share, hidden, sems = refs[2 * islands + 3 :]
    loads = copy_all(sems, [(mine[0], share), (messages[0], hidden)])
    rows, slots = share.shape
    group = norms.shape[0] // islands
    split = other[1].shape[0]

    def moved(d):
        if d == 0:
            return [(0, rows, other[0], 0)]
        first, last = (d - 1) * rows, d * rows
        cut = min(max(split - first, 0), rows)
        found = [(0, cut, other[1], first), (cut, rows, other[2], first + cut - split)]
        return [part for part in found if part[0] < part[1]]

    scales = []
    for d in range(islands):
        at = origin(spot[3], d, islands)
        norm = jnp.sum(norms[pl.ds(at * group, group)], axis=0)[:1, :1]
        scales.append(jnp.minimum(1.0, math.sqrt(entries) / jnp.sqrt(norm + 1e-06)) / islands)
    handed = [m for m in messages[:0:-1] if m.shape[0] > slots]

    def compute(at):
        for m in range(2):
            part = slice(m * rows, (m + 1) * rows)
            average = drift_sum[part, :]
            if handed:
                size = handed[0].shape[0] - slots
                n, first = divmod(m * rows, size)
                first += slots
                average = average + handed[n][first : first + rows, :].astype(F32)
            average = average * (1.0 / islands)
            pieces = []
            for d in [*range(1, islands), 0]:
                if d == 0 and m == 0:
                    for copy in loads:
                        copy.wait()
                factor = messages[d][:slots, :] if d else hidden[...]
                places = moved(d)
                if m == at:
                    places = [(0, rows, mine[d] if d else share, 0)]
                if len(places) > 1:
                    pieces += [(place, scales[d], factor) for place in places]
                    continue
                block = places[0][2][places[0][3] : places[0][3] + rows, :]
                average = average + scales[d] * dot(block, factor, ((1,), (0,)))
            total[part, :] = average
            for (low, high, ref, first), scale, factor in pieces:
                block = ref[first : first + high - low, :]
                here = slice(m * rows + low, m * rows + high)
                total[here, :] += scale * dot(block, factor, ((1,), (0,)))
        square[...] = jnp.sum(total[...] * total[...], axis=0, keepdims=True)

    for at in range(2):
        pl.when(spot[1] == at)(functools.partial(compute, at))
    peak = jnp.max(jnp.abs(total[...]))
    unit = jnp.maximum(peak, 1e-30) / 32768
    value = total[...] * (1 / unit)
    spread_out = value * 8193.0
    value = spread_out - (spread_out - value)
    scaled[...] = jnp.where(jnp.abs(value) < 2.0**-13, 0.0, value)
    sublane = lax.broadcasted_iota(jnp.int32, notes.shape, 1)
    notes[...] = jnp.where(sublane == 0, jnp.sum(square[...]), unit)


def hand_kernel(count, norms, *refs):
    shares, (_, top, bottom, passed) = refs[:count], refs[count:]
    passed[...] = norms[...]
    size = shares[0].shape[0]
    split = top.shape[0]
    for n, share in enumerate(shares):
        cut = min(max(split - n * size, 0), size)
        if cut:
            top[n * size : n * size + cut, :] = share[:cut, :]
        if cut < size:
            first = n * size + cut - split
            bottom[first : first + size - cut, :] = share[cut:, :]


def own_kernel(slots, block, slots_out, block_out):
    slots_out[...] = slots[...]
    block_out[...] = block[...]


def update_kernel(entries, pieces, cuts, notes, momentum, *refs):
    values = refs[: len(pieces)]
    new_momentum, outer_step, moved, step, in_sems, sems = refs[-6:]
    expert, part, _, island, across, _ = position()
    islands, experts, devices = (lax.axis_size(a) for a in AXES)
    rows, columns = values[0].shape
    half = momentum.shape[1] // devices
    size = rows // cuts
    parts = [(n, m) for n in range(len(pieces)) for m in range(cuts)]
    spots, loads = [], []
    for i, (n, m) in enumerate(parts):
        d, first = pieces[n]
        at = origin(island, d, islands)
        top = pl.multiple_of(lax.div(at, across) * half + first + m * size, 32)
        left = pl.multiple_of(lax.rem(at, across) * columns, columns)
        spots.append((0, pl.ds(top, size), pl.ds(left, columns)))
        here = moved.at[n, pl.ds(m * size, size)]
        loads.append(pltpu.make_async_copy(momentum.at[spots[i]], here, in_sems.at[i]))
        loads[-1].start()
    square = jnp.sum(notes[...], axis=0)[:1, :1]
    clip = jnp.minimum(1.0, 0.25 * math.sqrt(entries) / jnp.sqrt(square + 1e-06))
    stored = []
    for i, (n, m) in enumerate(parts):
        at = (origin(island, pieces[n][0], islands) * experts + expert) * devices + part
        unit = notes[pl.ds(at, 1)][0, 1:2, :1]
        here = slice(m * size, (m + 1) * size)
        clipped = (clip * unit) * values[n][here, :]
        loads[i].wait()
        fresh = 0.9 * moved[n, here, :] + clipped
        moved[n, here, :] = fresh
        step[n, here, :] = (0.7 * (clipped + 0.9 * fresh)).astype(BF16)
        for k, (held, out) in enumerate(((moved, new_momentum), (step, outer_step))):
            held = held.at[n, pl.ds(m * size, size)]
            stored.append(pltpu.make_async_copy(held, out.at[spots[i]], sems.at[i, k]))
            stored[-1].start()
    for copy in stored:
        copy.wait()


def body(
    tokens,
    token_grads,
    slot_token,
    slot_count,
    slot_prob,
    gate_weight,
    down_weight,
    drift,
    momentum,
):
    islands, experts, parts = (lax.axis_size(a) for a in AXES)
    devices = islands * experts * parts
    features, hidden = gate_weight.shape[2:]
    half = features // parts
    across = islands // parts
    columns = hidden // across
    entries = features * hidden * experts * parts
    slots = slot_token.shape[3]
    routed_rows = experts * slots
    holder = lax.axis_index("island") // across
    handed = half // 2 if islands == 4 else 0
    steps = [0, 1, 2] if handed else list(range(islands))
    pieces = [(d, 0, half, n, 0) for n, d in enumerate(steps)]
    if handed:
        pieces += [(3, 0, handed, 1, half), (3, handed, handed, 2, half)]
    block_rows = [half + (handed if d else 0) for d in steps]
    picked = pl.pallas_call(
        lambda *refs: pick_kernel(experts, *refs),
        in_specs=[ANY] * 5,
        out_specs=[VMEM] * experts,
        out_shape=[jax.ShapeDtypeStruct((2 * slots, half), BF16)] * experts,
        scratch_shapes=[
            pltpu.VMEM(slot_token.shape, jnp.int32),
            pltpu.SMEM(slot_count.shape, jnp.int32),
            pltpu.VMEM(slot_prob.shape, F32),
            pltpu.VMEM(tokens.shape, BF16),
            pltpu.VMEM(token_grads.shape, BF16),
            pltpu.SemaphoreType.DMA((5,)),
        ],
        compiler_params=params(56),
        name="pick_slots",
    )(slot_token, slot_count, slot_prob, tokens, token_grads)
    blocks = pl.pallas_call(
        lambda *refs: cut_kernel(islands, pieces, *refs),
        in_specs=[ANY],
        out_specs=[VMEM] * len(steps),
        out_shape=[jax.ShapeDtypeStruct((rows, columns), BF16) for rows in block_rows],
        scratch_shapes=[pltpu.SemaphoreType.DMA((len(pieces),))],
        compiler_params=params(50),
        name="cut_drift",
    )(drift)
    arrived = [picked[0]] + [swap(picked[d], "expert", d) for d in range(experts - 1, 0, -1)]
    drift_in = [blocks[0]] + [swap(blocks[d], "island", d) for d in steps[1:]]
    arrived[0], drift_in[0] = pl.pallas_call(
        own_kernel,
        in_specs=[VMEM] * 2,
        out_specs=[VMEM] * 2,
        out_shape=[
            jax.ShapeDtypeStruct((2 * slots, half), BF16),
            jax.ShapeDtypeStruct((half, columns), BF16),
        ],
        compiler_params=params(6),
        name="own_parts",
    )(arrived[0], drift_in[0])
    rows_block = jax.ShapeDtypeStruct((routed_rows, half), BF16)
    inputs, grads = pl.pallas_call(
        lambda *refs: gather_kernel(experts, *refs),
        in_specs=[VMEM] * experts,
        out_specs=[VMEM] * 2,
        out_shape=[rows_block] * 2,
        compiler_params=params(6 + routed_rows // 48),
        name="gather_slots",
    )(*arrived)

    inputs_all = [inputs] + [swap(inputs, "tensor", t) for t in range(1, parts)]
    grads_all = [grads] + [swap(grads, "tensor", t) for t in range(1, parts)]
    share = jax.ShapeDtypeStruct((half // parts, routed_rows), BF16)
    outputs = pl.pallas_call(
        lambda *refs: join_kernel(parts, len(steps), *refs),
        in_specs=[VMEM] * (parts + len(steps)),
        out_specs=[VMEM] * (parts + (3 if handed else 1)),
        out_shape=[share] * parts
        + [jax.ShapeDtypeStruct((half, columns), F32)]
        + [jax.ShapeDtypeStruct((handed, columns), BF16)] * (2 if handed else 0),
        compiler_params=params(14 + routed_rows // 48),
        name="join_blocks",
    )(*inputs_all, *drift_in)
    shares, (drift_sum, *relays) = outputs[:parts], outputs[parts:]

    own_moved = swap(shares[0], "tensor", 1)
    features_in = [swap(shares[d // across], "island", d) for d in range(1, islands)]

    tails = [2, 1] if handed else []
    message_rows = [routed_rows + (half - handed if d in tails else 0) for d in range(islands)]
    *messages, norms = pl.pallas_call(
        lambda *refs: hidden_kernel(parts, islands, tails, *refs),
        in_specs=[VMEM] * (2 + 2 * parts + len(tails)),
        out_specs=[VMEM] * (islands + 1),
        out_shape=[jax.ShapeDtypeStruct((rows, columns), BF16) for rows in message_rows]
        + [jax.ShapeDtypeStruct((devices, 8, 128), F32)],
        scratch_shapes=[pltpu.VMEM((across, routed_rows, columns), BF16)],
        compiler_params=params(18 + routed_rows // 48),
        name="hidden_grads",
    )(gate_weight, down_weight, *inputs_all, *grads_all, *relays)
    messages_in = [messages[0]] + [swap(messages[d], "island", d) for d in range(1, islands)]

    middle = (islands - 1) * (half // parts) // 2
    *halves, norms = pl.pallas_call(
        lambda *refs: hand_kernel(islands - 1, *refs),
        in_specs=[VMEM] * islands + [ANY],
        out_specs=[VMEM] * 3,
        out_shape=[jax.ShapeDtypeStruct((middle, routed_rows), BF16)] * 2
        + [jax.ShapeDtypeStruct(norms.shape, F32)],
        compiler_params=params(4 + routed_rows // 48),
        name="hand_on",
    )(norms, *features_in, own_moved)
    halves_moved = [swap(v, "tensor", 1) for v in halves]
    norms = lax.all_to_all(norms, AXES, split_axis=0, concat_axis=0, tiled=True)

    scaled, notes = pl.pallas_call(
        lambda *refs: average_kernel(islands, entries, *refs),
        in_specs=[VMEM] * 2 + [ANY] + [VMEM] * (islands + 2) + [ANY] + [VMEM] * (islands - 1),
        out_specs=[VMEM] * 2,
        out_shape=[
            jax.ShapeDtypeStruct((half, columns), F32),
            jax.ShapeDtypeStruct((devices, 8, 128), F32),
        ],
        scratch_shapes=[
            pltpu.VMEM((half, columns), F32),
            pltpu.VMEM((1, columns), F32),
            pltpu.VMEM((half // parts, routed_rows), BF16),
            pltpu.VMEM((routed_rows, columns), BF16),
            pltpu.SemaphoreType.DMA((2,)),
        ],
        compiler_params=params(8 + routed_rows // 48),
        name="average_block",
    )(norms, drift_sum, shares[0], *features_in, own_moved, *halves_moved, *messages_in)
    notes = lax.all_to_all(notes, AXES, split_axis=0, concat_axis=0, tiled=True)

    sent = scaled.astype(WIRE)
    values, last = {(0, 0): scaled}, {}
    steps = [1, 2] if handed else range(1, islands)
    for d in steps:
        values[d, 0] = swap(sent, "island", d)
    if handed:
        nothing = jnp.minimum(notes[0, 1, 0], 0.0).astype(WIRE)
        last[3, 0] = swap(values[1, 0][:handed] + nothing, "island", 2)
        last[3, handed] = swap(values[2, 0][handed:] + nothing, "island", 1)
    outs = []
    for values, cost, cuts in ((values, 12, 2), (last, 3, 2)):
        if not values:
            continue
        outs = pl.pallas_call(
            functools.partial(update_kernel, entries, list(values), cuts),
            in_specs=[VMEM, ANY] + [VMEM] * len(values) + [ANY] * len(outs),
            out_specs=[ANY, ANY],
            out_shape=[
                jax.ShapeDtypeStruct(momentum.shape, F32),
                jax.ShapeDtypeStruct(momentum.shape, BF16),
            ],
            scratch_shapes=[
                pltpu.VMEM((len(values), *next(iter(values.values())).shape), F32),
                pltpu.VMEM((len(values), *next(iter(values.values())).shape), BF16),
                pltpu.SemaphoreType.DMA((len(values) * cuts,)),
                pltpu.SemaphoreType.DMA((len(values) * cuts, 2)),
            ],
            input_output_aliases={2 + len(values) + n: n for n in range(len(outs))},
            cost_estimate=pl.CostEstimate(
                flops=0, bytes_accessed=cost * momentum.size, transcendentals=0
            ),
            compiler_params=params(50),
            name="update_pieces",
        )(notes, momentum, *[v.astype(F32) for v in values.values()], *outs)
    return tuple(outs)


def solution(mesh):
    return jax.shard_map(
        body,
        mesh=mesh,
        in_specs=(
            P("island", "expert", "tensor"),
            P("island", "expert", "tensor"),
            P("island", "expert", None, None),
            P("island", "expert", None),
            P("island", "expert", None, None),
            P("island", "expert", None, "tensor"),
            P("island", "expert", "tensor", None),
            P("island", "expert", None, "tensor"),
            P("expert", None, "tensor"),
        ),
        out_specs=(P("expert", None, "tensor"), P("expert", None, "tensor")),
        check_vma=False,
    )
```

```python
import functools
import math

import jax
import jax.numpy as jnp
from jax import lax
from jax.experimental import pallas as pl
from jax.experimental.pallas import tpu as pltpu
from jax.sharding import PartitionSpec as P

F32 = jnp.float32
BF16 = jnp.bfloat16
WIRE = jnp.float16
AXES = ("island", "expert", "tensor")

VMEM = pl.BlockSpec(memory_space=pltpu.VMEM)
ANY = pl.BlockSpec(memory_space=pl.ANY)


def params(mib):
    return pltpu.CompilerParams(vmem_limit_bytes=mib << 20)


def partner(at, step, size):
    return at ^ step if size & (size - 1) == 0 else (at + step) % size


def origin(at, step, size):
    return at ^ step if size & (size - 1) == 0 else (at - step) % size


def swap(value, axis, step):
    size = lax.axis_size(axis)
    return lax.ppermute(value, axis, [(at, partner(at, step, size)) for at in range(size)])


def position():
    island, expert, part = (lax.axis_index(a) for a in AXES)
    across = lax.axis_size("island") // lax.axis_size("tensor")
    return expert, part, lax.rem(island, across), island, across, part == lax.div(island, across)


def dot(a, b, contract):
    return lax.dot_general(a, b, (contract, ((), ())), preferred_element_type=F32)


def copy_all(sems, pairs):
    copies = [pltpu.make_async_copy(*pair, sems.at[n]) for n, pair in enumerate(pairs)]
    for copy in copies:
        copy.start()
    return copies


def pick_kernel(experts, *refs):
    spot = position()
    sources, outs = refs[:5], refs[5 : 5 + experts]
    table, count, weight, tokens, grads, sems = refs[5 + experts :]
    loads = copy_all(sems, list(zip(sources, refs[5 + experts : -1])))
    for copy in loads:
        copy.wait()
    slots = table.shape[-1]
    rows = lax.broadcasted_iota(jnp.int32, (slots, slots), 0)
    lanes = lax.broadcasted_iota(jnp.int32, (slots, slots), 1)

    def column(row):
        return jnp.sum(jnp.where(rows == lanes, row, 0), axis=1, keepdims=True)

    for d in range(experts):
        to = partner(spot[0], d, experts)
        live = lax.broadcasted_iota(jnp.int32, (slots, 1), 0) < count[0, 0, to]
        token = column(table[0, 0, pl.ds(to, 1), :].astype(F32)).astype(jnp.int32)
        chance = column(weight[0, 0, pl.ds(to, 1), :])
        ids = lax.broadcasted_iota(jnp.int32, (slots, tokens.shape[1]), 1)
        picks = jnp.where((ids == token) & live, 1.0, 0.0).astype(BF16)
        outs[d][:slots, :] = dot(picks, tokens[0], ((1,), (0,))).astype(BF16)
        chosen = dot(picks, grads[0], ((1,), (0,)))
        outs[d][slots:, :] = (chance * chosen).astype(BF16)


def cut_kernel(islands, pieces, drift, *refs):
    spot = position()
    *blocks, sems = refs
    rows, columns = blocks[0].shape
    pairs = []
    for d, first, count_rows, target, at_row in pieces:
        at = partner(spot[3], d, islands)
        top = pl.multiple_of(lax.div(at, spot[4]) * rows + first, 32)
        left = pl.multiple_of(lax.rem(at, spot[4]) * columns, columns)
        source = drift.at[0, 0, pl.ds(top, count_rows), pl.ds(left, columns)]
        pairs.append((source, blocks[target].at[pl.ds(at_row, count_rows)]))
    for copy in copy_all(sems, pairs):
        copy.wait()


def gather_kernel(count, *refs):
    arrived, (inputs, grads) = refs[:count], refs[count:]
    slots = arrived[0].shape[0] // 2
    for n, piece in enumerate(arrived):
        inputs[n * slots : (n + 1) * slots, :] = piece[:slots, :]
        grads[n * slots : (n + 1) * slots, :] = piece[slots:, :]


def join_kernel(parts, blocks, *refs):
    spot = position()
    away = spot[1] ^ lax.div(spot[3], spot[4])
    joined, drifts = refs[:parts], refs[parts : parts + blocks]
    shares, (drift_sum, *relays) = refs[parts + blocks :][:parts], refs[parts + blocks :][parts:]
    rows = drift_sum.shape[0]
    for n, ref in enumerate(relays):
        ref[...] = drifts[1 + n][rows:, :]
    size = shares[0].shape[0]
    first = pl.multiple_of(spot[1] * size, size)

    def take(share, source):
        share[...] = source[:, pl.ds(first, size)].T

    for r in range(parts):
        for t in range(parts):
            pl.when(partner(away, r, parts) == t)(functools.partial(take, shares[r], joined[t]))
    added = drifts[0][...].astype(F32)
    for other in drifts[1:]:
        added = added + other[:rows, :].astype(F32)
    drift_sum[...] = added


def hidden_kernel(parts, islands, tails, gate, down, *refs):
    spot = position()
    inputs, grads, refs = refs[:parts], refs[parts : 2 * parts], refs[2 * parts :]
    relays, (*messages, norms, hidden) = refs[: len(tails)], refs[len(tails) :]
    across, slots, columns = hidden.shape
    half = inputs[0].shape[1]
    starts = [pl.multiple_of(origin(spot[1], t, parts) * half, half) for t in range(parts)]
    hidden_gram = 0.0
    for r in range(across):
        first = r * columns
        value = 0.0
        back = 0.0
        for t in range(parts):
            block = gate[0, 0, pl.ds(starts[t], half), first : first + columns]
            value = value + dot(inputs[t][...], block, ((1,), (0,)))
            block = down[0, 0, first : first + columns, pl.ds(starts[t], half)]
            back = back + dot(grads[t][...], block, ((1,), (1,)))
        rounded = (back * (value / (1.0 + jnp.exp(-value)))).astype(BF16)
        hidden[r] = rounded
        hidden_gram = hidden_gram + dot(rounded, rounded, ((1,), (1,)))
    for d, message in enumerate(messages):
        block = lax.rem(partner(spot[3], d, islands), across)
        message[:slots, :] = hidden[pl.ds(block, 1)][0]
        if d in tails:
            message[slots:, :] = relays[tails.index(d)][...]
    input_gram = 0.0
    for t in range(parts):
        features = inputs[t][...]
        input_gram = input_gram + dot(features, features, ((1,), (1,)))
    norms[...] = jnp.full(norms.shape, jnp.sum(hidden_gram * input_gram), F32)


def average_kernel(islands, entries, norms, drift_sum, *refs):
    spot = position()
    mine, other, messages = refs[:islands], refs[islands : islands + 3], refs[islands + 3 : 2 * islands + 3]
    scaled, notes, total, square = refs[2 * islands + 3 :]
    rows, slots = mine[0].shape
    group = norms.shape[0] // islands

    def moved(d):
        if d == 0:
            return other[0][...]
        split = other[1].shape[0]
        first, last = (d - 1) * rows, d * rows
        above = other[1][first : min(last, split), :] if first < split else None
        below = other[2][max(first - split, 0) : last - split, :] if last > split else None
        found = [v for v in (above, below) if v is not None]
        return found[0] if len(found) == 1 else jnp.concatenate(found)

    scales = []
    for d in range(islands):
        at = origin(spot[3], d, islands)
        norm = jnp.sum(norms[pl.ds(at * group, group)], axis=0)[:1, :1]
        scales.append(jnp.minimum(1.0, math.sqrt(entries) / jnp.sqrt(norm + 1e-06)) / islands)
    handed = [m for m in messages[:0:-1] if m.shape[0] > slots]

    def compute(at):
        squares = 0.0
        for m in range(2):
            part = slice(m * rows, (m + 1) * rows)
            average = drift_sum[part, :]
            if handed:
                size = handed[0].shape[0] - slots
                n, first = divmod(m * rows, size)
                first += slots
                average = average + handed[n][first : first + rows, :].astype(F32)
            average = average * (1.0 / islands)
            for d in range(islands):
                factor = messages[d][:slots, :]
                average = average + scales[d] * dot(mine[d][...] if m == at else moved(d), factor, ((1,), (0,)))
            total[part, :] = average
            squares = squares + jnp.sum(average * average, axis=0, keepdims=True)
        square[...] = squares

    for at in range(2):
        pl.when(spot[1] == at)(functools.partial(compute, at))
    peak = jnp.max(jnp.abs(total[...]))
    unit = jnp.maximum(peak, 1e-30) / 32768
    value = total[...] * (1 / unit)
    spread_out = value * 8193.0
    value = spread_out - (spread_out - value)
    scaled[...] = jnp.where(jnp.abs(value) < 2.0**-13, 0.0, value)
    sublane = lax.broadcasted_iota(jnp.int32, notes.shape, 1)
    notes[...] = jnp.where(sublane == 0, jnp.sum(square[...]), unit)


def hand_kernel(count, norms, *refs):
    shares, (_, top, bottom) = refs[:count], refs[count:]
    size = shares[0].shape[0]
    split = top.shape[0]
    for n, share in enumerate(shares):
        cut = min(max(split - n * size, 0), size)
        if cut:
            top[n * size : n * size + cut, :] = share[:cut, :]
        if cut < size:
            first = n * size + cut - split
            bottom[first : first + size - cut, :] = share[cut:, :]


def own_kernel(slots, block, slots_out, block_out):
    slots_out[...] = slots[...]
    block_out[...] = block[...]


def update_kernel(entries, pieces, cuts, notes, momentum, *refs):
    values = refs[: len(pieces)]
    new_momentum, outer_step, moved, step, in_sems, sems = refs[-6:]
    expert, part, _, island, across, _ = position()
    islands, experts, devices = (lax.axis_size(a) for a in AXES)
    rows, columns = values[0].shape
    half = momentum.shape[1] // devices
    size = rows // cuts
    parts = [(n, m) for n in range(len(pieces)) for m in range(cuts)]
    spots, loads = [], []
    for i, (n, m) in enumerate(parts):
        d, first = pieces[n]
        at = origin(island, d, islands)
        top = pl.multiple_of(lax.div(at, across) * half + first + m * size, 32)
        left = pl.multiple_of(lax.rem(at, across) * columns, columns)
        spots.append((0, pl.ds(top, size), pl.ds(left, columns)))
        here = moved.at[n, pl.ds(m * size, size)]
        loads.append(pltpu.make_async_copy(momentum.at[spots[i]], here, in_sems.at[i]))
        loads[-1].start()
    square = jnp.sum(notes[...], axis=0)[:1, :1]
    clip = jnp.minimum(1.0, 0.25 * math.sqrt(entries) / jnp.sqrt(square + 1e-06))
    stored = []
    for i, (n, m) in enumerate(parts):
        at = (origin(island, pieces[n][0], islands) * experts + expert) * devices + part
        unit = notes[pl.ds(at, 1)][0, 1:2, :1]
        here = slice(m * size, (m + 1) * size)
        clipped = (clip * unit) * values[n][here, :]
        loads[i].wait()
        fresh = 0.9 * moved[n, here, :] + clipped
        moved[n, here, :] = fresh
        step[n, here, :] = (0.7 * (clipped + 0.9 * fresh)).astype(BF16)
        for k, (held, out) in enumerate(((moved, new_momentum), (step, outer_step))):
            held = held.at[n, pl.ds(m * size, size)]
            stored.append(pltpu.make_async_copy(held, out.at[spots[i]], sems.at[i, k]))
            stored[-1].start()
    for copy in stored:
        copy.wait()


def body(
    tokens,
    token_grads,
    slot_token,
    slot_count,
    slot_prob,
    gate_weight,
    down_weight,
    drift,
    momentum,
):
    islands, experts, parts = (lax.axis_size(a) for a in AXES)
    devices = islands * experts * parts
    features, hidden = gate_weight.shape[2:]
    half = features // parts
    across = islands // parts
    columns = hidden // across
    entries = features * hidden * experts * parts
    slots = slot_token.shape[3]
    routed_rows = experts * slots
    holder = lax.axis_index("island") // across
    handed = half // 2 if islands == 4 else 0
    steps = [0, 1, 2] if handed else list(range(islands))
    pieces = [(d, 0, half, n, 0) for n, d in enumerate(steps)]
    if handed:
        pieces += [(3, 0, handed, 1, half), (3, handed, handed, 2, half)]
    block_rows = [half + (handed if d else 0) for d in steps]
    picked = pl.pallas_call(
        lambda *refs: pick_kernel(experts, *refs),
        in_specs=[ANY] * 5,
        out_specs=[VMEM] * experts,
        out_shape=[jax.ShapeDtypeStruct((2 * slots, half), BF16)] * experts,
        scratch_shapes=[
            pltpu.VMEM(slot_token.shape, jnp.int32),
            pltpu.SMEM(slot_count.shape, jnp.int32),
            pltpu.VMEM(slot_prob.shape, F32),
            pltpu.VMEM(tokens.shape, BF16),
            pltpu.VMEM(token_grads.shape, BF16),
            pltpu.SemaphoreType.DMA((5,)),
        ],
        compiler_params=params(56),
        name="pick_slots",
    )(slot_token, slot_count, slot_prob, tokens, token_grads)
    blocks = pl.pallas_call(
        lambda *refs: cut_kernel(islands, pieces, *refs),
        in_specs=[ANY],
        out_specs=[VMEM] * len(steps),
        out_shape=[jax.ShapeDtypeStruct((rows, columns), BF16) for rows in block_rows],
        scratch_shapes=[pltpu.SemaphoreType.DMA((len(pieces),))],
        compiler_params=params(50),
        name="cut_drift",
    )(drift)
    arrived = [picked[0]] + [swap(picked[d], "expert", d) for d in range(experts - 1, 0, -1)]
    drift_in = [blocks[0]] + [swap(blocks[d], "island", d) for d in steps[1:]]
    arrived[0], drift_in[0] = pl.pallas_call(
        own_kernel,
        in_specs=[VMEM] * 2,
        out_specs=[VMEM] * 2,
        out_shape=[
            jax.ShapeDtypeStruct((2 * slots, half), BF16),
            jax.ShapeDtypeStruct((half, columns), BF16),
        ],
        compiler_params=params(6),
        name="own_parts",
    )(arrived[0], drift_in[0])
    rows_block = jax.ShapeDtypeStruct((routed_rows, half), BF16)
    inputs, grads = pl.pallas_call(
        lambda *refs: gather_kernel(experts, *refs),
        in_specs=[VMEM] * experts,
        out_specs=[VMEM] * 2,
        out_shape=[rows_block] * 2,
        compiler_params=params(6 + routed_rows // 48),
        name="gather_slots",
    )(*arrived)

    inputs_all = [inputs] + [swap(inputs, "tensor", t) for t in range(1, parts)]
    grads_all = [grads] + [swap(grads, "tensor", t) for t in range(1, parts)]
    share = jax.ShapeDtypeStruct((half // parts, routed_rows), BF16)
    outputs = pl.pallas_call(
        lambda *refs: join_kernel(parts, len(steps), *refs),
        in_specs=[VMEM] * (parts + len(steps)),
        out_specs=[VMEM] * (parts + (3 if handed else 1)),
        out_shape=[share] * parts
        + [jax.ShapeDtypeStruct((half, columns), F32)]
        + [jax.ShapeDtypeStruct((handed, columns), BF16)] * (2 if handed else 0),
        compiler_params=params(14 + routed_rows // 48),
        name="join_blocks",
    )(*inputs_all, *drift_in)
    shares, (drift_sum, *relays) = outputs[:parts], outputs[parts:]

    own_moved = swap(shares[0], "tensor", 1)
    features_in = [swap(shares[d // across], "island", d) for d in range(1, islands)]

    tails = [2, 1] if handed else []
    message_rows = [routed_rows + (half - handed if d in tails else 0) for d in range(islands)]
    *messages, norms = pl.pallas_call(
        lambda *refs: hidden_kernel(parts, islands, tails, *refs),
        in_specs=[VMEM] * (2 + 2 * parts + len(tails)),
        out_specs=[VMEM] * (islands + 1),
        out_shape=[jax.ShapeDtypeStruct((rows, columns), BF16) for rows in message_rows]
        + [jax.ShapeDtypeStruct((devices, 8, 128), F32)],
        scratch_shapes=[pltpu.VMEM((across, routed_rows, columns), BF16)],
        compiler_params=params(18 + routed_rows // 48),
        name="hidden_grads",
    )(gate_weight, down_weight, *inputs_all, *grads_all, *relays)
    messages_in = [messages[0]] + [swap(messages[d], "island", d) for d in range(1, islands)]

    middle = (islands - 1) * (half // parts) // 2
    norms = lax.all_to_all(norms, AXES, split_axis=0, concat_axis=0, tiled=True)
    halves = pl.pallas_call(
        lambda *refs: hand_kernel(islands - 1, *refs),
        in_specs=[ANY] + [VMEM] * (islands - 1) + [ANY],
        out_specs=[VMEM] * 2,
        out_shape=[jax.ShapeDtypeStruct((middle, routed_rows), BF16)] * 2,
        compiler_params=params(4 + routed_rows // 48),
        name="hand_on",
    )(norms, *features_in, own_moved)
    halves_moved = [swap(v, "tensor", 1) for v in halves]

    scaled, notes = pl.pallas_call(
        lambda *refs: average_kernel(islands, entries, *refs),
        in_specs=[VMEM] * (5 + 2 * islands),
        out_specs=[VMEM] * 2,
        out_shape=[
            jax.ShapeDtypeStruct((half, columns), F32),
            jax.ShapeDtypeStruct((devices, 8, 128), F32),
        ],
        scratch_shapes=[pltpu.VMEM((half, columns), F32), pltpu.VMEM((1, columns), F32)],
        compiler_params=params(8 + routed_rows // 48),
        name="average_block",
    )(norms, drift_sum, shares[0], *features_in, own_moved, *halves_moved, *messages_in)
    notes = lax.all_to_all(notes, AXES, split_axis=0, concat_axis=0, tiled=True)

    sent = scaled.astype(WIRE)
    values, last = {(0, 0): scaled}, {}
    steps = [1, 2] if handed else range(1, islands)
    for d in steps:
        values[d, 0] = swap(sent, "island", d)
    if handed:
        nothing = jnp.minimum(notes[0, 1, 0], 0.0).astype(WIRE)
        last[3, 0] = swap(values[1, 0][:handed] + nothing, "island", 2)
        last[3, handed] = swap(values[2, 0][handed:] + nothing, "island", 1)
    outs = []
    for values, cost, cuts in ((values, 12, 2), (last, 3, 2)):
        if not values:
            continue
        outs = pl.pallas_call(
            functools.partial(update_kernel, entries, list(values), cuts),
            in_specs=[VMEM, ANY] + [VMEM] * len(values) + [ANY] * len(outs),
            out_specs=[ANY, ANY],
            out_shape=[
                jax.ShapeDtypeStruct(momentum.shape, F32),
                jax.ShapeDtypeStruct(momentum.shape, BF16),
            ],
            scratch_shapes=[
                pltpu.VMEM((len(values), *next(iter(values.values())).shape), F32),
                pltpu.VMEM((len(values), *next(iter(values.values())).shape), BF16),
                pltpu.SemaphoreType.DMA((len(values) * cuts,)),
                pltpu.SemaphoreType.DMA((len(values) * cuts, 2)),
            ],
            input_output_aliases={2 + len(values) + n: n for n in range(len(outs))},
            cost_estimate=pl.CostEstimate(
                flops=0, bytes_accessed=cost * momentum.size, transcendentals=0
            ),
            compiler_params=params(50),
            name="update_pieces",
        )(notes, momentum, *[v.astype(F32) for v in values.values()], *outs)
    return tuple(outs)


def solution(mesh):
    return jax.shard_map(
        body,
        mesh=mesh,
        in_specs=(
            P("island", "expert", "tensor"),
            P("island", "expert", "tensor"),
            P("island", "expert", None, None),
            P("island", "expert", None),
            P("island", "expert", None, None),
            P("island", "expert", None, "tensor"),
            P("island", "expert", "tensor", None),
            P("island", "expert", None, "tensor"),
            P("expert", None, "tensor"),
        ),
        out_specs=(P("expert", None, "tensor"), P("expert", None, "tensor")),
        check_vma=False,
    )
```

```python
import functools
import math

import jax
import jax.numpy as jnp
from jax import lax
from jax.experimental import pallas as pl
from jax.experimental.pallas import tpu as pltpu
from jax.sharding import PartitionSpec as P

F32 = jnp.float32
BF16 = jnp.bfloat16
WIRE = jnp.float16
AXES = ("island", "expert", "tensor")

VMEM = pl.BlockSpec(memory_space=pltpu.VMEM)
ANY = pl.BlockSpec(memory_space=pl.ANY)


def params(mib):
    return pltpu.CompilerParams(vmem_limit_bytes=mib << 20)


def partner(at, step, size):
    return at ^ step if size & (size - 1) == 0 else (at + step) % size


def origin(at, step, size):
    return at ^ step if size & (size - 1) == 0 else (at - step) % size


def swap(value, axis, step):
    size = lax.axis_size(axis)
    return lax.ppermute(value, axis, [(at, partner(at, step, size)) for at in range(size)])


def position():
    island, expert, part = (lax.axis_index(a) for a in AXES)
    across = lax.axis_size("island") // lax.axis_size("tensor")
    return expert, part, lax.rem(island, across), island, across, part == lax.div(island, across)


def dot(a, b, contract):
    return lax.dot_general(a, b, (contract, ((), ())), preferred_element_type=F32)


def copy_all(sems, pairs):
    copies = [pltpu.make_async_copy(*pair, sems.at[n]) for n, pair in enumerate(pairs)]
    for copy in copies:
        copy.start()
    return copies


def pick_kernel(experts, *refs):
    spot = position()
    sources, outs = refs[:5], refs[5 : 5 + experts]
    table, count, weight, tokens, grads, sems = refs[5 + experts :]
    loads = copy_all(sems, list(zip(sources, refs[5 + experts : -1])))
    for copy in loads:
        copy.wait()
    slots = table.shape[-1]
    rows = lax.broadcasted_iota(jnp.int32, (slots, slots), 0)
    lanes = lax.broadcasted_iota(jnp.int32, (slots, slots), 1)

    def column(row):
        return jnp.sum(jnp.where(rows == lanes, row, 0), axis=1, keepdims=True)

    for d in range(experts):
        to = partner(spot[0], d, experts)
        live = lax.broadcasted_iota(jnp.int32, (slots, 1), 0) < count[0, 0, to]
        token = column(table[0, 0, pl.ds(to, 1), :].astype(F32)).astype(jnp.int32)
        chance = column(weight[0, 0, pl.ds(to, 1), :])
        ids = lax.broadcasted_iota(jnp.int32, (slots, tokens.shape[1]), 1)
        picks = jnp.where((ids == token) & live, 1.0, 0.0).astype(BF16)
        outs[d][:slots, :] = dot(picks, tokens[0], ((1,), (0,))).astype(BF16)
        chosen = dot(picks, grads[0], ((1,), (0,)))
        outs[d][slots:, :] = (chance * chosen).astype(BF16)


def cut_kernel(islands, pieces, drift, *refs):
    spot = position()
    *blocks, sems = refs
    rows, columns = blocks[0].shape
    pairs = []
    for d, first, count_rows, target, at_row in pieces:
        at = partner(spot[3], d, islands)
        top = pl.multiple_of(lax.div(at, spot[4]) * rows + first, 32)
        left = pl.multiple_of(lax.rem(at, spot[4]) * columns, columns)
        source = drift.at[0, 0, pl.ds(top, count_rows), pl.ds(left, columns)]
        pairs.append((source, blocks[target].at[pl.ds(at_row, count_rows)]))
    for copy in copy_all(sems, pairs):
        copy.wait()


def gather_kernel(count, *refs):
    arrived, (inputs, grads) = refs[:count], refs[count:]
    slots = arrived[0].shape[0] // 2
    for n, piece in enumerate(arrived):
        inputs[n * slots : (n + 1) * slots, :] = piece[:slots, :]
        grads[n * slots : (n + 1) * slots, :] = piece[slots:, :]


def join_kernel(parts, blocks, *refs):
    spot = position()
    away = spot[1] ^ lax.div(spot[3], spot[4])
    joined, drifts = refs[:parts], refs[parts : parts + blocks]
    shares, (drift_sum, *relays) = refs[parts + blocks :][:parts], refs[parts + blocks :][parts:]
    rows = drift_sum.shape[0]
    for n, ref in enumerate(relays):
        ref[...] = drifts[1 + n][rows:, :]
    size = shares[0].shape[0]
    first = pl.multiple_of(spot[1] * size, size)

    def take(share, source):
        share[...] = source[:, pl.ds(first, size)].T

    for r in range(parts):
        for t in range(parts):
            pl.when(partner(away, r, parts) == t)(functools.partial(take, shares[r], joined[t]))
    added = drifts[0][...].astype(F32)
    for other in drifts[1:]:
        added = added + other[:rows, :].astype(F32)
    drift_sum[...] = added


def hidden_kernel(parts, islands, tails, gate, down, *refs):
    spot = position()
    inputs, grads, refs = refs[:parts], refs[parts : 2 * parts], refs[2 * parts :]
    relays, (*messages, norms, hidden) = refs[: len(tails)], refs[len(tails) :]
    across, slots, columns = hidden.shape
    half = inputs[0].shape[1]
    starts = [pl.multiple_of(origin(spot[1], t, parts) * half, half) for t in range(parts)]
    hidden_gram = 0.0
    for r in range(across):
        first = r * columns
        value = 0.0
        back = 0.0
        for t in range(parts):
            block = gate[0, 0, pl.ds(starts[t], half), first : first + columns]
            value = value + dot(inputs[t][...], block, ((1,), (0,)))
            block = down[0, 0, first : first + columns, pl.ds(starts[t], half)]
            back = back + dot(grads[t][...], block, ((1,), (1,)))
        rounded = (back * (value / (1.0 + jnp.exp(-value)))).astype(BF16)
        hidden[r] = rounded
        hidden_gram = hidden_gram + dot(rounded, rounded, ((1,), (1,)))
    for d, message in enumerate(messages):
        block = lax.rem(partner(spot[3], d, islands), across)
        message[:slots, :] = hidden[pl.ds(block, 1)][0]
        if d in tails:
            message[slots:, :] = relays[tails.index(d)][...]
    input_gram = 0.0
    for t in range(parts):
        features = inputs[t][...]
        input_gram = input_gram + dot(features, features, ((1,), (1,)))
    norms[...] = jnp.full(norms.shape, jnp.sum(hidden_gram * input_gram), F32)


def average_kernel(islands, entries, norms, drift_sum, *refs):
    spot = position()
    mine, other, messages = refs[:islands], refs[islands : islands + 3], refs[islands + 3 : 2 * islands + 3]
    scaled, notes, total, square = refs[2 * islands + 3 :]
    rows, slots = mine[0].shape
    group = norms.shape[0] // islands

    def moved(d):
        if d == 0:
            return other[0][...]
        split = other[1].shape[0]
        first, last = (d - 1) * rows, d * rows
        above = other[1][first : min(last, split), :] if first < split else None
        below = other[2][max(first - split, 0) : last - split, :] if last > split else None
        found = [v for v in (above, below) if v is not None]
        return found[0] if len(found) == 1 else jnp.concatenate(found)

    scales = []
    for d in range(islands):
        at = origin(spot[3], d, islands)
        norm = jnp.sum(norms[pl.ds(at * group, group)], axis=0)[:1, :1]
        scales.append(jnp.minimum(1.0, math.sqrt(entries) / jnp.sqrt(norm + 1e-06)) / islands)
    handed = [m for m in messages[:0:-1] if m.shape[0] > slots]

    def compute(at):
        squares = 0.0
        for m in range(2):
            part = slice(m * rows, (m + 1) * rows)
            average = drift_sum[part, :]
            if handed:
                size = handed[0].shape[0] - slots
                n, first = divmod(m * rows, size)
                first += slots
                average = average + handed[n][first : first + rows, :].astype(F32)
            average = average * (1.0 / islands)
            for d in range(islands):
                factor = messages[d][:slots, :]
                average = average + scales[d] * dot(mine[d][...] if m == at else moved(d), factor, ((1,), (0,)))
            total[part, :] = average
            squares = squares + jnp.sum(average * average, axis=0, keepdims=True)
        square[...] = squares

    for at in range(2):
        pl.when(spot[1] == at)(functools.partial(compute, at))
    peak = jnp.max(jnp.abs(total[...]))
    unit = jnp.maximum(peak, 1e-30) / 32768
    value = total[...] * (1 / unit)
    spread_out = value * 8193.0
    value = spread_out - (spread_out - value)
    scaled[...] = jnp.where(jnp.abs(value) < 2.0**-13, 0.0, value)
    sublane = lax.broadcasted_iota(jnp.int32, notes.shape, 1)
    notes[...] = jnp.where(sublane == 0, jnp.sum(square[...]), unit)


def hand_kernel(count, norms, *refs):
    shares, (_, top, bottom) = refs[:count], refs[count:]
    size = shares[0].shape[0]
    split = top.shape[0]
    for n, share in enumerate(shares):
        cut = min(max(split - n * size, 0), size)
        if cut:
            top[n * size : n * size + cut, :] = share[:cut, :]
        if cut < size:
            first = n * size + cut - split
            bottom[first : first + size - cut, :] = share[cut:, :]


def pass_kernel(norms, share, passed):
    passed[...] = norms[...]


def own_kernel(slots, block, slots_out, block_out):
    slots_out[...] = slots[...]
    block_out[...] = block[...]


def update_kernel(entries, pieces, cuts, notes, momentum, *refs):
    values = refs[: len(pieces)]
    new_momentum, outer_step, moved, step, in_sems, sems = refs[-6:]
    expert, part, _, island, across, _ = position()
    islands, experts, devices = (lax.axis_size(a) for a in AXES)
    rows, columns = values[0].shape
    half = momentum.shape[1] // devices
    size = rows // cuts
    parts = [(n, m) for n in range(len(pieces)) for m in range(cuts)]
    spots, loads = [], []
    for i, (n, m) in enumerate(parts):
        d, first = pieces[n]
        at = origin(island, d, islands)
        top = pl.multiple_of(lax.div(at, across) * half + first + m * size, 32)
        left = pl.multiple_of(lax.rem(at, across) * columns, columns)
        spots.append((0, pl.ds(top, size), pl.ds(left, columns)))
        here = moved.at[n, pl.ds(m * size, size)]
        loads.append(pltpu.make_async_copy(momentum.at[spots[i]], here, in_sems.at[i]))
        loads[-1].start()
    square = jnp.sum(notes[...], axis=0)[:1, :1]
    clip = jnp.minimum(1.0, 0.25 * math.sqrt(entries) / jnp.sqrt(square + 1e-06))
    stored = []
    for i, (n, m) in enumerate(parts):
        at = (origin(island, pieces[n][0], islands) * experts + expert) * devices + part
        unit = notes[pl.ds(at, 1)][0, 1:2, :1]
        here = slice(m * size, (m + 1) * size)
        clipped = (clip * unit) * values[n][here, :]
        loads[i].wait()
        fresh = 0.9 * moved[n, here, :] + clipped
        moved[n, here, :] = fresh
        step[n, here, :] = (0.7 * (clipped + 0.9 * fresh)).astype(BF16)
        for k, (held, out) in enumerate(((moved, new_momentum), (step, outer_step))):
            held = held.at[n, pl.ds(m * size, size)]
            stored.append(pltpu.make_async_copy(held, out.at[spots[i]], sems.at[i, k]))
            stored[-1].start()
    for copy in stored:
        copy.wait()


def body(
    tokens,
    token_grads,
    slot_token,
    slot_count,
    slot_prob,
    gate_weight,
    down_weight,
    drift,
    momentum,
):
    islands, experts, parts = (lax.axis_size(a) for a in AXES)
    devices = islands * experts * parts
    features, hidden = gate_weight.shape[2:]
    half = features // parts
    across = islands // parts
    columns = hidden // across
    entries = features * hidden * experts * parts
    slots = slot_token.shape[3]
    routed_rows = experts * slots
    holder = lax.axis_index("island") // across
    handed = half // 2 if islands == 4 else 0
    steps = [0, 1, 2] if handed else list(range(islands))
    pieces = [(d, 0, half, n, 0) for n, d in enumerate(steps)]
    if handed:
        pieces += [(3, 0, handed, 1, half), (3, handed, handed, 2, half)]
    block_rows = [half + (handed if d else 0) for d in steps]
    picked = pl.pallas_call(
        lambda *refs: pick_kernel(experts, *refs),
        in_specs=[ANY] * 5,
        out_specs=[VMEM] * experts,
        out_shape=[jax.ShapeDtypeStruct((2 * slots, half), BF16)] * experts,
        scratch_shapes=[
            pltpu.VMEM(slot_token.shape, jnp.int32),
            pltpu.SMEM(slot_count.shape, jnp.int32),
            pltpu.VMEM(slot_prob.shape, F32),
            pltpu.VMEM(tokens.shape, BF16),
            pltpu.VMEM(token_grads.shape, BF16),
            pltpu.SemaphoreType.DMA((5,)),
        ],
        compiler_params=params(56),
        name="pick_slots",
    )(slot_token, slot_count, slot_prob, tokens, token_grads)
    blocks = pl.pallas_call(
        lambda *refs: cut_kernel(islands, pieces, *refs),
        in_specs=[ANY],
        out_specs=[VMEM] * len(steps),
        out_shape=[jax.ShapeDtypeStruct((rows, columns), BF16) for rows in block_rows],
        scratch_shapes=[pltpu.SemaphoreType.DMA((len(pieces),))],
        compiler_params=params(50),
        name="cut_drift",
    )(drift)
    arrived = [picked[0]] + [swap(picked[d], "expert", d) for d in range(experts - 1, 0, -1)]
    drift_in = [blocks[0]] + [swap(blocks[d], "island", d) for d in steps[1:]]
    arrived[0], drift_in[0] = pl.pallas_call(
        own_kernel,
        in_specs=[VMEM] * 2,
        out_specs=[VMEM] * 2,
        out_shape=[
            jax.ShapeDtypeStruct((2 * slots, half), BF16),
            jax.ShapeDtypeStruct((half, columns), BF16),
        ],
        compiler_params=params(6),
        name="own_parts",
    )(arrived[0], drift_in[0])
    rows_block = jax.ShapeDtypeStruct((routed_rows, half), BF16)
    inputs, grads = pl.pallas_call(
        lambda *refs: gather_kernel(experts, *refs),
        in_specs=[VMEM] * experts,
        out_specs=[VMEM] * 2,
        out_shape=[rows_block] * 2,
        compiler_params=params(6 + routed_rows // 48),
        name="gather_slots",
    )(*arrived)

    inputs_all = [inputs] + [swap(inputs, "tensor", t) for t in range(1, parts)]
    grads_all = [grads] + [swap(grads, "tensor", t) for t in range(1, parts)]
    share = jax.ShapeDtypeStruct((half // parts, routed_rows), BF16)
    outputs = pl.pallas_call(
        lambda *refs: join_kernel(parts, len(steps), *refs),
        in_specs=[VMEM] * (parts + len(steps)),
        out_specs=[VMEM] * (parts + (3 if handed else 1)),
        out_shape=[share] * parts
        + [jax.ShapeDtypeStruct((half, columns), F32)]
        + [jax.ShapeDtypeStruct((handed, columns), BF16)] * (2 if handed else 0),
        compiler_params=params(14 + routed_rows // 48),
        name="join_blocks",
    )(*inputs_all, *drift_in)
    shares, (drift_sum, *relays) = outputs[:parts], outputs[parts:]

    own_moved = swap(shares[0], "tensor", 1)
    features_in = [swap(shares[d // across], "island", d) for d in range(1, islands)]

    tails = [2, 1] if handed else []
    message_rows = [routed_rows + (half - handed if d in tails else 0) for d in range(islands)]
    *messages, norms = pl.pallas_call(
        lambda *refs: hidden_kernel(parts, islands, tails, *refs),
        in_specs=[VMEM] * (2 + 2 * parts + len(tails)),
        out_specs=[VMEM] * (islands + 1),
        out_shape=[jax.ShapeDtypeStruct((rows, columns), BF16) for rows in message_rows]
        + [jax.ShapeDtypeStruct((devices, 8, 128), F32)],
        scratch_shapes=[pltpu.VMEM((across, routed_rows, columns), BF16)],
        compiler_params=params(18 + routed_rows // 48),
        name="hidden_grads",
    )(gate_weight, down_weight, *inputs_all, *grads_all, *relays)
    messages_in = [messages[0]] + [swap(messages[d], "island", d) for d in range(1, islands)]

    middle = (islands - 1) * (half // parts) // 2
    norms = pl.pallas_call(
        pass_kernel,
        in_specs=[VMEM, ANY],
        out_specs=VMEM,
        out_shape=jax.ShapeDtypeStruct(norms.shape, F32),
        compiler_params=params(2),
        name="pass_norms",
    )(norms, features_in[0])
    norms = lax.all_to_all(norms, AXES, split_axis=0, concat_axis=0, tiled=True)
    halves = pl.pallas_call(
        lambda *refs: hand_kernel(islands - 1, *refs),
        in_specs=[ANY] + [VMEM] * (islands - 1) + [ANY],
        out_specs=[VMEM] * 2,
        out_shape=[jax.ShapeDtypeStruct((middle, routed_rows), BF16)] * 2,
        compiler_params=params(4 + routed_rows // 48),
        name="hand_on",
    )(norms, *features_in, own_moved)
    halves_moved = [swap(v, "tensor", 1) for v in halves]

    scaled, notes = pl.pallas_call(
        lambda *refs: average_kernel(islands, entries, *refs),
        in_specs=[VMEM] * (5 + 2 * islands),
        out_specs=[VMEM] * 2,
        out_shape=[
            jax.ShapeDtypeStruct((half, columns), F32),
            jax.ShapeDtypeStruct((devices, 8, 128), F32),
        ],
        scratch_shapes=[pltpu.VMEM((half, columns), F32), pltpu.VMEM((1, columns), F32)],
        compiler_params=params(8 + routed_rows // 48),
        name="average_block",
    )(norms, drift_sum, shares[0], *features_in, own_moved, *halves_moved, *messages_in)
    notes = lax.all_to_all(notes, AXES, split_axis=0, concat_axis=0, tiled=True)

    sent = scaled.astype(WIRE)
    values, last = {(0, 0): scaled}, {}
    steps = [1, 2] if handed else range(1, islands)
    for d in steps:
        values[d, 0] = swap(sent, "island", d)
    if handed:
        nothing = jnp.minimum(notes[0, 1, 0], 0.0).astype(WIRE)
        last[3, 0] = swap(values[1, 0][:handed] + nothing, "island", 2)
        last[3, handed] = swap(values[2, 0][handed:] + nothing, "island", 1)
    outs = []
    for values, cost, cuts in ((values, 12, 2), (last, 3, 2)):
        if not values:
            continue
        outs = pl.pallas_call(
            functools.partial(update_kernel, entries, list(values), cuts),
            in_specs=[VMEM, ANY] + [VMEM] * len(values) + [ANY] * len(outs),
            out_specs=[ANY, ANY],
            out_shape=[
                jax.ShapeDtypeStruct(momentum.shape, F32),
                jax.ShapeDtypeStruct(momentum.shape, BF16),
            ],
            scratch_shapes=[
                pltpu.VMEM((len(values), *next(iter(values.values())).shape), F32),
                pltpu.VMEM((len(values), *next(iter(values.values())).shape), BF16),
                pltpu.SemaphoreType.DMA((len(values) * cuts,)),
                pltpu.SemaphoreType.DMA((len(values) * cuts, 2)),
            ],
            input_output_aliases={2 + len(values) + n: n for n in range(len(outs))},
            cost_estimate=pl.CostEstimate(
                flops=0, bytes_accessed=cost * momentum.size, transcendentals=0
            ),
            compiler_params=params(50),
            name="update_pieces",
        )(notes, momentum, *[v.astype(F32) for v in values.values()], *outs)
    return tuple(outs)


def solution(mesh):
    return jax.shard_map(
        body,
        mesh=mesh,
        in_specs=(
            P("island", "expert", "tensor"),
            P("island", "expert", "tensor"),
            P("island", "expert", None, None),
            P("island", "expert", None),
            P("island", "expert", None, None),
            P("island", "expert", None, "tensor"),
            P("island", "expert", "tensor", None),
            P("island", "expert", None, "tensor"),
            P("expert", None, "tensor"),
        ),
        out_specs=(P("expert", None, "tensor"), P("expert", None, "tensor")),
        check_vma=False,
    )
```

```python
import functools
import math

import jax
import jax.numpy as jnp
from jax import lax
from jax.experimental import pallas as pl
from jax.experimental.pallas import tpu as pltpu
from jax.sharding import PartitionSpec as P

F32 = jnp.float32
BF16 = jnp.bfloat16
WIRE = jnp.float16
AXES = ("island", "expert", "tensor")

VMEM = pl.BlockSpec(memory_space=pltpu.VMEM)
ANY = pl.BlockSpec(memory_space=pl.ANY)


def params(mib):
    return pltpu.CompilerParams(vmem_limit_bytes=mib << 20)


def partner(at, step, size):
    return at ^ step if size & (size - 1) == 0 else (at + step) % size


def origin(at, step, size):
    return at ^ step if size & (size - 1) == 0 else (at - step) % size


def swap(value, axis, step):
    size = lax.axis_size(axis)
    return lax.ppermute(value, axis, [(at, partner(at, step, size)) for at in range(size)])


def position():
    island, expert, part = (lax.axis_index(a) for a in AXES)
    across = lax.axis_size("island") // lax.axis_size("tensor")
    return expert, part, lax.rem(island, across), island, across, part == lax.div(island, across)


def dot(a, b, contract):
    return lax.dot_general(a, b, (contract, ((), ())), preferred_element_type=F32)


def copy_all(sems, pairs):
    copies = [pltpu.make_async_copy(*pair, sems.at[n]) for n, pair in enumerate(pairs)]
    for copy in copies:
        copy.start()
    return copies


def pick_kernel(experts, *refs):
    spot = position()
    sources, outs = refs[:5], refs[5 : 5 + experts]
    table, count, weight, tokens, grads, sems = refs[5 + experts :]
    loads = copy_all(sems, list(zip(sources, refs[5 + experts : -1])))
    for copy in loads:
        copy.wait()
    slots = table.shape[-1]
    rows = lax.broadcasted_iota(jnp.int32, (slots, slots), 0)
    lanes = lax.broadcasted_iota(jnp.int32, (slots, slots), 1)

    def column(row):
        return jnp.sum(jnp.where(rows == lanes, row, 0), axis=1, keepdims=True)

    for d in range(experts):
        to = partner(spot[0], d, experts)
        live = lax.broadcasted_iota(jnp.int32, (slots, 1), 0) < count[0, 0, to]
        token = column(table[0, 0, pl.ds(to, 1), :].astype(F32)).astype(jnp.int32)
        chance = column(weight[0, 0, pl.ds(to, 1), :])
        ids = lax.broadcasted_iota(jnp.int32, (slots, tokens.shape[1]), 1)
        picks = jnp.where((ids == token) & live, 1.0, 0.0).astype(BF16)
        outs[d][:slots, :] = dot(picks, tokens[0], ((1,), (0,))).astype(BF16)
        chosen = dot(picks, grads[0], ((1,), (0,)))
        outs[d][slots:, :] = (chance * chosen).astype(BF16)


def cut_kernel(islands, pieces, drift, *refs):
    spot = position()
    *blocks, sems = refs
    rows, columns = blocks[0].shape
    pairs = []
    for d, first, count_rows, target, at_row in pieces:
        at = partner(spot[3], d, islands)
        top = pl.multiple_of(lax.div(at, spot[4]) * rows + first, 32)
        left = pl.multiple_of(lax.rem(at, spot[4]) * columns, columns)
        source = drift.at[0, 0, pl.ds(top, count_rows), pl.ds(left, columns)]
        pairs.append((source, blocks[target].at[pl.ds(at_row, count_rows)]))
    for copy in copy_all(sems, pairs):
        copy.wait()


def gather_kernel(count, *refs):
    arrived, (inputs, grads) = refs[:count], refs[count:]
    slots = arrived[0].shape[0] // 2
    for n, piece in enumerate(arrived):
        inputs[n * slots : (n + 1) * slots, :] = piece[:slots, :]
        grads[n * slots : (n + 1) * slots, :] = piece[slots:, :]


def join_kernel(parts, blocks, *refs):
    spot = position()
    away = spot[1] ^ lax.div(spot[3], spot[4])
    joined, drifts = refs[:parts], refs[parts : parts + blocks]
    shares, (drift_sum, *relays) = refs[parts + blocks :][:parts], refs[parts + blocks :][parts:]
    rows = drift_sum.shape[0]
    for n, ref in enumerate(relays):
        ref[...] = drifts[1 + n][rows:, :]
    size = shares[0].shape[0]
    first = pl.multiple_of(spot[1] * size, size)

    def take(share, source):
        share[...] = source[:, pl.ds(first, size)].T

    for r in range(parts):
        for t in range(parts):
            pl.when(partner(away, r, parts) == t)(functools.partial(take, shares[r], joined[t]))
    added = drifts[0][...].astype(F32)
    for other in drifts[1:]:
        added = added + other[:rows, :].astype(F32)
    drift_sum[...] = added


def hidden_kernel(parts, islands, tails, gate, down, *refs):
    spot = position()
    inputs, grads, refs = refs[:parts], refs[parts : 2 * parts], refs[2 * parts :]
    relays, (*messages, norms, hidden) = refs[: len(tails)], refs[len(tails) :]
    across, slots, columns = hidden.shape
    half = inputs[0].shape[1]
    starts = [pl.multiple_of(origin(spot[1], t, parts) * half, half) for t in range(parts)]
    hidden_gram = 0.0
    for r in range(across):
        first = r * columns
        value = 0.0
        back = 0.0
        for t in range(parts):
            block = gate[0, 0, pl.ds(starts[t], half), first : first + columns]
            value = value + dot(inputs[t][...], block, ((1,), (0,)))
            block = down[0, 0, first : first + columns, pl.ds(starts[t], half)]
            back = back + dot(grads[t][...], block, ((1,), (1,)))
        rounded = (back * (value / (1.0 + jnp.exp(-value)))).astype(BF16)
        hidden[r] = rounded
        hidden_gram = hidden_gram + dot(rounded, rounded, ((1,), (1,)))
    for d, message in enumerate(messages):
        block = lax.rem(partner(spot[3], d, islands), across)
        message[:slots, :] = hidden[pl.ds(block, 1)][0]
        if d in tails:
            message[slots:, :] = relays[tails.index(d)][...]
    input_gram = 0.0
    for t in range(parts):
        features = inputs[t][...]
        input_gram = input_gram + dot(features, features, ((1,), (1,)))
    norms[...] = jnp.full(norms.shape, jnp.sum(hidden_gram * input_gram), F32)


def average_kernel(islands, entries, norms, drift_sum, *refs):
    spot = position()
    mine, other, messages = refs[:islands], refs[islands : islands + 3], refs[islands + 3 : 2 * islands + 3]
    scaled, notes, total, square = refs[2 * islands + 3 :]
    rows, slots = mine[0].shape
    group = norms.shape[0] // islands

    def moved(d):
        if d == 0:
            return other[0][...]
        split = other[1].shape[0]
        first, last = (d - 1) * rows, d * rows
        above = other[1][first : min(last, split), :] if first < split else None
        below = other[2][max(first - split, 0) : last - split, :] if last > split else None
        found = [v for v in (above, below) if v is not None]
        return found[0] if len(found) == 1 else jnp.concatenate(found)

    scales = []
    for d in range(islands):
        at = origin(spot[3], d, islands)
        norm = jnp.sum(norms[pl.ds(at * group, group)], axis=0)[:1, :1]
        scales.append(jnp.minimum(1.0, math.sqrt(entries) / jnp.sqrt(norm + 1e-06)) / islands)
    handed = [m for m in messages[:0:-1] if m.shape[0] > slots]

    def compute(at):
        squares = 0.0
        for m in range(2):
            part = slice(m * rows, (m + 1) * rows)
            average = drift_sum[part, :]
            if handed:
                size = handed[0].shape[0] - slots
                n, first = divmod(m * rows, size)
                first += slots
                average = average + handed[n][first : first + rows, :].astype(F32)
            average = average * (1.0 / islands)
            for d in range(islands):
                factor = messages[d][:slots, :]
                average = average + scales[d] * dot(mine[d][...] if m == at else moved(d), factor, ((1,), (0,)))
            total[part, :] = average
            squares = squares + jnp.sum(average * average, axis=0, keepdims=True)
        square[...] = squares

    for at in range(2):
        pl.when(spot[1] == at)(functools.partial(compute, at))
    peak = jnp.max(jnp.abs(total[...]))
    unit = jnp.maximum(peak, 1e-30) / 32768
    value = total[...] * (1 / unit)
    spread_out = value * 8193.0
    value = spread_out - (spread_out - value)
    scaled[...] = jnp.where(jnp.abs(value) < 2.0**-13, 0.0, value)
    sublane = lax.broadcasted_iota(jnp.int32, notes.shape, 1)
    notes[...] = jnp.where(sublane == 0, jnp.sum(square[...]), unit)


def hand_kernel(count, norms, *refs):
    shares, (_, top, bottom) = refs[:count], refs[count:]
    size = shares[0].shape[0]
    split = top.shape[0]
    for n, share in enumerate(shares):
        cut = min(max(split - n * size, 0), size)
        if cut:
            top[n * size : n * size + cut, :] = share[:cut, :]
        if cut < size:
            first = n * size + cut - split
            bottom[first : first + size - cut, :] = share[cut:, :]


def own_kernel(slots, block, slots_out, block_out):
    slots_out[...] = slots[...]
    block_out[...] = block[...]


def update_kernel(entries, pieces, cuts, notes, momentum, *refs):
    values = refs[: len(pieces)]
    new_momentum, outer_step, moved, step, in_sems, sems = refs[-6:]
    expert, part, _, island, across, _ = position()
    islands, experts, devices = (lax.axis_size(a) for a in AXES)
    rows, columns = values[0].shape
    half = momentum.shape[1] // devices
    size = rows // cuts
    parts = [(n, m) for n in range(len(pieces)) for m in range(cuts)]
    spots, loads = [], []
    for i, (n, m) in enumerate(parts):
        d, first = pieces[n]
        at = origin(island, d, islands)
        top = pl.multiple_of(lax.div(at, across) * half + first + m * size, 32)
        left = pl.multiple_of(lax.rem(at, across) * columns, columns)
        spots.append((0, pl.ds(top, size), pl.ds(left, columns)))
        here = moved.at[n, pl.ds(m * size, size)]
        loads.append(pltpu.make_async_copy(momentum.at[spots[i]], here, in_sems.at[i]))
        loads[-1].start()
    square = jnp.sum(notes[...], axis=0)[:1, :1]
    clip = jnp.minimum(1.0, 0.25 * math.sqrt(entries) / jnp.sqrt(square + 1e-06))
    stored = []
    for i, (n, m) in enumerate(parts):
        at = (origin(island, pieces[n][0], islands) * experts + expert) * devices + part
        unit = notes[pl.ds(at, 1)][0, 1:2, :1]
        here = slice(m * size, (m + 1) * size)
        clipped = (clip * unit) * values[n][here, :]
        loads[i].wait()
        fresh = 0.9 * moved[n, here, :] + clipped
        moved[n, here, :] = fresh
        step[n, here, :] = (0.7 * (clipped + 0.9 * fresh)).astype(BF16)
        for k, (held, out) in enumerate(((moved, new_momentum), (step, outer_step))):
            held = held.at[n, pl.ds(m * size, size)]
            stored.append(pltpu.make_async_copy(held, out.at[spots[i]], sems.at[i, k]))
            stored[-1].start()
    for copy in stored:
        copy.wait()


def body(
    tokens,
    token_grads,
    slot_token,
    slot_count,
    slot_prob,
    gate_weight,
    down_weight,
    drift,
    momentum,
):
    islands, experts, parts = (lax.axis_size(a) for a in AXES)
    devices = islands * experts * parts
    features, hidden = gate_weight.shape[2:]
    half = features // parts
    across = islands // parts
    columns = hidden // across
    entries = features * hidden * experts * parts
    slots = slot_token.shape[3]
    routed_rows = experts * slots
    holder = lax.axis_index("island") // across
    handed = half // 2 if islands == 4 else 0
    steps = [0, 1, 2] if handed else list(range(islands))
    pieces = [(d, 0, half, n, 0) for n, d in enumerate(steps)]
    if handed:
        pieces += [(3, 0, handed, 1, half), (3, handed, handed, 2, half)]
    block_rows = [half + (handed if d else 0) for d in steps]
    picked = pl.pallas_call(
        lambda *refs: pick_kernel(experts, *refs),
        in_specs=[ANY] * 5,
        out_specs=[VMEM] * experts,
        out_shape=[jax.ShapeDtypeStruct((2 * slots, half), BF16)] * experts,
        scratch_shapes=[
            pltpu.VMEM(slot_token.shape, jnp.int32),
            pltpu.SMEM(slot_count.shape, jnp.int32),
            pltpu.VMEM(slot_prob.shape, F32),
            pltpu.VMEM(tokens.shape, BF16),
            pltpu.VMEM(token_grads.shape, BF16),
            pltpu.SemaphoreType.DMA((5,)),
        ],
        compiler_params=params(56),
        name="pick_slots",
    )(slot_token, slot_count, slot_prob, tokens, token_grads)
    blocks = pl.pallas_call(
        lambda *refs: cut_kernel(islands, pieces, *refs),
        in_specs=[ANY],
        out_specs=[VMEM] * len(steps),
        out_shape=[jax.ShapeDtypeStruct((rows, columns), BF16) for rows in block_rows],
        scratch_shapes=[pltpu.SemaphoreType.DMA((len(pieces),))],
        compiler_params=params(50),
        name="cut_drift",
    )(drift)
    arrived = [picked[0]] + [swap(picked[d], "expert", d) for d in range(experts - 1, 0, -1)]
    drift_in = [blocks[0]] + [swap(blocks[d], "island", d) for d in steps[1:]]
    arrived[0], drift_in[0] = pl.pallas_call(
        own_kernel,
        in_specs=[VMEM] * 2,
        out_specs=[VMEM] * 2,
        out_shape=[
            jax.ShapeDtypeStruct((2 * slots, half), BF16),
            jax.ShapeDtypeStruct((half, columns), BF16),
        ],
        compiler_params=params(6),
        name="own_parts",
    )(arrived[0], drift_in[0])
    rows_block = jax.ShapeDtypeStruct((routed_rows, half), BF16)
    inputs, grads = pl.pallas_call(
        lambda *refs: gather_kernel(experts, *refs),
        in_specs=[VMEM] * experts,
        out_specs=[VMEM] * 2,
        out_shape=[rows_block] * 2,
        compiler_params=params(6 + routed_rows // 48),
        name="gather_slots",
    )(*arrived)

    inputs_all = [inputs] + [swap(inputs, "tensor", t) for t in range(1, parts)]
    grads_all = [grads] + [swap(grads, "tensor", t) for t in range(1, parts)]
    share = jax.ShapeDtypeStruct((half // parts, routed_rows), BF16)
    outputs = pl.pallas_call(
        lambda *refs: join_kernel(parts, len(steps), *refs),
        in_specs=[VMEM] * (parts + len(steps)),
        out_specs=[VMEM] * (parts + (3 if handed else 1)),
        out_shape=[share] * parts
        + [jax.ShapeDtypeStruct((half, columns), F32)]
        + [jax.ShapeDtypeStruct((handed, columns), BF16)] * (2 if handed else 0),
        compiler_params=params(14 + routed_rows // 48),
        name="join_blocks",
    )(*inputs_all, *drift_in)
    shares, (drift_sum, *relays) = outputs[:parts], outputs[parts:]

    own_moved = swap(shares[0], "tensor", 1)
    features_in = [swap(shares[d // across], "island", d) for d in range(1, islands)]

    tails = [2, 1] if handed else []
    message_rows = [routed_rows + (half - handed if d in tails else 0) for d in range(islands)]
    *messages, norms = pl.pallas_call(
        lambda *refs: hidden_kernel(parts, islands, tails, *refs),
        in_specs=[VMEM] * (2 + 2 * parts + len(tails)),
        out_specs=[VMEM] * (islands + 1),
        out_shape=[jax.ShapeDtypeStruct((rows, columns), BF16) for rows in message_rows]
        + [jax.ShapeDtypeStruct((devices, 8, 128), F32)],
        scratch_shapes=[pltpu.VMEM((across, routed_rows, columns), BF16)],
        compiler_params=params(18 + routed_rows // 48),
        name="hidden_grads",
    )(gate_weight, down_weight, *inputs_all, *grads_all, *relays)
    messages_in = [messages[0]] + [swap(messages[d], "island", d) for d in range(1, islands)]

    middle = (islands - 1) * (half // parts) // 2
    norms = lax.all_to_all(norms, AXES, split_axis=0, concat_axis=0, tiled=True)
    halves = pl.pallas_call(
        lambda *refs: hand_kernel(islands - 1, *refs),
        in_specs=[ANY] + [VMEM] * (islands - 1) + [ANY],
        out_specs=[VMEM] * 2,
        out_shape=[jax.ShapeDtypeStruct((middle, routed_rows), BF16)] * 2,
        compiler_params=params(4 + routed_rows // 48),
        name="hand_on",
    )(norms, *features_in, own_moved)
    halves_moved = [swap(v, "tensor", 1) for v in halves]

    scaled, notes = pl.pallas_call(
        lambda *refs: average_kernel(islands, entries, *refs),
        in_specs=[VMEM] * (5 + 2 * islands),
        out_specs=[VMEM] * 2,
        out_shape=[
            jax.ShapeDtypeStruct((half, columns), F32),
            jax.ShapeDtypeStruct((devices, 8, 128), F32),
        ],
        scratch_shapes=[pltpu.VMEM((half, columns), F32), pltpu.VMEM((1, columns), F32)],
        compiler_params=params(8 + routed_rows // 48),
        name="average_block",
    )(norms, drift_sum, shares[0], *features_in, own_moved, *halves_moved, *messages_in)
    notes = lax.all_to_all(notes, AXES, split_axis=0, concat_axis=0, tiled=True)

    sent = scaled.astype(WIRE)
    values, last = {(0, 0): scaled}, {}
    steps = [1, 2] if handed else range(1, islands)
    for d in steps:
        values[d, 0] = swap(sent, "island", d)
    if handed:
        nothing = jnp.minimum(notes[0, 1, 0], 0.0).astype(WIRE)
        last[3, 0] = swap(values[1, 0][:handed] + nothing, "island", 2)
        last[3, handed] = swap(values[2, 0][handed:] + nothing, "island", 1)
    outs = []
    for values, cost, cuts in ((values, 12, 4), (last, 3, 4)):
        if not values:
            continue
        outs = pl.pallas_call(
            functools.partial(update_kernel, entries, list(values), cuts),
            in_specs=[VMEM, ANY] + [VMEM] * len(values) + [ANY] * len(outs),
            out_specs=[ANY, ANY],
            out_shape=[
                jax.ShapeDtypeStruct(momentum.shape, F32),
                jax.ShapeDtypeStruct(momentum.shape, BF16),
            ],
            scratch_shapes=[
                pltpu.VMEM((len(values), *next(iter(values.values())).shape), F32),
                pltpu.VMEM((len(values), *next(iter(values.values())).shape), BF16),
                pltpu.SemaphoreType.DMA((len(values) * cuts,)),
                pltpu.SemaphoreType.DMA((len(values) * cuts, 2)),
            ],
            input_output_aliases={2 + len(values) + n: n for n in range(len(outs))},
            cost_estimate=pl.CostEstimate(
                flops=0, bytes_accessed=cost * momentum.size, transcendentals=0
            ),
            compiler_params=params(50),
            name="update_pieces",
        )(notes, momentum, *[v.astype(F32) for v in values.values()], *outs)
    return tuple(outs)


def solution(mesh):
    return jax.shard_map(
        body,
        mesh=mesh,
        in_specs=(
            P("island", "expert", "tensor"),
            P("island", "expert", "tensor"),
            P("island", "expert", None, None),
            P("island", "expert", None),
            P("island", "expert", None, None),
            P("island", "expert", None, "tensor"),
            P("island", "expert", "tensor", None),
            P("island", "expert", None, "tensor"),
            P("expert", None, "tensor"),
        ),
        out_specs=(P("expert", None, "tensor"), P("expert", None, "tensor")),
        check_vma=False,
    )
```
